256 devices in a mesh: ctx: 8 (over y, core), br: 32 (over z, x).
Axes of the slice: x: 4, y: 4, z: 8, core: 2. Of those that a mesh axis runs over, the one named last changes fastest.
Arguments:
- prompt_key_value: bfloat16 [2, 16384, 1024], P(None, 'ctx'), may hold values from -10 to 10
- suffix_page_store: bfloat16 [1024, 2, 128, 1024], P('br', None, None, 'ctx'), may hold values from -8 to 8
- page_table: int32 [512, 2], P('br'), may hold values from 0 to 1023, as said below
- lengths: int32 [512], replicated, may hold values from 1 to 253
- parents: int32 [3, 512], replicated, may hold values from 0 to 511, as said below
- queries: bfloat16 [3, 512, 8192], P(None, 'br', 'ctx'), may hold values from -6.4 to 6.4
- fresh_key_value: bfloat16 [3, 2, 512, 1024], P(None, None, 'br', 'ctx'), may hold values from -8 to 8
Outputs:
- attention: bfloat16 [3, 512, 8192], P(None, 'br', 'ctx')
The draws below stay inside these ranges and needn't reach their ends.
Inputs may be any that keep to these rules, and one draw needn't show every extreme that they name: `page_table`: the 2 pages of the 16 branches of one device of br are exactly that device's 16 * 2 pages of suffix_page_store, each named once. The branches of one device of br form aligned groups of 1 consecutive branches; all parents of one group lie on one device of br, and different groups of one device take their parents from different devices.
All inputs are finite; a program needn't handle non-finite values.
Results may differ from the reference program's by a relative error of at most 0.002.
Values may be sent and summed in bfloat16 or wider, within the bound.
A program may use at most 128 MiB of HBM per device.

```python
import math
import jax
import jax.numpy as jnp
from jax import lax

QUERY_HEADS = 64
KEY_VALUE_HEADS = 8
HEAD_SIZE = 128
PAGE_POSITIONS = 128
PAGES = 2
DECODE_STEPS = 3
BR_DEV = 16
PROMPT_PER_SHARD = 2048
BRANCH_TOTAL = 512
PROMPT_LENGTH = 16384
POOL_PAGES = 1024
LMAX = 253
N_CTX = 8
N_BR = 32


def draw_prompt_key_value(key, part):
    key = jax.random.fold_in(key, 13)
    first_key, second_key = jax.random.split(key)
    single_shape = (PROMPT_LENGTH, KEY_VALUE_HEADS * HEAD_SIZE)
    key_part = jnp.clip(jax.random.normal(first_key, single_shape, jnp.float32), -5.0, 5.0)
    value_part = jnp.clip(3.0 * jax.random.normal(second_key, single_shape, jnp.float32), -10.0, 10.0)
    return jnp.stack([key_part, value_part]).astype(jnp.bfloat16)


def draw_queries(key, part):
    key = jax.random.fold_in(key, 17)
    shape_all = (DECODE_STEPS, BRANCH_TOTAL, QUERY_HEADS * HEAD_SIZE)
    values = jnp.clip(2.5 * jax.random.normal(key, shape_all, jnp.float32), -6.375, 6.375)
    return values.astype(jnp.bfloat16)


def draw_page_table(key, part):
    key = jax.random.fold_in(key, 5)
    key_list = jax.random.split(key, N_BR)
    page_order = jax.vmap(lambda one_key: jax.random.permutation(one_key, BR_DEV * PAGES))(key_list)
    page_base = jnp.arange(N_BR)[:, None] * (BR_DEV * PAGES)
    return (page_order + page_base).reshape(BRANCH_TOTAL, PAGES).astype(jnp.int32)


def draw_lengths(key, part):
    key = jax.random.fold_in(key, 7)
    first_key, second_key = jax.random.split(key)
    values = jax.random.randint(first_key, (BRANCH_TOTAL,), 1, LMAX + 1)
    long_spot = jax.random.randint(second_key, (), 0, BRANCH_TOTAL)
    return jnp.where(jnp.arange(BRANCH_TOTAL) == long_spot, LMAX, values).astype(jnp.int32)


def draw_parents(key, part):
    key = jax.random.fold_in(key, 11)
    slot_count = max(1, BR_DEV // N_BR)
    group_count = BR_DEV // slot_count
    key_list = jax.random.split(key, DECODE_STEPS * N_BR + 1)
    owners = jax.vmap(lambda one_key: jax.random.permutation(one_key, N_BR)[:group_count])(key_list[:-1])
    owners = jnp.repeat(owners, slot_count, axis=1).reshape(DECODE_STEPS, BRANCH_TOTAL)
    local_pick = jax.random.randint(key_list[-1], (DECODE_STEPS, BRANCH_TOTAL), 0, BR_DEV)
    return (owners * BR_DEV + local_pick).astype(jnp.int32)


def block_scale(rng, shape, pieces, low, top_value):
    factor_of = 1.0
    for axis_at, blocks in pieces:
        heights = jax.random.uniform(jax.random.fold_in(jax.random.fold_in(rng, 6), axis_at), (blocks,), jnp.float32, low / len(pieces), top_value / len(pieces))
        factor_of = factor_of * jnp.repeat(jnp.exp(heights), shape[axis_at] // blocks).reshape((-1,) + (1,) * (len(shape) - 1 - axis_at))
    return factor_of


def normal_values(key, extent, scale, bound, shards=(), held_as=jnp.bfloat16):
    entries = jax.random.normal(key, extent, jnp.float32) * scale
    if len(shards) > 0:
        entries = block_scale(key, extent, shards, -0.22, 0.18) * entries
    return jnp.clip(entries, min=-bound, max=bound).astype(held_as)


def setup_inputs(seed: int = 0) -> dict:
    keys = jax.random.split(jax.random.key(seed), 8)
    return {
        "prompt_key_value": draw_prompt_key_value(jax.random.fold_in(keys[7], 71), 0),
        "suffix_page_store": normal_values(keys[1], (POOL_PAGES, 2, PAGE_POSITIONS, KEY_VALUE_HEADS * HEAD_SIZE), 1.5, 8.0, ((0, 32), (3, 8))),
        "page_table": draw_page_table(jax.random.fold_in(keys[7], 71), 0),
        "lengths": draw_lengths(jax.random.fold_in(keys[7], 71), 0),
        "parents": draw_parents(jax.random.fold_in(keys[7], 71), 0),
        "queries": draw_queries(jax.random.fold_in(keys[7], 71), 0),
        "fresh_key_value": normal_values(keys[6], (DECODE_STEPS, 2, BRANCH_TOTAL, KEY_VALUE_HEADS * HEAD_SIZE), 1.5, 8.0, ((2, 32), (3, 8))),
    }


NEG_FILL = -1e+30

def block_stats(scores, values, einsum_form):
    peak_value = lax.optimization_barrier(jnp.max(scores, axis=-1))
    weights = jnp.exp(scores - peak_value[..., None])
    weight_total = lax.optimization_barrier(jnp.sum(weights, axis=-1))
    rounded = lax.optimization_barrier(weights.astype(jnp.bfloat16)).astype(jnp.float32)
    summed = jnp.einsum(einsum_form, rounded, values.astype(jnp.float32))
    return (peak_value, weight_total, summed)

def reference(prompt_key_value, suffix_page_store, page_table, lengths, parents, queries, fresh_key_value):
    group_width = QUERY_HEADS // KEY_VALUE_HEADS
    score_scale = 1.0 / math.sqrt(HEAD_SIZE)
    branch_rows = page_table.shape[0]
    suffix_length = PAGES * PAGE_POSITIONS
    suffix_in_pages = suffix_page_store[page_table]
    suffix_tokens = jnp.swapaxes(suffix_in_pages, 1, 2).reshape(branch_rows, 2, suffix_length, KEY_VALUE_HEADS * HEAD_SIZE)
    length = lengths
    prompt_block_list = jnp.moveaxis(prompt_key_value.reshape(2, N_CTX, PROMPT_PER_SHARD, KEY_VALUE_HEADS, HEAD_SIZE), 1, 0)
    position = jnp.arange(suffix_length, dtype=jnp.int32)
    results = []
    for decode_step_index in range(DECODE_STEPS):
        parent = parents[decode_step_index]
        suffix_tokens = suffix_tokens[parent]
        length = length[parent]
        fresh_token = jnp.swapaxes(fresh_key_value[decode_step_index], 0, 1)
        target_mask = (position[None, :] == length[:, None])[:, None, :, None]
        suffix_tokens = jnp.where(target_mask, fresh_token[:, :, None, :], suffix_tokens)
        length = length + 1
        query_head_rows = queries[decode_step_index].astype(jnp.float32).reshape(branch_rows, KEY_VALUE_HEADS, group_width, HEAD_SIZE)

        def prompt_block(block_kv):
            scores = jnp.einsum('bgrd,tgd->bgrt', query_head_rows, block_kv[0].astype(jnp.float32)) * score_scale
            return block_stats(scores, block_kv[1], 'bgrt,tgd->bgrd')
        prompt_peaks, prompt_totals, prompt_sums = lax.map(prompt_block, prompt_block_list)
        branch_suffix_keys = suffix_tokens[:, 0].astype(jnp.float32).reshape(branch_rows, suffix_length, KEY_VALUE_HEADS, HEAD_SIZE)
        branch_suffix_values = suffix_tokens[:, 1].reshape(branch_rows, suffix_length, KEY_VALUE_HEADS, HEAD_SIZE)
        scores = jnp.einsum('bgrd,btgd->bgrt', query_head_rows, branch_suffix_keys) * score_scale
        live_mask = (position[None, :] < length[:, None])[:, None, None, :]
        scores = jnp.where(live_mask, scores, NEG_FILL)
        suffix_peak, suffix_total, suffix_sum = block_stats(scores, branch_suffix_values, 'bgrt,btgd->bgrd')
        block_peaks = jnp.concatenate([prompt_peaks, suffix_peak[None]], axis=0)
        totals = jnp.concatenate([prompt_totals, suffix_total[None]], axis=0)
        block_sums = jnp.concatenate([prompt_sums, suffix_sum[None]], axis=0)
        overall = lax.optimization_barrier(jnp.max(block_peaks, axis=0))
        factor = jnp.exp(block_peaks - overall[None])
        denominator = lax.optimization_barrier(jnp.sum(factor * totals, axis=0))
        numerator = lax.optimization_barrier(jnp.sum(factor[..., None] * block_sums, axis=0))
        attention = (numerator / denominator[..., None]).reshape(branch_rows, QUERY_HEADS * HEAD_SIZE)
        results.append(attention.astype(jnp.bfloat16))
    return jnp.stack(results)
```

```python
import functools
import math

import jax
import jax.numpy as jnp
from jax import lax
from jax.experimental import pallas as pl
from jax.experimental.pallas import tpu as pltpu
from jax.sharding import PartitionSpec as P

QUERY_HEADS = 64
KEY_VALUE_HEADS = 8
HEAD_SIZE = 128


NEG_FILL = -1e30


def joined_2(part, axis, combine):
    gathered = jax.tree.map(lambda a: lax.all_gather(a, axis), part)

    def take(source):
        return jax.tree.map(lambda a: lax.dynamic_index_in_dim(a, source, 0, False), gathered)

    return lax.fori_loop(
        1, lax.axis_size(axis), lambda source, state: combine(state, take(source)), take(0)
    )


def block_stats(scores, values, einsum_form):
    peak_value = jnp.max(scores, axis=-1)
    weights = jnp.exp(scores - peak_value[..., None])
    weight_total = jnp.sum(weights, axis=-1)
    rounded = weights.astype(jnp.bfloat16)
    summed = jnp.einsum(einsum_form, rounded, values, preferred_element_type=jnp.float32)
    return (peak_value, weight_total, summed)


def fold_pair(left_stats, right_stats):
    peak_value = jnp.maximum(left_stats[0], right_stats[0])
    left_weight = jnp.exp(left_stats[0] - peak_value)
    right_weight = jnp.exp(right_stats[0] - peak_value)
    weight_total = left_stats[1] * left_weight + right_stats[1] * right_weight
    summed = left_stats[2] * left_weight[..., None] + right_stats[2] * right_weight[..., None]
    return (peak_value, weight_total, summed)


def suffix_stats(query_head_rows, suffix_tokens, live_length, score_scale):
    row_count = suffix_tokens.shape[0]
    suffix_length = suffix_tokens.shape[2]
    kv_local = query_head_rows.shape[1]
    branch_suffix_keys = suffix_tokens[:, 0].reshape(row_count, suffix_length, kv_local, HEAD_SIZE)
    branch_suffix_values = suffix_tokens[:, 1].reshape(
        row_count, suffix_length, kv_local, HEAD_SIZE
    )
    scores = (
        jnp.einsum(
            "bgrd,btgd->bgrt",
            query_head_rows,
            branch_suffix_keys,
            preferred_element_type=jnp.float32,
        )
        * score_scale
    )
    live_mask = jnp.arange(suffix_length, dtype=jnp.int32)[None, :] < live_length[:, None]
    scores = jnp.where(live_mask[:, None, None, :], scores, NEG_FILL)
    return block_stats(scores, branch_suffix_values, "bgrt,btgd->bgrd")


def routing(parent, branch_per_shard, br_index, slot_rank, slot_match):
    grid_owner = (parent // branch_per_shard).reshape(-1, branch_per_shard)
    grid_local = (parent % branch_per_shard).reshape(-1, branch_per_shard)
    matched = (grid_owner == br_index)[:, :, None] & slot_match[None, :, :]
    outgoing = jnp.sum(jnp.where(matched, grid_local[:, :, None], 0), axis=1)
    own_owner = (
        lax.dynamic_slice_in_dim(parent, br_index * branch_per_shard, branch_per_shard)
        // branch_per_shard
    )
    incoming = own_owner * slot_match.shape[1] + slot_rank
    return (outgoing, incoming, own_owner)


def move_suffix(suffix_tokens, outgoing, incoming):
    dest_count = outgoing.shape[0]
    slot_count = outgoing.shape[1]
    tail_shape = suffix_tokens.shape[1:]
    outbound = suffix_tokens[outgoing.reshape(-1)].reshape((dest_count, slot_count) + tail_shape)
    arrived = lax.all_to_all(outbound, "br", split_axis=0, concat_axis=0, tiled=True)
    return arrived.reshape((dest_count * slot_count,) + tail_shape)[incoming]


def append_token(suffix_tokens, position_at, fresh_token):
    suffix_length = suffix_tokens.shape[2]
    target_mask = jnp.arange(suffix_length, dtype=jnp.int32)[None, :] == position_at[:, None]
    return jnp.where(
        target_mask[:, None, :, None], jnp.swapaxes(fresh_token, 0, 1)[:, :, None, :], suffix_tokens
    )


def general(
    prompt_key_value, suffix_page_store, page_table, lengths, parents, queries, fresh_key_value
):
    br_count = lax.axis_size("br")
    br_index = lax.axis_index("br")
    ctx_index = lax.axis_index("ctx")
    branch_per_shard = page_table.shape[0]
    page_count = page_table.shape[1]
    pool_dev = suffix_page_store.shape[0]
    page_rows = suffix_page_store.shape[2]
    head_width = suffix_page_store.shape[3]
    step_count = queries.shape[0]
    kv_local = head_width // HEAD_SIZE
    group_width = QUERY_HEADS // KEY_VALUE_HEADS
    slot_count = max(1, branch_per_shard // br_count)
    score_scale = 1.0 / math.sqrt(HEAD_SIZE)
    slot_rank = jnp.arange(branch_per_shard, dtype=jnp.int32) % slot_count
    slot_match = slot_rank[:, None] == jnp.arange(slot_count, dtype=jnp.int32)[None, :]
    gathered_pages = suffix_page_store[page_table - br_index * pool_dev]
    suffix_tokens = jnp.swapaxes(gathered_pages, 1, 2).reshape(
        branch_per_shard, 2, page_count * page_rows, head_width
    )
    length = lengths
    head_listing = lax.all_gather(queries, "ctx", axis=2, tiled=True)
    shared_prompt_keys = prompt_key_value[0].reshape(-1, KEY_VALUE_HEADS, HEAD_SIZE)
    shared_prompt_values = prompt_key_value[1].reshape(-1, KEY_VALUE_HEADS, HEAD_SIZE)
    outputs = []
    for decode_step_index in range(step_count):
        parent = parents[decode_step_index]
        outgoing, incoming, own_owner = routing(
            parent, branch_per_shard, br_index, slot_rank, slot_match
        )
        parent_length = length[parent]
        own_parent_length = lax.dynamic_slice_in_dim(
            parent_length, br_index * branch_per_shard, branch_per_shard
        )
        fresh_token = fresh_key_value[decode_step_index]
        query_mine = queries[decode_step_index].reshape(
            branch_per_shard, kv_local, group_width, HEAD_SIZE
        )
        suffix_tokens = append_token(
            move_suffix(suffix_tokens, outgoing, incoming), own_parent_length, fresh_token
        )
        suffix_part = suffix_stats(query_mine, suffix_tokens, own_parent_length + 1, score_scale)
        length = parent_length + 1
        query_complete = head_listing[decode_step_index].reshape(
            branch_per_shard, KEY_VALUE_HEADS, group_width, HEAD_SIZE
        )
        prompt_scores = (
            jnp.einsum(
                "bgrd,tgd->bgrt",
                query_complete,
                shared_prompt_keys,
                preferred_element_type=jnp.float32,
            )
            * score_scale
        )
        prompt_part = block_stats(prompt_scores, shared_prompt_values, "bgrt,tgd->bgrd")
        head_start = ctx_index * kv_local
        own_heads = tuple(
            (lax.dynamic_slice_in_dim(member, head_start, kv_local, 1) for member in prompt_part)
        )
        joined = fold_pair(own_heads, suffix_part)
        placed = tuple(
            (
                lax.dynamic_update_slice_in_dim(whole_part, own_part, head_start, 1)
                for whole_part, own_part in zip(prompt_part, joined)
            )
        )
        merged = joined_2((placed[0], placed[1], placed[2]), "ctx", fold_pair)
        combined = tuple(
            (lax.dynamic_slice_in_dim(member, head_start, kv_local, 1) for member in merged)
        )
        attention = (combined[2] / combined[1][..., None]).reshape(
            branch_per_shard, kv_local * group_width * HEAD_SIZE
        )
        outputs.append(attention.astype(jnp.bfloat16))
    return jnp.stack(outputs)


STEPS = 3
BRANCHES = 16
NODES = STEPS * BRANCHES
CAP = 8
LIVE = 96
FIRST = 16
KEYS = 4096
ROWS = 8 * NODES
MASKED = -1e30
EXP_SCALE = math.log2(math.e) / math.sqrt(HEAD_SIZE)
BF = jnp.bfloat16
F32 = jnp.float32
NT = (((1,), (1,)), ((), ()))


def onehot(condition):
    return jnp.where(condition, 1.0, 0.0).astype(BF)


def iota(shape, axis):
    return lax.broadcasted_iota(jnp.int32, shape, axis)


def stacked(rows, count, width):
    at = iota((count, width), 0)
    out = jnp.zeros((count, width), F32)
    for index, row in enumerate(rows):
        out = jnp.where(at == index, row.astype(F32), out)
    return out.astype(BF)


def dot(left, right):
    return jnp.dot(left, right, preferred_element_type=F32)


def dot_nt(left, right):
    return lax.dot_general(left, right, NT, preferred_element_type=F32)


def softmax_block(query, key, value):
    raw = dot_nt(query, key)
    peak = jnp.max(raw, axis=1, keepdims=True)
    weight = jnp.exp2((raw - peak) * EXP_SCALE)
    total = jnp.sum(weight, axis=1, keepdims=True)
    return peak, total, dot(weight.astype(BF), value)


def kernel(
    br_count, ctx_count,
    page_ref, len_ref, par_ref, q_ref, fresh_ref, pkv_ref, pages_ref,
    out_ref, flag_ref,
    kbuf, vbuf, kcat, vcat, qbuf, sendm, recvm, qcat, part_send, part_recv, suffix_out, ret_send, ret_recv, num,
    kv_sem, page_sem, q_send, q_recv, m_send, m_recv, p_send, p_recv, r_send, r_recv,
):
    me_c = lax.axis_index("ctx")
    me_r = lax.axis_index("br")

    def peer_c(i):
        return lax.rem(me_c + i, ctx_count)

    def peer_r(i):
        return lax.rem(me_r + i, br_count)

    def head_at(i):
        chip = lax.rem(me_c // 2 + i // 2, ctx_count // 2)
        return chip * 2 + lax.rem(me_c + lax.rem(i, 2), 2)

    barrier = pltpu.get_barrier_semaphore()

    @pl.loop(1, ctx_count)
    def _(i):
        pl.semaphore_signal(barrier, inc=1, device_id={"ctx": peer_c(i)}, device_id_type=pl.DeviceIdType.MESH)

    @pl.loop(1, br_count)
    def _(i):
        pl.semaphore_signal(barrier, inc=1, device_id={"br": peer_r(i)}, device_id_type=pl.DeviceIdType.MESH)

    def kv_copy(i, which):
        g = head_at(i)
        buffer = kbuf if which == 0 else vbuf
        return pltpu.make_async_copy(
            pkv_ref.at[which, :, pl.ds(pl.multiple_of(g * HEAD_SIZE, HEAD_SIZE), HEAD_SIZE)],
            buffer.at[g], kv_sem.at[which, g])

    key_pages = pltpu.make_async_copy(pages_ref.at[:, 0], kcat.at[pl.ds(0, 32), :, pl.ds(0, HEAD_SIZE)], page_sem.at[0])
    value_pages = pltpu.make_async_copy(pages_ref.at[:, 1], vcat.at[pl.ds(0, 32)], page_sem.at[1])

    @pl.loop(0, ctx_count)
    def _(i):
        kv_copy(i, 0).start()
        kv_copy(i, 1).start()

    key_pages.start()
    value_pages.start()

    parent = par_ref[...]
    device = lax.shift_right_logical(parent, 4)
    place = parent & 15
    width = parent.shape[1]
    row_at = iota((width, width), 0)
    pick1 = onehot(row_at == parent[1:2])
    pick2 = onehot(row_at == parent[2:3])
    first = dot(stacked([device[0:1], place[0:1]], 16, width), pick1)
    second = dot(stacked([first[0:1], first[1:2], device[1:2], place[1:2]], 16, width), pick2)
    anc_dev = [device[0:1].astype(F32), first[0:1], second[0:1]]
    anc_loc = [place[0:1].astype(F32), first[1:2], second[1:2]]
    missing = jnp.full((1, width), -1.0, F32)
    par_hi = [missing, device[1:2].astype(F32), device[2:3].astype(F32) + 32.0]
    par_lo = [missing, place[1:2].astype(F32), place[2:3].astype(F32)]
    old_hi = [missing, missing, second[2:3]]
    old_lo = [missing, missing, second[3:4]]

    owner = iota((br_count, width), 0).astype(F32)
    to_owner = [onehot(owner == anc_dev[s]) for s in range(STEPS)]
    j = iota((128, 256), 0)
    lane = iota((128, 256), 1)
    b = lane & 127
    same_home = (j >> 4) == (b >> 4)
    counting = onehot(same_home & ((lane >= 128) | (j < b)))
    slots = [[], [], []]
    pair_count = []
    for tile in range(width // 128):
        cut = [m[:, tile * 128:(tile + 1) * 128] for m in to_owner]
        counted = dot(jnp.concatenate(cut, axis=0), counting)
        before = jnp.zeros((br_count, 128), F32)
        for s in range(STEPS):
            block = counted[s * br_count:(s + 1) * br_count]
            slots[s].append(jnp.sum(cut[s].astype(F32) * (block[:, :128] + before), axis=0, keepdims=True))
            before = before + block[:, 128:]
        pair_count.append(before)
    slot = [jnp.concatenate(parts, axis=1) for parts in slots]
    count = jnp.concatenate(pair_count, axis=1)
    most = jnp.max(count)
    fullest = jnp.max(jnp.sum(count, axis=1, keepdims=True)) / BRANCHES
    over = (most > CAP) | (fullest > LIVE)
    flag_ref[...] = jnp.where(over, 1, 0) + jnp.zeros((8, 128), jnp.int32)

    node = iota((128, STEPS * width), 0)
    column = iota((128, STEPS * width), 1)
    mine = onehot(((column & (width - 1)) == me_r * BRANCHES + (node & 15)) & ((node >> 4) == column // width))
    whither = jnp.concatenate([stacked([anc_dev[s], slot[s]], 16, width) for s in range(STEPS)], axis=1)
    own_row = dot_nt(whither, mine)
    own_col = dot_nt(mine, whither)
    own_addr_row = own_row[0:1] * CAP + own_row[1:2]
    own_addr_col = own_col[:NODES, 0:1] * CAP + own_col[:NODES, 1:2]
    at = iota((2 * CAP * br_count, 128), 0)
    is_node = iota((2 * CAP * br_count, 128), 1) < NODES
    placed = is_node & ((at >> 1).astype(F32) == own_addr_row)
    padding = jnp.zeros((128 - NODES, 640), BF)
    queries = q_ref[...]
    fresh_key = jnp.concatenate([fresh_ref[s, 0] for s in range(STEPS)], axis=0)
    fresh_value = jnp.concatenate([fresh_ref[s, 1] for s in range(STEPS)], axis=0)
    low = jnp.concatenate([jnp.concatenate([queries[:, :512], fresh_key], axis=1), padding], axis=0)
    high = jnp.concatenate([jnp.concatenate([queries[:, 512:], fresh_value], axis=1), padding], axis=0)
    sendm[...] = (dot(onehot(placed & ((at & 1) == 0)), low) + dot(onehot(placed & ((at & 1) == 1)), high)).astype(BF)

    def message(i, source):
        peer = peer_r(i)
        return pltpu.make_async_remote_copy(
            src_ref=sendm.at[pl.ds(pl.multiple_of(peer * 16, 16), 16)],
            dst_ref=recvm.at[pl.ds(pl.multiple_of(source * 16, 16), 16)],
            send_sem=m_send.at[peer], recv_sem=m_recv.at[source],
            device_id={"br": peer}, device_id_type=pl.DeviceIdType.MESH)

    def query_copy(i, source):
        peer = head_at(i)
        return pltpu.make_async_remote_copy(
            src_ref=q_ref, dst_ref=qbuf.at[source],
            send_sem=q_send.at[peer], recv_sem=q_recv.at[source],
            device_id={"ctx": peer}, device_id_type=pl.DeviceIdType.MESH)

    pl.semaphore_wait(barrier, ctx_count - 1 + br_count - 1)

    @pl.loop(1, ctx_count)
    def _(i):
        query_copy(i, me_c).start()

    @pl.loop(1, br_count)
    def _(i):
        message(i, me_r).start()

    own16 = pl.ds(pl.multiple_of(me_r * 16, 16), 16)
    recvm[own16, :] = sendm[own16, :]
    qbuf[me_c] = queries

    here = (iota((br_count, width), 0) == me_r).astype(F32)
    home_count = jnp.sum(here * count, axis=0, keepdims=True)
    col_at = iota((width, width), 1)
    earlier = onehot(((row_at & 15) == 0) & ((row_at >> 4) < (col_at >> 4)))
    ahead = dot(stacked([home_count], 16, width), earlier)[0:1]
    home = lax.shift_right_logical(iota((1, width), 1), 4).astype(F32)
    local_at = (iota((1, width), 1) & 15).astype(F32)
    ones = jnp.ones((1, width), F32)
    live_rows = iota((128, width), 0).astype(F32)
    chosen, known = [], []
    for s in range(STEPS):
        arrives = anc_dev[s] == me_r.astype(F32)
        place_at = jnp.where(arrives, ahead + slot[s] + FIRST, -1.0)
        chosen.append(onehot(live_rows == place_at))
        known.append(stacked([
            ones, home, slot[s], anc_loc[s], home + 32.0 * s, local_at,
            par_hi[s], par_lo[s], old_hi[s], old_lo[s]], 16, width))
    chosen = jnp.concatenate(chosen, axis=1)
    known = jnp.concatenate(known, axis=1)
    row_info = dot_nt(known, chosen)
    col_info = dot_nt(chosen, known)[FIRST:FIRST + LIVE]
    addr_row = jnp.where(row_info[0:1] > 0.5, row_info[1:2] * CAP + row_info[2:3], -1.0)
    addr_col = jnp.where(col_info[:, 0:1] > 0.5, col_info[:, 1:2] * CAP + col_info[:, 2:3], -1.0)
    self_col = jnp.where(col_info[:, 0:1] > 0.5, col_info[:, 4:5] * 16.0 + col_info[:, 5:6], -100.0)
    lane_live = iota((LIVE, 128), 1)
    extra_query = onehot((lane_live.astype(F32) == col_info[:, 3:4]) | (lane_live == iota((LIVE, 128), 0) + FIRST))
    on_path = self_col == row_info[4:5] * 16.0 + row_info[5:6]
    on_path = on_path | (self_col == row_info[6:7] * 16.0 + row_info[7:8])
    on_path = on_path | (self_col == row_info[8:9] * 16.0 + row_info[9:10])
    seen = on_path | ((lane_live < FIRST) & (self_col > -1.0))
    kcat[32, pl.ds(0, LIVE), pl.ds(128, 128)] = jnp.where(seen, 0.0, MASKED).astype(BF)
    kcat[32, pl.ds(LIVE, 128 - LIVE), pl.ds(128, 128)] = jnp.full((128 - LIVE, 128), MASKED, BF)
    kcat[32, pl.ds(LIVE, 128 - LIVE), pl.ds(0, 128)] = jnp.zeros((128 - LIVE, 128), BF)
    vcat[32, pl.ds(LIVE, 128 - LIVE)] = jnp.zeros((128 - LIVE, 128), BF)

    page_at = iota((32, 128), 0)
    page_lane = iota((32, 128), 1)
    live = jnp.where(page_lane < FIRST, 0, 128)
    for branch in range(BRANCHES):
        length = len_ref[me_r * BRANCHES + branch]
        for page in range(2):
            number = page_ref[branch, page] - me_r * 32
            held = jnp.clip(length - 128 * page, 0, 128)
            live = jnp.where((page_at == number) & (page_lane == branch), held, live)
    position = iota((128, 128), 0)
    for page in range(32):
        kcat[page, :, pl.ds(128, 128)] = jnp.where(position < live[page:page + 1], 0.0, MASKED).astype(BF)

    stat_lane = iota((NODES, 128), 1)

    def part_copy(i, source):
        peer = head_at(i)
        return pltpu.make_async_remote_copy(
            src_ref=part_send.at[peer], dst_ref=part_recv.at[source],
            send_sem=p_send.at[peer], recv_sem=p_recv.at[source],
            device_id={"ctx": peer}, device_id_type=pl.DeviceIdType.MESH)

    @pl.loop(0, ctx_count)
    def _(i):
        g = head_at(i)

        @pl.when(i > 0)
        def _():
            query_copy(i, g).wait_recv()

        kv_copy(i, 0).wait()
        kv_copy(i, 1).wait()
        key = kbuf[g]
        value = vbuf[g]
        stat = jnp.zeros((NODES, 128), F32)
        for half in range(2):
            rows = jnp.concatenate(
                [qbuf[g, :, pl.ds((4 * half + h) * 128, 128)] for h in range(4)], axis=0)
            peak, total, summed = softmax_block(rows, key, value)
            part_send[g, pl.ds(half * 4 * NODES, 4 * NODES)] = summed
            for h in range(4):
                cut = slice(h * NODES, (h + 1) * NODES)
                stat = jnp.where(stat_lane == 4 * half + h, peak[cut], stat)
                stat = jnp.where(stat_lane == 8 + 4 * half + h, total[cut], stat)
        part_send[g, pl.ds(ROWS, NODES)] = stat

        @pl.when(i > 0)
        def _():
            part_copy(i, me_c).start()

    @pl.loop(1, br_count)
    def _(i):
        message(0, peer_r(i)).wait_recv()

    gather = iota((LIVE, 2 * CAP * br_count), 1)
    taken = (gather >> 1).astype(F32) == addr_col
    got = recvm[...]
    got_low = dot(onehot(taken & ((gather & 1) == 0)), got).astype(BF)
    got_high = dot(onehot(taken & ((gather & 1) == 1)), got).astype(BF)
    kcat[32, pl.ds(0, LIVE), pl.ds(0, 128)] = got_low[:, 512:]
    vcat[32, pl.ds(0, LIVE)] = got_high[:, 512:]
    for h in range(8):
        source = got_low if h < 4 else got_high
        qcat[h, :, pl.ds(0, 128)] = source[:, (h % 4) * 128:(h % 4 + 1) * 128]
        qcat[h, :, pl.ds(128, 128)] = extra_query
    key_pages.wait()
    value_pages.wait()
    live_lane = iota((LIVE, 128), 1)
    suffix_out[:, pl.ds(0, FIRST)] = jnp.zeros((9, FIRST, 128), F32)
    suffix_out[:, pl.ds(FIRST + LIVE, 128 - FIRST - LIVE)] = jnp.zeros((9, 128 - FIRST - LIVE, 128), F32)

    def suffix_head(h, stat):
        key = kcat[...].reshape(33 * 128, 256)
        value = vcat[...].reshape(33 * 128, 128)
        peak, total, summed = softmax_block(qcat[h], key, value)
        suffix_out[h, pl.ds(FIRST, LIVE)] = summed
        stat = jnp.where(live_lane == h, peak, stat)
        return jnp.where(live_lane == 8 + h, total, stat)

    suffix_out[8, pl.ds(FIRST, LIVE)] = lax.fori_loop(0, 8, suffix_head, jnp.zeros((LIVE, 128), F32))
    back = jnp.where(iota((CAP * br_count, 128), 0).astype(F32) == addr_row, 1.0, 0.0)
    for h in range(9):
        ret_send[:, pl.ds(h * 128, 128)] = jnp.dot(
            back, suffix_out[h], precision=lax.Precision.HIGHEST, preferred_element_type=F32)

    def returned(i, source):
        peer = peer_r(i)
        return pltpu.make_async_remote_copy(
            src_ref=ret_send.at[pl.ds(pl.multiple_of(peer * CAP, CAP), CAP)],
            dst_ref=ret_recv.at[pl.ds(pl.multiple_of(source * CAP, CAP), CAP)],
            send_sem=r_send.at[peer], recv_sem=r_recv.at[source],
            device_id={"br": peer}, device_id_type=pl.DeviceIdType.MESH)

    @pl.loop(1, br_count)
    def _(i):
        returned(i, me_r).start()

    own8 = pl.ds(pl.multiple_of(me_r * CAP, CAP), CAP)
    ret_recv[own8, :] = ret_send[own8, :]

    part_recv[me_c] = part_send[me_c]

    @pl.loop(1, ctx_count)
    def _(i):
        part_copy(0, head_at(i)).wait_recv()

    stats = [part_recv[c, pl.ds(ROWS, NODES)] for c in range(8)]
    top = functools.reduce(jnp.maximum, stats)
    factors = [jnp.exp2((stat - top) * EXP_SCALE) for stat in stats]
    den = jnp.zeros((NODES, 128), F32)
    for c in range(8):
        den = den + factors[c] * pltpu.roll(stats[c], 120, 1)
    for h in range(8):
        summed = jnp.zeros((NODES, 128), F32)
        for c in range(8):
            summed = summed + factors[c][:, h:h + 1] * part_recv[c, pl.ds(h * NODES, NODES)]
        num[h] = summed

    @pl.loop(1, br_count)
    def _(i):
        returned(0, peer_r(i)).wait_recv()

    mine_back = jnp.where(iota((NODES, CAP * br_count), 1).astype(F32) == own_addr_col, 1.0, 0.0)

    def back_home(h):
        return jnp.dot(mine_back, ret_recv[:, pl.ds(h * 128, 128)],
                       precision=lax.Precision.HIGHEST, preferred_element_type=F32)

    suffix_stat = back_home(8)
    overall = jnp.maximum(top, suffix_stat)
    prompt_factor = jnp.exp2((top - overall) * EXP_SCALE)
    suffix_factor = jnp.exp2((suffix_stat - overall) * EXP_SCALE)
    den = prompt_factor * den + suffix_factor * pltpu.roll(suffix_stat, 120, 1)
    for h in range(8):
        joined = prompt_factor[:, h:h + 1] * num[h] + suffix_factor[:, h:h + 1] * back_home(h)
        out_ref[:, pl.ds(h * 128, 128)] = (joined / den[:, h:h + 1]).astype(BF)

    @pl.loop(1, ctx_count)
    def _(i):
        query_copy(i, me_c).wait_send()
        part_copy(i, me_c).wait_send()

    @pl.loop(1, br_count)
    def _(i):
        message(i, me_r).wait_send()
        returned(i, me_r).wait_send()


def local(
    prompt_key_value, suffix_page_store, page_table, lengths, parents, queries, fresh_key_value
):
    br_count = lax.axis_size("br")
    ctx_count = lax.axis_size("ctx")
    vmem = pl.BlockSpec(memory_space=pltpu.VMEM)
    smem = pl.BlockSpec(memory_space=pltpu.SMEM)
    anywhere = pl.BlockSpec(memory_space=pl.ANY)
    dma = pltpu.SemaphoreType.DMA
    slots = CAP * br_count
    out, flag = pl.pallas_call(
        functools.partial(kernel, br_count, ctx_count),
        out_shape=(
            jax.ShapeDtypeStruct((NODES, 1024), BF),
            jax.ShapeDtypeStruct((8, 128), jnp.int32),
        ),
        in_specs=[smem, smem, vmem, vmem, vmem, anywhere, anywhere],
        out_specs=(vmem, vmem),
        scratch_shapes=[
            pltpu.VMEM((8, 2048, 128), BF),
            pltpu.VMEM((8, 2048, 128), BF),
            pltpu.VMEM((33, 128, 256), BF),
            pltpu.VMEM((33, 128, 128), BF),
            pltpu.VMEM((8, NODES, 1024), BF),
            pltpu.VMEM((2 * slots, 640), BF),
            pltpu.VMEM((2 * slots, 640), BF),
            pltpu.VMEM((8, LIVE, 256), BF),
            pltpu.VMEM((8, ROWS + NODES, 128), F32),
            pltpu.VMEM((8, ROWS + NODES, 128), F32),
            pltpu.VMEM((9, 128, 128), F32),
            pltpu.VMEM((slots, 1152), F32),
            pltpu.VMEM((slots, 1152), F32),
            pltpu.VMEM((8, NODES, 128), F32),
            dma((2, 8)), dma((2,)), dma((8,)), dma((8,)), dma((32,)), dma((32,)),
            dma((8,)), dma((8,)), dma((32,)), dma((32,)),
        ],
        compiler_params=pltpu.CompilerParams(
            collective_id=0, has_side_effects=True, vmem_limit_bytes=56 * 1024 * 1024
        ),
    )(
        page_table, lengths, parents, queries.reshape(NODES, 1024), fresh_key_value,
        prompt_key_value, suffix_page_store,
    )
    operands = (
        prompt_key_value, suffix_page_store, page_table, lengths, parents, queries, fresh_key_value
    )
    return lax.cond(
        flag[0, 0] > 0,
        lambda *whole: general(*whole),
        lambda *whole: out.reshape(STEPS, BRANCHES, 1024),
        *operands,
    )


def solution(mesh):
    in_specs = (
        P(None, "ctx", None),
        P("br", None, None, "ctx"),
        P("br", None),
        P(),
        P(),
        P(None, "br", "ctx"),
        P(None, None, "br", "ctx"),
    )
    out_specs = P(None, "br", "ctx")
    return jax.shard_map(local, mesh=mesh, in_specs=in_specs, out_specs=out_specs, check_vma=False)
```

```python
import functools
import math

import jax
import jax.numpy as jnp
from jax import lax
from jax.experimental import pallas as pl
from jax.experimental.pallas import tpu as pltpu
from jax.sharding import PartitionSpec as P

QUERY_HEADS = 64
KEY_VALUE_HEADS = 8
HEAD_SIZE = 128


NEG_FILL = -1e30


def joined_2(part, axis, combine):
    gathered = jax.tree.map(lambda a: lax.all_gather(a, axis), part)

    def take(source):
        return jax.tree.map(lambda a: lax.dynamic_index_in_dim(a, source, 0, False), gathered)

    return lax.fori_loop(
        1, lax.axis_size(axis), lambda source, state: combine(state, take(source)), take(0)
    )


def block_stats(scores, values, einsum_form):
    peak_value = jnp.max(scores, axis=-1)
    weights = jnp.exp(scores - peak_value[..., None])
    weight_total = jnp.sum(weights, axis=-1)
    rounded = weights.astype(jnp.bfloat16)
    summed = jnp.einsum(einsum_form, rounded, values, preferred_element_type=jnp.float32)
    return (peak_value, weight_total, summed)


def fold_pair(left_stats, right_stats):
    peak_value = jnp.maximum(left_stats[0], right_stats[0])
    left_weight = jnp.exp(left_stats[0] - peak_value)
    right_weight = jnp.exp(right_stats[0] - peak_value)
    weight_total = left_stats[1] * left_weight + right_stats[1] * right_weight
    summed = left_stats[2] * left_weight[..., None] + right_stats[2] * right_weight[..., None]
    return (peak_value, weight_total, summed)


def suffix_stats(query_head_rows, suffix_tokens, live_length, score_scale):
    row_count = suffix_tokens.shape[0]
    suffix_length = suffix_tokens.shape[2]
    kv_local = query_head_rows.shape[1]
    branch_suffix_keys = suffix_tokens[:, 0].reshape(row_count, suffix_length, kv_local, HEAD_SIZE)
    branch_suffix_values = suffix_tokens[:, 1].reshape(
        row_count, suffix_length, kv_local, HEAD_SIZE
    )
    scores = (
        jnp.einsum(
            "bgrd,btgd->bgrt",
            query_head_rows,
            branch_suffix_keys,
            preferred_element_type=jnp.float32,
        )
        * score_scale
    )
    live_mask = jnp.arange(suffix_length, dtype=jnp.int32)[None, :] < live_length[:, None]
    scores = jnp.where(live_mask[:, None, None, :], scores, NEG_FILL)
    return block_stats(scores, branch_suffix_values, "bgrt,btgd->bgrd")


def routing(parent, branch_per_shard, br_index, slot_rank, slot_match):
    grid_owner = (parent // branch_per_shard).reshape(-1, branch_per_shard)
    grid_local = (parent % branch_per_shard).reshape(-1, branch_per_shard)
    matched = (grid_owner == br_index)[:, :, None] & slot_match[None, :, :]
    outgoing = jnp.sum(jnp.where(matched, grid_local[:, :, None], 0), axis=1)
    own_owner = (
        lax.dynamic_slice_in_dim(parent, br_index * branch_per_shard, branch_per_shard)
        // branch_per_shard
    )
    incoming = own_owner * slot_match.shape[1] + slot_rank
    return (outgoing, incoming, own_owner)


def move_suffix(suffix_tokens, outgoing, incoming):
    dest_count = outgoing.shape[0]
    slot_count = outgoing.shape[1]
    tail_shape = suffix_tokens.shape[1:]
    outbound = suffix_tokens[outgoing.reshape(-1)].reshape((dest_count, slot_count) + tail_shape)
    arrived = lax.all_to_all(outbound, "br", split_axis=0, concat_axis=0, tiled=True)
    return arrived.reshape((dest_count * slot_count,) + tail_shape)[incoming]


def append_token(suffix_tokens, position_at, fresh_token):
    suffix_length = suffix_tokens.shape[2]
    target_mask = jnp.arange(suffix_length, dtype=jnp.int32)[None, :] == position_at[:, None]
    return jnp.where(
        target_mask[:, None, :, None], jnp.swapaxes(fresh_token, 0, 1)[:, :, None, :], suffix_tokens
    )


def general(
    prompt_key_value, suffix_page_store, page_table, lengths, parents, queries, fresh_key_value
):
    br_count = lax.axis_size("br")
    br_index = lax.axis_index("br")
    ctx_index = lax.axis_index("ctx")
    branch_per_shard = page_table.shape[0]
    page_count = page_table.shape[1]
    pool_dev = suffix_page_store.shape[0]
    page_rows = suffix_page_store.shape[2]
    head_width = suffix_page_store.shape[3]
    step_count = queries.shape[0]
    kv_local = head_width // HEAD_SIZE
    group_width = QUERY_HEADS // KEY_VALUE_HEADS
    slot_count = max(1, branch_per_shard // br_count)
    score_scale = 1.0 / math.sqrt(HEAD_SIZE)
    slot_rank = jnp.arange(branch_per_shard, dtype=jnp.int32) % slot_count
    slot_match = slot_rank[:, None] == jnp.arange(slot_count, dtype=jnp.int32)[None, :]
    gathered_pages = suffix_page_store[page_table - br_index * pool_dev]
    suffix_tokens = jnp.swapaxes(gathered_pages, 1, 2).reshape(
        branch_per_shard, 2, page_count * page_rows, head_width
    )
    length = lengths
    head_listing = lax.all_gather(queries, "ctx", axis=2, tiled=True)
    shared_prompt_keys = prompt_key_value[0].reshape(-1, KEY_VALUE_HEADS, HEAD_SIZE)
    shared_prompt_values = prompt_key_value[1].reshape(-1, KEY_VALUE_HEADS, HEAD_SIZE)
    outputs = []
    for decode_step_index in range(step_count):
        parent = parents[decode_step_index]
        outgoing, incoming, own_owner = routing(
            parent, branch_per_shard, br_index, slot_rank, slot_match
        )
        parent_length = length[parent]
        own_parent_length = lax.dynamic_slice_in_dim(
            parent_length, br_index * branch_per_shard, branch_per_shard
        )
        fresh_token = fresh_key_value[decode_step_index]
        query_mine = queries[decode_step_index].reshape(
            branch_per_shard, kv_local, group_width, HEAD_SIZE
        )
        suffix_tokens = append_token(
            move_suffix(suffix_tokens, outgoing, incoming), own_parent_length, fresh_token
        )
        suffix_part = suffix_stats(query_mine, suffix_tokens, own_parent_length + 1, score_scale)
        length = parent_length + 1
        query_complete = head_listing[decode_step_index].reshape(
            branch_per_shard, KEY_VALUE_HEADS, group_width, HEAD_SIZE
        )
        prompt_scores = (
            jnp.einsum(
                "bgrd,tgd->bgrt",
                query_complete,
                shared_prompt_keys,
                preferred_element_type=jnp.float32,
            )
            * score_scale
        )
        prompt_part = block_stats(prompt_scores, shared_prompt_values, "bgrt,tgd->bgrd")
        head_start = ctx_index * kv_local
        own_heads = tuple(
            (lax.dynamic_slice_in_dim(member, head_start, kv_local, 1) for member in prompt_part)
        )
        joined = fold_pair(own_heads, suffix_part)
        placed = tuple(
            (
                lax.dynamic_update_slice_in_dim(whole_part, own_part, head_start, 1)
                for whole_part, own_part in zip(prompt_part, joined)
            )
        )
        merged = joined_2((placed[0], placed[1], placed[2]), "ctx", fold_pair)
        combined = tuple(
            (lax.dynamic_slice_in_dim(member, head_start, kv_local, 1) for member in merged)
        )
        attention = (combined[2] / combined[1][..., None]).reshape(
            branch_per_shard, kv_local * group_width * HEAD_SIZE
        )
        outputs.append(attention.astype(jnp.bfloat16))
    return jnp.stack(outputs)


STEPS = 3
BRANCHES = 16
NODES = STEPS * BRANCHES
CAP = 8
LIVE = 96
FIRST = 16
KEYS = 4096
ROWS = 8 * NODES
MASKED = -1e30
EXP_SCALE = math.log2(math.e) / math.sqrt(HEAD_SIZE)
BF = jnp.bfloat16
F32 = jnp.float32
NT = (((1,), (1,)), ((), ()))


def onehot(condition):
    return jnp.where(condition, 1.0, 0.0).astype(BF)


def iota(shape, axis):
    return lax.broadcasted_iota(jnp.int32, shape, axis)


def stacked(rows, count, width):
    at = iota((count, width), 0)
    out = jnp.zeros((count, width), F32)
    for index, row in enumerate(rows):
        out = jnp.where(at == index, row.astype(F32), out)
    return out.astype(BF)


def dot(left, right):
    return jnp.dot(left, right, preferred_element_type=F32)


def dot_nt(left, right):
    return lax.dot_general(left, right, NT, preferred_element_type=F32)


def softmax_block(query, key, value):
    raw = dot_nt(query, key)
    peak = jnp.max(raw, axis=1, keepdims=True)
    weight = jnp.exp2((raw - peak) * EXP_SCALE)
    total = jnp.sum(weight, axis=1, keepdims=True)
    return peak, total, dot(weight.astype(BF), value)


def kernel(
    br_count, ctx_count,
    page_ref, len_ref, par_ref, q_ref, fresh_ref, pkv_ref, pages_ref,
    out_ref, flag_ref,
    kbuf, vbuf, kcat, vcat, qbuf, sendm, recvm, qcat, part_send, part_recv, suffix_stat, code_high, code_low,
    stat_send, stat_recv, ret_send, ret_recv, num,
    kv_sem, page_sem, q_send, q_recv, m_send, m_recv, p_send, p_recv, r_send, r_recv, s_send, s_recv,
):
    me_c = lax.axis_index("ctx")
    me_r = lax.axis_index("br")

    def peer_c(i):
        return lax.rem(me_c + i, ctx_count)

    def peer_r(i):
        return lax.rem(me_r + i, br_count)

    def head_at(i):
        chip = lax.rem(me_c // 2 + i // 2, ctx_count // 2)
        return chip * 2 + lax.rem(me_c + lax.rem(i, 2), 2)

    barrier = pltpu.get_barrier_semaphore()

    @pl.loop(1, ctx_count)
    def _(i):
        pl.semaphore_signal(barrier, inc=1, device_id={"ctx": peer_c(i)}, device_id_type=pl.DeviceIdType.MESH)

    @pl.loop(1, br_count)
    def _(i):
        pl.semaphore_signal(barrier, inc=1, device_id={"br": peer_r(i)}, device_id_type=pl.DeviceIdType.MESH)

    def kv_copy(i, which):
        g = head_at(i)
        buffer = kbuf if which == 0 else vbuf
        return pltpu.make_async_copy(
            pkv_ref.at[which, :, pl.ds(pl.multiple_of(g * HEAD_SIZE, HEAD_SIZE), HEAD_SIZE)],
            buffer.at[g], kv_sem.at[which, g])

    key_pages = pltpu.make_async_copy(pages_ref.at[:, 0], kcat.at[pl.ds(0, 32), :, pl.ds(0, HEAD_SIZE)], page_sem.at[0])
    value_pages = pltpu.make_async_copy(pages_ref.at[:, 1], vcat.at[pl.ds(0, 32)], page_sem.at[1])

    @pl.loop(0, ctx_count)
    def _(i):
        kv_copy(i, 0).start()
        kv_copy(i, 1).start()

    key_pages.start()
    value_pages.start()

    parent = par_ref[...]
    device = lax.shift_right_logical(parent, 4)
    place = parent & 15
    width = parent.shape[1]
    row_at = iota((width, width), 0)
    pick1 = onehot(row_at == parent[1:2])
    pick2 = onehot(row_at == parent[2:3])
    first = dot(stacked([device[0:1], place[0:1]], 16, width), pick1)
    second = dot(stacked([first[0:1], first[1:2], device[1:2], place[1:2]], 16, width), pick2)
    anc_dev = [device[0:1].astype(F32), first[0:1], second[0:1]]
    anc_loc = [place[0:1].astype(F32), first[1:2], second[1:2]]
    missing = jnp.full((1, width), -1.0, F32)
    par_hi = [missing, device[1:2].astype(F32), device[2:3].astype(F32) + 32.0]
    par_lo = [missing, place[1:2].astype(F32), place[2:3].astype(F32)]
    old_hi = [missing, missing, second[2:3]]
    old_lo = [missing, missing, second[3:4]]

    owner = iota((br_count, width), 0).astype(F32)
    to_owner = [onehot(owner == anc_dev[s]) for s in range(STEPS)]
    j = iota((128, 256), 0)
    lane = iota((128, 256), 1)
    b = lane & 127
    same_home = (j >> 4) == (b >> 4)
    counting = onehot(same_home & ((lane >= 128) | (j < b)))
    slots = [[], [], []]
    pair_count = []
    for tile in range(width // 128):
        cut = [m[:, tile * 128:(tile + 1) * 128] for m in to_owner]
        counted = dot(jnp.concatenate(cut, axis=0), counting)
        before = jnp.zeros((br_count, 128), F32)
        for s in range(STEPS):
            block = counted[s * br_count:(s + 1) * br_count]
            slots[s].append(jnp.sum(cut[s].astype(F32) * (block[:, :128] + before), axis=0, keepdims=True))
            before = before + block[:, 128:]
        pair_count.append(before)
    slot = [jnp.concatenate(parts, axis=1) for parts in slots]
    count = jnp.concatenate(pair_count, axis=1)
    most = jnp.max(count)
    fullest = jnp.max(jnp.sum(count, axis=1, keepdims=True)) / BRANCHES
    over = (most > CAP) | (fullest > LIVE)
    flag_ref[0, 0] = jnp.where(over, 1, 0)

    node = iota((128, STEPS * width), 0)
    column = iota((128, STEPS * width), 1)
    mine = onehot(((column & (width - 1)) == me_r * BRANCHES + (node & 15)) & ((node >> 4) == column // width))
    whither = jnp.concatenate([stacked([anc_dev[s], slot[s]], 16, width) for s in range(STEPS)], axis=1)
    own_row = dot_nt(whither, mine)
    own_col = dot_nt(mine, whither)
    own_addr_row = own_row[0:1] * CAP + own_row[1:2]
    own_addr_col = own_col[:NODES, 0:1] * CAP + own_col[:NODES, 1:2]
    at = iota((2 * CAP * br_count, 128), 0)
    is_node = iota((2 * CAP * br_count, 128), 1) < NODES
    placed = is_node & ((at >> 1).astype(F32) == own_addr_row)
    padding = jnp.zeros((128 - NODES, 640), BF)
    queries = q_ref[...]
    fresh_key = jnp.concatenate([fresh_ref[s, 0] for s in range(STEPS)], axis=0)
    fresh_value = jnp.concatenate([fresh_ref[s, 1] for s in range(STEPS)], axis=0)
    low = jnp.concatenate([jnp.concatenate([queries[:, :512], fresh_key], axis=1), padding], axis=0)
    high = jnp.concatenate([jnp.concatenate([queries[:, 512:], fresh_value], axis=1), padding], axis=0)
    sendm[...] = (dot(onehot(placed & ((at & 1) == 0)), low) + dot(onehot(placed & ((at & 1) == 1)), high)).astype(BF)

    def message(i, source):
        peer = peer_r(i)
        return pltpu.make_async_remote_copy(
            src_ref=sendm.at[pl.ds(pl.multiple_of(peer * 16, 16), 16)],
            dst_ref=recvm.at[pl.ds(pl.multiple_of(source * 16, 16), 16)],
            send_sem=m_send.at[peer], recv_sem=m_recv.at[source],
            device_id={"br": peer}, device_id_type=pl.DeviceIdType.MESH)

    def query_copy(i, source):
        peer = head_at(i)
        return pltpu.make_async_remote_copy(
            src_ref=q_ref, dst_ref=qbuf.at[source],
            send_sem=q_send.at[peer], recv_sem=q_recv.at[source],
            device_id={"ctx": peer}, device_id_type=pl.DeviceIdType.MESH)

    pl.semaphore_wait(barrier, ctx_count - 1 + br_count - 1)

    @pl.loop(1, ctx_count)
    def _(i):
        query_copy(i, me_c).start()

    @pl.loop(1, br_count)
    def _(i):
        message(i, me_r).start()

    own16 = pl.ds(pl.multiple_of(me_r * 16, 16), 16)
    recvm[own16, :] = sendm[own16, :]
    qbuf[me_c] = queries

    here = (iota((br_count, width), 0) == me_r).astype(F32)
    home_count = jnp.sum(here * count, axis=0, keepdims=True)
    col_at = iota((width, width), 1)
    earlier = onehot(((row_at & 15) == 0) & ((row_at >> 4) < (col_at >> 4)))
    ahead = dot(stacked([home_count], 16, width), earlier)[0:1]
    home = lax.shift_right_logical(iota((1, width), 1), 4).astype(F32)
    local_at = (iota((1, width), 1) & 15).astype(F32)
    ones = jnp.ones((1, width), F32)
    live_rows = iota((128, width), 0).astype(F32)
    chosen, known = [], []
    for s in range(STEPS):
        arrives = anc_dev[s] == me_r.astype(F32)
        place_at = jnp.where(arrives, ahead + slot[s] + FIRST, -1.0)
        chosen.append(onehot(live_rows == place_at))
        known.append(stacked([
            ones, home, slot[s], anc_loc[s], home + 32.0 * s, local_at,
            par_hi[s], par_lo[s], old_hi[s], old_lo[s]], 16, width))
    chosen = jnp.concatenate(chosen, axis=1)
    known = jnp.concatenate(known, axis=1)
    row_info = dot_nt(known, chosen)
    col_info = dot_nt(chosen, known)[FIRST:FIRST + LIVE]
    addr_row = jnp.where(row_info[0:1] > 0.5, row_info[1:2] * CAP + row_info[2:3], -1.0)
    addr_col = jnp.where(col_info[:, 0:1] > 0.5, col_info[:, 1:2] * CAP + col_info[:, 2:3], -1.0)
    self_col = jnp.where(col_info[:, 0:1] > 0.5, col_info[:, 4:5] * 16.0 + col_info[:, 5:6], -100.0)
    lane_live = iota((LIVE, 128), 1)
    extra_query = onehot((lane_live.astype(F32) == col_info[:, 3:4]) | (lane_live == iota((LIVE, 128), 0) + FIRST))
    on_path = self_col == row_info[4:5] * 16.0 + row_info[5:6]
    on_path = on_path | (self_col == row_info[6:7] * 16.0 + row_info[7:8])
    on_path = on_path | (self_col == row_info[8:9] * 16.0 + row_info[9:10])
    seen = on_path | ((lane_live < FIRST) & (self_col > -1.0))
    kcat[32, pl.ds(0, LIVE), pl.ds(128, 128)] = jnp.where(seen, 0.0, MASKED).astype(BF)
    kcat[32, pl.ds(LIVE, 128 - LIVE), pl.ds(128, 128)] = jnp.full((128 - LIVE, 128), MASKED, BF)
    kcat[32, pl.ds(LIVE, 128 - LIVE), pl.ds(0, 128)] = jnp.zeros((128 - LIVE, 128), BF)
    vcat[32, pl.ds(LIVE, 128 - LIVE)] = jnp.zeros((128 - LIVE, 128), BF)

    page_at = iota((32, 128), 0)
    page_lane = iota((32, 128), 1)
    live = jnp.where(page_lane < FIRST, 0, 128)
    for branch in range(BRANCHES):
        length = len_ref[me_r * BRANCHES + branch]
        for page in range(2):
            number = page_ref[page, branch] - me_r * 32
            held = jnp.clip(length - 128 * page, 0, 128)
            live = jnp.where((page_at == number) & (page_lane == branch), held, live)
    position = iota((128, 128), 0)
    for page in range(32):
        kcat[page, :, pl.ds(128, 128)] = jnp.where(position < live[page:page + 1], 0.0, MASKED).astype(BF)

    stat_lane = iota((NODES, 128), 1)

    def part_copy(i, source):
        peer = head_at(i)
        return pltpu.make_async_remote_copy(
            src_ref=part_send.at[peer], dst_ref=part_recv.at[source],
            send_sem=p_send.at[peer], recv_sem=p_recv.at[source],
            device_id={"ctx": peer}, device_id_type=pl.DeviceIdType.MESH)

    @pl.loop(0, ctx_count)
    def _(i):
        g = head_at(i)

        @pl.when(i > 0)
        def _():
            query_copy(i, g).wait_recv()

        kv_copy(i, 0).wait()
        kv_copy(i, 1).wait()
        key = kbuf[g]
        value = vbuf[g]
        stat = jnp.zeros((NODES, 128), F32)
        for half in range(2):
            rows = jnp.concatenate(
                [qbuf[g, :, pl.ds((4 * half + h) * 128, 128)] for h in range(4)], axis=0)
            peak, total, summed = softmax_block(rows, key, value)
            part_send[g, pl.ds(half * 4 * NODES, 4 * NODES)] = summed
            for h in range(4):
                cut = slice(h * NODES, (h + 1) * NODES)
                stat = jnp.where(stat_lane == 4 * half + h, peak[cut], stat)
                stat = jnp.where(stat_lane == 8 + 4 * half + h, total[cut], stat)
        part_send[g, pl.ds(ROWS, NODES)] = stat

        @pl.when(i > 0)
        def _():
            part_copy(i, me_c).start()

    @pl.loop(1, br_count)
    def _(i):
        message(0, peer_r(i)).wait_recv()

    gather = iota((LIVE, 2 * CAP * br_count), 1)
    taken = (gather >> 1).astype(F32) == addr_col
    got = recvm[...]
    got_low = dot(onehot(taken & ((gather & 1) == 0)), got).astype(BF)
    got_high = dot(onehot(taken & ((gather & 1) == 1)), got).astype(BF)
    kcat[32, pl.ds(0, LIVE), pl.ds(0, 128)] = got_low[:, 512:]
    vcat[32, pl.ds(0, LIVE)] = got_high[:, 512:]
    for h in range(8):
        source = got_low if h < 4 else got_high
        qcat[pl.ds(h * LIVE, LIVE), pl.ds(0, 128)] = source[:, (h % 4) * 128:(h % 4 + 1) * 128]
        qcat[pl.ds(h * LIVE, LIVE), pl.ds(128, 128)] = extra_query
    key_pages.wait()
    value_pages.wait()
    live_lane = iota((LIVE, 128), 1)
    lane_rows = iota((4 * LIVE, 128), 1)
    @pl.loop(0, 2)
    def _(part):
        key = kcat[...].reshape(33 * 128, 256)
        value = vcat[...].reshape(33 * 128, 128)
        rows = pl.ds(pl.multiple_of(part * 4 * LIVE, 4 * LIVE), 4 * LIVE)
        peak, total, summed = softmax_block(qcat[rows], key, value)
        largest = jnp.max(jnp.abs(summed), axis=1, keepdims=True)
        unit = largest / 32767.0
        coded = jnp.round(summed * jnp.where(largest > 0.0, 32767.0 / largest, 0.0))
        upper = jnp.floor(coded / 256.0)
        code_high[rows] = upper.astype(BF)
        code_low[rows] = (coded - 256.0 * upper).astype(BF)
        suffix_stat[rows] = jnp.where(
            lane_rows == 0, peak, jnp.where(lane_rows == 1, total, unit))

    address = addr_row[:, FIRST:FIRST + LIVE]
    back = jnp.where(iota((CAP * br_count, LIVE), 0).astype(F32) == address, 1.0, 0.0)
    stat = jnp.zeros((LIVE, 128), F32)
    for h in range(8):
        for kind in range(3):
            stat = jnp.where(live_lane == 8 * kind + h, suffix_stat[pl.ds(h * LIVE, LIVE), kind:kind + 1], stat)
    stat_send[...] = jnp.dot(back, stat, precision=lax.Precision.HIGHEST, preferred_element_type=F32)
    slot_row = iota((2 * CAP * br_count, LIVE), 0)
    held = (slot_row >> 1).astype(F32) == address
    spread = jnp.concatenate([onehot(held & ((slot_row & 1) == half)) for half in range(2)], axis=1)

    def rowed(code, h):
        return jnp.concatenate([code[pl.ds(h * LIVE, LIVE)], code[pl.ds((h + 4) * LIVE, LIVE)]], axis=0)

    for h in range(4):
        upper = dot(spread, rowed(code_high, h))
        lower = dot(spread, rowed(code_low, h))
        ret_send[:, pl.ds(h * 128, 128)] = (256.0 * upper + lower).astype(jnp.int32).astype(jnp.int16)

    def returned(i, source):
        peer = peer_r(i)
        return pltpu.make_async_remote_copy(
            src_ref=ret_send.at[pl.ds(pl.multiple_of(peer * 16, 16), 16)],
            dst_ref=ret_recv.at[pl.ds(pl.multiple_of(source * 16, 16), 16)],
            send_sem=r_send.at[peer], recv_sem=r_recv.at[source],
            device_id={"br": peer}, device_id_type=pl.DeviceIdType.MESH)

    def returned_stat(i, source):
        peer = peer_r(i)
        return pltpu.make_async_remote_copy(
            src_ref=stat_send.at[pl.ds(pl.multiple_of(peer * CAP, CAP), CAP)],
            dst_ref=stat_recv.at[pl.ds(pl.multiple_of(source * CAP, CAP), CAP)],
            send_sem=s_send.at[peer], recv_sem=s_recv.at[source],
            device_id={"br": peer}, device_id_type=pl.DeviceIdType.MESH)

    @pl.loop(1, br_count)
    def _(i):
        returned_stat(i, me_r).start()
        returned(i, me_r).start()

    own8 = pl.ds(pl.multiple_of(me_r * CAP, CAP), CAP)
    stat_recv[own8, :] = stat_send[own8, :]
    ret_recv[own16, :] = ret_send[own16, :]

    part_recv[me_c] = part_send[me_c]

    @pl.loop(1, ctx_count)
    def _(i):
        part_copy(0, head_at(i)).wait_recv()

    stats = [part_recv[c, pl.ds(ROWS, NODES)] for c in range(8)]
    top = functools.reduce(jnp.maximum, stats)
    factors = [jnp.exp2((stat - top) * EXP_SCALE) for stat in stats]
    den = jnp.zeros((NODES, 128), F32)
    for c in range(8):
        den = den + factors[c] * pltpu.roll(stats[c], 120, 1)
    for h in range(8):
        summed = jnp.zeros((NODES, 128), F32)
        for c in range(8):
            summed = summed + factors[c][:, h:h + 1] * part_recv[c, pl.ds(h * NODES, NODES)]
        num[h] = summed

    @pl.loop(1, br_count)
    def _(i):
        returned_stat(0, peer_r(i)).wait_recv()
        returned(0, peer_r(i)).wait_recv()

    mine_back = jnp.where(iota((NODES, CAP * br_count), 1).astype(F32) == own_addr_col, 1.0, 0.0)
    back_stat = jnp.dot(mine_back, stat_recv[...], precision=lax.Precision.HIGHEST, preferred_element_type=F32)
    slot_at = iota((NODES, 2 * CAP * br_count), 1)
    mine_at = (slot_at >> 1).astype(F32) == own_addr_col
    collect = jnp.concatenate([onehot(mine_at & ((slot_at & 1) == half)) for half in range(2)], axis=0)
    arrived = ret_recv[...].astype(jnp.int32)
    upper = dot(collect, (arrived >> 8).astype(F32).astype(BF))
    lower = dot(collect, (arrived & 255).astype(F32).astype(BF))
    coded = 256.0 * upper + lower
    overall = jnp.maximum(top, back_stat)
    prompt_factor = jnp.exp2((top - overall) * EXP_SCALE)
    suffix_factor = jnp.exp2((back_stat - overall) * EXP_SCALE)
    den = prompt_factor * den + suffix_factor * pltpu.roll(back_stat, 120, 1)
    unit = suffix_factor * pltpu.roll(back_stat, 112, 1)
    for h in range(8):
        back_home = coded[(h // 4) * NODES:(h // 4 + 1) * NODES, (h % 4) * 128:(h % 4 + 1) * 128]
        joined = prompt_factor[:, h:h + 1] * num[h] + unit[:, h:h + 1] * back_home
        out_ref[:, pl.ds(h * 128, 128)] = (joined / den[:, h:h + 1]).astype(BF)

    @pl.loop(1, ctx_count)
    def _(i):
        query_copy(i, me_c).wait_send()
        part_copy(i, me_c).wait_send()

    @pl.loop(1, br_count)
    def _(i):
        message(i, me_r).wait_send()
        returned_stat(i, me_r).wait_send()
        returned(i, me_r).wait_send()


def local(
    prompt_key_value, suffix_page_store, page_table, lengths, parents, queries, fresh_key_value
):
    br_count = lax.axis_size("br")
    ctx_count = lax.axis_size("ctx")
    vmem = pl.BlockSpec(memory_space=pltpu.VMEM)
    smem = pl.BlockSpec(memory_space=pltpu.SMEM)
    anywhere = pl.BlockSpec(memory_space=pl.ANY)
    dma = pltpu.SemaphoreType.DMA
    slots = CAP * br_count
    out, flag = pl.pallas_call(
        functools.partial(kernel, br_count, ctx_count),
        out_shape=(
            jax.ShapeDtypeStruct((NODES, 1024), BF),
            jax.ShapeDtypeStruct((1, 1), jnp.int32),
        ),
        in_specs=[smem, smem, vmem, vmem, vmem, anywhere, anywhere],
        out_specs=(vmem, smem),
        scratch_shapes=[
            pltpu.VMEM((8, 2048, 128), BF),
            pltpu.VMEM((8, 2048, 128), BF),
            pltpu.VMEM((33, 128, 256), BF),
            pltpu.VMEM((33, 128, 128), BF),
            pltpu.VMEM((8, NODES, 1024), BF),
            pltpu.VMEM((2 * slots, 640), BF),
            pltpu.VMEM((2 * slots, 640), BF),
            pltpu.VMEM((8 * LIVE, 256), BF),
            pltpu.VMEM((8, ROWS + NODES, 128), F32),
            pltpu.VMEM((8, ROWS + NODES, 128), F32),
            pltpu.VMEM((8 * LIVE, 128), F32),
            pltpu.VMEM((8 * LIVE, 128), BF),
            pltpu.VMEM((8 * LIVE, 128), BF),
            pltpu.VMEM((slots, 128), F32),
            pltpu.VMEM((slots, 128), F32),
            pltpu.VMEM((2 * slots, 512), jnp.int16),
            pltpu.VMEM((2 * slots, 512), jnp.int16),
            pltpu.VMEM((8, NODES, 128), F32),
            dma((2, 8)), dma((2,)), dma((8,)), dma((8,)), dma((32,)), dma((32,)),
            dma((8,)), dma((8,)), dma((32,)), dma((32,)), dma((32,)), dma((32,)),
        ],
        compiler_params=pltpu.CompilerParams(
            collective_id=0, has_side_effects=True, vmem_limit_bytes=56 * 1024 * 1024
        ),
    )(
        page_table.T, lengths, parents, queries.reshape(NODES, 1024), fresh_key_value,
        prompt_key_value, suffix_page_store,
    )
    operands = (
        prompt_key_value, suffix_page_store, page_table, lengths, parents, queries, fresh_key_value
    )
    return lax.cond(
        flag[0, 0] > 0,
        lambda *whole: general(*whole),
        lambda *whole: out.reshape(STEPS, BRANCHES, 1024),
        *operands,
    )


def solution(mesh):
    in_specs = (
        P(None, "ctx", None),
        P("br", None, None, "ctx"),
        P("br", None),
        P(),
        P(),
        P(None, "br", "ctx"),
        P(None, None, "br", "ctx"),
    )
    out_specs = P(None, "br", "ctx")
    return jax.shard_map(local, mesh=mesh, in_specs=in_specs, out_specs=out_specs, check_vma=False)
```

```python
import functools
import math

import jax
import jax.numpy as jnp
from jax import lax
from jax.experimental import pallas as pl
from jax.experimental.pallas import tpu as pltpu
from jax.sharding import PartitionSpec as P

QUERY_HEADS = 64
KEY_VALUE_HEADS = 8
HEAD_SIZE = 128


NEG_FILL = -1e30


def joined_2(part, axis, combine):
    gathered = jax.tree.map(lambda a: lax.all_gather(a, axis), part)

    def take(source):
        return jax.tree.map(lambda a: lax.dynamic_index_in_dim(a, source, 0, False), gathered)

    return lax.fori_loop(
        1, lax.axis_size(axis), lambda source, state: combine(state, take(source)), take(0)
    )


def block_stats(scores, values, einsum_form):
    peak_value = jnp.max(scores, axis=-1)
    weights = jnp.exp(scores - peak_value[..., None])
    weight_total = jnp.sum(weights, axis=-1)
    rounded = weights.astype(jnp.bfloat16)
    summed = jnp.einsum(einsum_form, rounded, values, preferred_element_type=jnp.float32)
    return (peak_value, weight_total, summed)


def fold_pair(left_stats, right_stats):
    peak_value = jnp.maximum(left_stats[0], right_stats[0])
    left_weight = jnp.exp(left_stats[0] - peak_value)
    right_weight = jnp.exp(right_stats[0] - peak_value)
    weight_total = left_stats[1] * left_weight + right_stats[1] * right_weight
    summed = left_stats[2] * left_weight[..., None] + right_stats[2] * right_weight[..., None]
    return (peak_value, weight_total, summed)


def suffix_stats(query_head_rows, suffix_tokens, live_length, score_scale):
    row_count = suffix_tokens.shape[0]
    suffix_length = suffix_tokens.shape[2]
    kv_local = query_head_rows.shape[1]
    branch_suffix_keys = suffix_tokens[:, 0].reshape(row_count, suffix_length, kv_local, HEAD_SIZE)
    branch_suffix_values = suffix_tokens[:, 1].reshape(
        row_count, suffix_length, kv_local, HEAD_SIZE
    )
    scores = (
        jnp.einsum(
            "bgrd,btgd->bgrt",
            query_head_rows,
            branch_suffix_keys,
            preferred_element_type=jnp.float32,
        )
        * score_scale
    )
    live_mask = jnp.arange(suffix_length, dtype=jnp.int32)[None, :] < live_length[:, None]
    scores = jnp.where(live_mask[:, None, None, :], scores, NEG_FILL)
    return block_stats(scores, branch_suffix_values, "bgrt,btgd->bgrd")


def routing(parent, branch_per_shard, br_index, slot_rank, slot_match):
    grid_owner = (parent // branch_per_shard).reshape(-1, branch_per_shard)
    grid_local = (parent % branch_per_shard).reshape(-1, branch_per_shard)
    matched = (grid_owner == br_index)[:, :, None] & slot_match[None, :, :]
    outgoing = jnp.sum(jnp.where(matched, grid_local[:, :, None], 0), axis=1)
    own_owner = (
        lax.dynamic_slice_in_dim(parent, br_index * branch_per_shard, branch_per_shard)
        // branch_per_shard
    )
    incoming = own_owner * slot_match.shape[1] + slot_rank
    return (outgoing, incoming, own_owner)


def move_suffix(suffix_tokens, outgoing, incoming):
    dest_count = outgoing.shape[0]
    slot_count = outgoing.shape[1]
    tail_shape = suffix_tokens.shape[1:]
    outbound = suffix_tokens[outgoing.reshape(-1)].reshape((dest_count, slot_count) + tail_shape)
    arrived = lax.all_to_all(outbound, "br", split_axis=0, concat_axis=0, tiled=True)
    return arrived.reshape((dest_count * slot_count,) + tail_shape)[incoming]


def append_token(suffix_tokens, position_at, fresh_token):
    suffix_length = suffix_tokens.shape[2]
    target_mask = jnp.arange(suffix_length, dtype=jnp.int32)[None, :] == position_at[:, None]
    return jnp.where(
        target_mask[:, None, :, None], jnp.swapaxes(fresh_token, 0, 1)[:, :, None, :], suffix_tokens
    )


def general(
    prompt_key_value, suffix_page_store, page_table, lengths, parents, queries, fresh_key_value
):
    br_count = lax.axis_size("br")
    br_index = lax.axis_index("br")
    ctx_index = lax.axis_index("ctx")
    branch_per_shard = page_table.shape[0]
    page_count = page_table.shape[1]
    pool_dev = suffix_page_store.shape[0]
    page_rows = suffix_page_store.shape[2]
    head_width = suffix_page_store.shape[3]
    step_count = queries.shape[0]
    kv_local = head_width // HEAD_SIZE
    group_width = QUERY_HEADS // KEY_VALUE_HEADS
    slot_count = max(1, branch_per_shard // br_count)
    score_scale = 1.0 / math.sqrt(HEAD_SIZE)
    slot_rank = jnp.arange(branch_per_shard, dtype=jnp.int32) % slot_count
    slot_match = slot_rank[:, None] == jnp.arange(slot_count, dtype=jnp.int32)[None, :]
    gathered_pages = suffix_page_store[page_table - br_index * pool_dev]
    suffix_tokens = jnp.swapaxes(gathered_pages, 1, 2).reshape(
        branch_per_shard, 2, page_count * page_rows, head_width
    )
    length = lengths
    head_listing = lax.all_gather(queries, "ctx", axis=2, tiled=True)
    shared_prompt_keys = prompt_key_value[0].reshape(-1, KEY_VALUE_HEADS, HEAD_SIZE)
    shared_prompt_values = prompt_key_value[1].reshape(-1, KEY_VALUE_HEADS, HEAD_SIZE)
    outputs = []
    for decode_step_index in range(step_count):
        parent = parents[decode_step_index]
        outgoing, incoming, own_owner = routing(
            parent, branch_per_shard, br_index, slot_rank, slot_match
        )
        parent_length = length[parent]
        own_parent_length = lax.dynamic_slice_in_dim(
            parent_length, br_index * branch_per_shard, branch_per_shard
        )
        fresh_token = fresh_key_value[decode_step_index]
        query_mine = queries[decode_step_index].reshape(
            branch_per_shard, kv_local, group_width, HEAD_SIZE
        )
        suffix_tokens = append_token(
            move_suffix(suffix_tokens, outgoing, incoming), own_parent_length, fresh_token
        )
        suffix_part = suffix_stats(query_mine, suffix_tokens, own_parent_length + 1, score_scale)
        length = parent_length + 1
        query_complete = head_listing[decode_step_index].reshape(
            branch_per_shard, KEY_VALUE_HEADS, group_width, HEAD_SIZE
        )
        prompt_scores = (
            jnp.einsum(
                "bgrd,tgd->bgrt",
                query_complete,
                shared_prompt_keys,
                preferred_element_type=jnp.float32,
            )
            * score_scale
        )
        prompt_part = block_stats(prompt_scores, shared_prompt_values, "bgrt,tgd->bgrd")
        head_start = ctx_index * kv_local
        own_heads = tuple(
            (lax.dynamic_slice_in_dim(member, head_start, kv_local, 1) for member in prompt_part)
        )
        joined = fold_pair(own_heads, suffix_part)
        placed = tuple(
            (
                lax.dynamic_update_slice_in_dim(whole_part, own_part, head_start, 1)
                for whole_part, own_part in zip(prompt_part, joined)
            )
        )
        merged = joined_2((placed[0], placed[1], placed[2]), "ctx", fold_pair)
        combined = tuple(
            (lax.dynamic_slice_in_dim(member, head_start, kv_local, 1) for member in merged)
        )
        attention = (combined[2] / combined[1][..., None]).reshape(
            branch_per_shard, kv_local * group_width * HEAD_SIZE
        )
        outputs.append(attention.astype(jnp.bfloat16))
    return jnp.stack(outputs)


STEPS = 3
BRANCHES = 16
NODES = STEPS * BRANCHES
CAP = 8
QUAD = 4
LIVE = 96
LATE = 16
ROWS = 8 * NODES
MASKED = -1e30
EXP_SCALE = math.log2(math.e) / math.sqrt(HEAD_SIZE)
BF = jnp.bfloat16
F32 = jnp.float32
NT = (((1,), (1,)), ((), ()))


def onehot(condition):
    return jnp.where(condition, 1.0, 0.0).astype(BF)


def iota(shape, axis):
    return lax.broadcasted_iota(jnp.int32, shape, axis)


def stacked(rows, count, width):
    at = iota((count, width), 0)
    out = jnp.zeros((count, width), F32)
    for index, row in enumerate(rows):
        out = jnp.where(at == index, row.astype(F32), out)
    return out.astype(BF)


def dot(left, right):
    return jnp.dot(left, right, preferred_element_type=F32)


def dot_nt(left, right):
    return lax.dot_general(left, right, NT, preferred_element_type=F32)


def softmax_block(query, key, value):
    raw = dot_nt(query, key)
    peak = jnp.max(raw, axis=1, keepdims=True)
    weight = jnp.exp2((raw - peak) * EXP_SCALE)
    total = jnp.sum(weight, axis=1, keepdims=True)
    return peak, total, dot(weight.astype(BF), value)


def kernel(
    br_count, ctx_count,
    page_ref, len_ref, par_ref, q_ref, fresh_ref, pkv_ref, pages_ref,
    out_ref, flag_ref,
    kbuf, vbuf, kpage, vpage, qbuf, send_a, recv_a, send_b, recv_b, qrows, part_send, part_recv,
    code_high, code_low, late_high, late_low, stat_send, stat_recv, ret_send, ret_recv, num,
    kv_sem, g_send, g_recv, page_sem, q_send, q_recv, a_send, a_recv, b_send, b_recv, p_send, p_recv,
    r_send, r_recv, s_send, s_recv,
):
    me_c = lax.axis_index("ctx")
    me_r = lax.axis_index("br")

    core = lax.rem(me_c, 2)
    chip = me_c // 2
    chips = ctx_count // 2
    partner = me_c + 1 - 2 * core

    def peer_r(i):
        return lax.rem(me_r + i, br_count)

    def chip_at(t):
        return lax.rem(chip + t, chips)

    barrier = pltpu.get_barrier_semaphore()

    @pl.loop(1, chips)
    def _(t):
        pl.semaphore_signal(
            barrier, inc=1, device_id={"ctx": chip_at(t) * 2 + core}, device_id_type=pl.DeviceIdType.MESH)

    pl.semaphore_signal(barrier, inc=1, device_id={"ctx": partner}, device_id_type=pl.DeviceIdType.MESH)

    @pl.loop(1, br_count)
    def _(i):
        pl.semaphore_signal(barrier, inc=1, device_id={"br": peer_r(i)}, device_id_type=pl.DeviceIdType.MESH)

    def head_columns(t, parity):
        return pl.ds(pl.multiple_of((chip_at(t) * 2 + parity) * HEAD_SIZE, HEAD_SIZE), HEAD_SIZE)

    def kv_copy(t, which):
        buffer = kbuf if which == 0 else vbuf
        return pltpu.make_async_copy(
            pkv_ref.at[which, :, head_columns(t, core)], buffer.at[t, 0], kv_sem.at[which, t])

    def kv_give(t, which):
        buffer = kbuf if which == 0 else vbuf
        return pltpu.make_async_remote_copy(
            src_ref=pkv_ref.at[which, :, head_columns(t, 1 - core)], dst_ref=buffer.at[t, 1],
            send_sem=g_send.at[which, t], recv_sem=g_recv.at[which, t],
            device_id={"ctx": partner}, device_id_type=pl.DeviceIdType.MESH)

    key_pages = pltpu.make_async_copy(pages_ref.at[:, 0], kpage, page_sem.at[0])
    value_pages = pltpu.make_async_copy(pages_ref.at[:, 1], vpage, page_sem.at[1])

    @pl.loop(0, chips)
    def _(t):
        kv_copy(t, 0).start()
        kv_copy(t, 1).start()

    key_pages.start()
    value_pages.start()

    parent = par_ref[...]
    device = lax.shift_right_logical(parent, 4)
    place = parent & 15
    width = parent.shape[1]
    row_at = iota((width, width), 0)
    pick1 = onehot(row_at == parent[1:2])
    pick2 = onehot(row_at == parent[2:3])
    first = dot(stacked([device[0:1], place[0:1]], 16, width), pick1)
    second = dot(stacked([first[0:1], first[1:2], device[1:2], place[1:2]], 16, width), pick2)
    anc_dev = [device[0:1].astype(F32), first[0:1], second[0:1]]
    anc_loc = [place[0:1].astype(F32), first[1:2], second[1:2]]
    missing = jnp.full((1, width), -1.0, F32)
    par_hi = [missing, device[1:2].astype(F32), device[2:3].astype(F32) + 32.0]
    par_lo = [missing, place[1:2].astype(F32), place[2:3].astype(F32)]
    old_hi = [missing, missing, second[2:3]]
    old_lo = [missing, missing, second[3:4]]

    owner = iota((br_count, width), 0).astype(F32)
    to_owner = [onehot(owner == anc_dev[s]) for s in range(STEPS)]
    j = iota((128, 256), 0)
    lane = iota((128, 256), 1)
    b = lane & 127
    same_home = (j >> 4) == (b >> 4)
    counting = onehot(same_home & ((lane >= 128) | (j < b)))
    slots = [[], [], []]
    pair_count = []
    for tile in range(width // 128):
        cut = [m[:, tile * 128:(tile + 1) * 128] for m in to_owner]
        counted = dot(jnp.concatenate(cut, axis=0), counting)
        before = jnp.zeros((br_count, 128), F32)
        for s in range(STEPS):
            block = counted[s * br_count:(s + 1) * br_count]
            slots[s].append(jnp.sum(cut[s].astype(F32) * (block[:, :128] + before), axis=0, keepdims=True))
            before = before + block[:, 128:]
        pair_count.append(before)
    slot = [jnp.concatenate(parts, axis=1) for parts in slots]
    count = jnp.concatenate(pair_count, axis=1)
    most = jnp.max(count)
    first_count = jnp.minimum(count, QUAD)
    fullest = jnp.max(jnp.sum(first_count, axis=1, keepdims=True)) / BRANCHES
    latest = jnp.max(jnp.sum(count - first_count, axis=1, keepdims=True)) / BRANCHES
    over = (most > CAP) | (fullest > LIVE) | (latest > LATE)
    flag_ref[0, 0] = jnp.where(over, 1, 0)

    node = iota((128, STEPS * width), 0)
    column = iota((128, STEPS * width), 1)
    mine = onehot(((column & (width - 1)) == me_r * BRANCHES + (node & 15)) & ((node >> 4) == column // width))
    whither = jnp.concatenate([stacked([anc_dev[s], slot[s]], 16, width) for s in range(STEPS)], axis=1)
    own_row = dot_nt(whither, mine)
    own_col = dot_nt(mine, whither)
    own_dev, own_slot = own_col[:NODES, 0:1], own_col[:NODES, 1:2]
    at = iota((16 * br_count, 128), 0)
    is_node = iota((16 * br_count, 128), 1) < NODES
    own_pair = is_node & ((at >> 1).astype(F32) == own_row[0:1] * CAP + own_row[1:2])
    quad_row = own_row[0:1] * QUAD + own_row[1:2]
    own_first = is_node & (own_row[1:2] < QUAD) & ((at >> 2).astype(F32) == quad_row)
    own_late = is_node & (own_row[1:2] >= QUAD) & ((at >> 2).astype(F32) == quad_row - QUAD)
    queries = q_ref[...]

    def padded(rows):
        return jnp.concatenate([rows, jnp.zeros((128 - NODES, rows.shape[1]), BF)], axis=0)

    fresh = [padded(jnp.concatenate([fresh_ref[s, kind] for s in range(STEPS)], axis=0)) for kind in range(2)]
    quarters = jnp.concatenate([padded(queries[:, 256 * n:256 * (n + 1)]) for n in range(4)], axis=0)

    def spread_over(rows, parts, mask):
        return jnp.concatenate([onehot(mask & ((rows & (parts - 1)) == part)) for part in range(parts)], axis=1)

    send_a[:, pl.ds(0, 256)] = dot(spread_over(at, 4, own_first), quarters).astype(BF)
    send_a[:, pl.ds(256, 128)] = dot(spread_over(at, 2, own_pair), jnp.concatenate(fresh, axis=0)).astype(BF)
    send_b[...] = dot(spread_over(at, 4, own_late), quarters).astype(BF)

    def rows16(index):
        return pl.ds(pl.multiple_of(index * 16, 16), 16)

    def to_br(i, source, send, recv, send_sem, recv_sem):
        peer = peer_r(i)
        return pltpu.make_async_remote_copy(
            src_ref=send.at[rows16(peer)], dst_ref=recv.at[rows16(source)],
            send_sem=send_sem.at[peer], recv_sem=recv_sem.at[source],
            device_id={"br": peer}, device_id_type=pl.DeviceIdType.MESH)

    def message_a(i, source):
        return to_br(i, source, send_a, recv_a, a_send, a_recv)

    def message_b(i, source):
        return to_br(i, source, send_b, recv_b, b_send, b_recv)

    def query_copy(t, source):
        return pltpu.make_async_remote_copy(
            src_ref=q_ref, dst_ref=qbuf.at[source],
            send_sem=q_send.at[t], recv_sem=q_recv.at[source],
            device_id={"ctx": chip_at(t) * 2 + core}, device_id_type=pl.DeviceIdType.MESH)

    pl.semaphore_wait(barrier, chips + br_count - 1)

    @pl.loop(1, chips)
    def _(t):
        query_copy(t, chip).start()
        kv_give(t, 0).start()
        kv_give(t, 1).start()

    kv_give(0, 0).start()
    kv_give(0, 1).start()

    @pl.loop(1, br_count)
    def _(i):
        message_a(i, me_r).start()

    @pl.loop(1, br_count)
    def _(i):
        message_b(i, me_r).start()

    own16 = rows16(me_r)
    recv_a[own16, :] = send_a[own16, :]
    recv_b[own16, :] = send_b[own16, :]
    qbuf[chip] = queries

    here = (iota((br_count, width), 0) == me_r).astype(F32)
    home_count = jnp.sum(here * count, axis=0, keepdims=True)
    col_at = iota((width, width), 1)
    earlier = onehot(((row_at & 15) == 0) & ((row_at >> 4) < (col_at >> 4)))
    home_first = jnp.minimum(home_count, QUAD)
    ahead = dot(stacked([home_first, home_count - home_first], 16, width), earlier)
    home = lax.shift_right_logical(iota((1, width), 1), 4).astype(F32)
    local_at = (iota((1, width), 1) & 15).astype(F32)
    ones = jnp.ones((1, width), F32)
    live_rows = iota((128, width), 0).astype(F32)
    chosen, known = [], []
    for s in range(STEPS):
        arrives = anc_dev[s] == me_r.astype(F32)
        first_at = ahead[0:1] + slot[s]
        late_at = ahead[1:2] + slot[s] - QUAD
        late_at = jnp.where((slot[s] < CAP) & (late_at < LATE), late_at + LIVE, -1.0)
        place_at = jnp.where(slot[s] < QUAD, jnp.where(first_at < LIVE, first_at, -1.0), late_at)
        place_at = jnp.where(arrives, place_at, -1.0)
        chosen.append(onehot(live_rows == place_at))
        known.append(stacked([
            ones, home, slot[s], anc_loc[s], home + 32.0 * s, local_at,
            par_hi[s], par_lo[s], old_hi[s], old_lo[s]], 16, width))
    chosen = jnp.concatenate(chosen, axis=1)
    known = jnp.concatenate(known, axis=1)
    row_info = dot_nt(known, chosen)
    col_info = dot_nt(chosen, known)
    here_row = row_info[0:1] > 0.5
    here_col = col_info[:, 0:1] > 0.5
    slot_row, slot_col = row_info[2:3], col_info[:, 2:3]
    pair_col = jnp.where(here_col, col_info[:, 1:2] * CAP + slot_col, -1.0)
    quad_col = jnp.where(here_col, col_info[:, 1:2] * QUAD + slot_col, -1.0)
    quad_row = jnp.where(here_row, row_info[1:2] * QUAD + slot_row, -1.0)
    self_row = jnp.where(here_row, row_info[4:5] * 16.0 + row_info[5:6], -100.0)
    on_path = self_row == col_info[:, 4:5] * 16.0 + col_info[:, 5:6]
    on_path = on_path | (self_row == col_info[:, 6:7] * 16.0 + col_info[:, 7:8])
    on_path = on_path | (self_row == col_info[:, 8:9] * 16.0 + col_info[:, 9:10])
    path = jnp.where(on_path, 1.0, 0.0)
    anc_col = col_info[:, 3:4]
    length_col = jnp.zeros((128, 1), F32)
    for branch in range(BRANCHES):
        length_col = jnp.where(anc_col == branch, len_ref[me_r * BRANCHES + branch].astype(F32), length_col)

    stat_lane = iota((NODES, 128), 1)

    def part_copy(t, source):
        peer = chip_at(t)
        return pltpu.make_async_remote_copy(
            src_ref=part_send.at[peer], dst_ref=part_recv.at[source],
            send_sem=p_send.at[peer], recv_sem=p_recv.at[source],
            device_id={"ctx": peer * 2 + core}, device_id_type=pl.DeviceIdType.MESH)

    def prompt_block(t, block):
        where = chip_at(t)
        if block == 0:
            kv_copy(t, 0).wait()
            kv_copy(t, 1).wait()
        else:
            kv_give(t, 0).wait_recv()
            kv_give(t, 1).wait_recv()
        key = kbuf[t, block]
        value = vbuf[t, block]
        old = part_send[where, pl.ds(ROWS, NODES)]
        stat = jnp.zeros((NODES, 128), F32)
        for half in range(2):
            heads = range(4 * half, 4 * half + 4)
            rows = jnp.concatenate([qbuf[where, :, pl.ds(h * 128, 128)] for h in heads], axis=0)
            peak, total, summed = softmax_block(rows, key, value)
            part = pl.ds(half * 4 * NODES, 4 * NODES)
            if block == 1:
                old_peak = jnp.concatenate([old[:, h:h + 1] for h in heads], axis=0)
                old_total = jnp.concatenate([old[:, 8 + h:9 + h] for h in heads], axis=0)
                joint = jnp.maximum(peak, old_peak)
                old_factor = jnp.exp2((old_peak - joint) * EXP_SCALE)
                factor = jnp.exp2((peak - joint) * EXP_SCALE)
                total = old_factor * old_total + factor * total
                summed = old_factor * part_send[where, part] + factor * summed
                peak = joint
            part_send[where, part] = summed
            for h in heads:
                cut = slice((h - 4 * half) * NODES, (h - 4 * half + 1) * NODES)
                stat = jnp.where(stat_lane == h, peak[cut], stat)
                stat = jnp.where(stat_lane == 8 + h, total[cut], stat)
        part_send[where, pl.ds(ROWS, NODES)] = stat

    prompt_block(0, 0)

    @pl.loop(1, chips)
    def _(t):
        query_copy(t, chip_at(t)).wait_recv()
        prompt_block(t, 0)
        prompt_block(t, 1)
        part_copy(t, chip).start()

    @pl.loop(1, br_count)
    def _(i):
        message_a(0, peer_r(i)).wait_recv()

    got_a = recv_a[...]
    gather = iota((128, 16 * br_count), 1)
    pairs = (gather >> 1).astype(F32) == pair_col
    new_key = dot(onehot(pairs & ((gather & 1) == 0)), got_a[:, 256:]).astype(BF)
    new_value = dot(onehot(pairs & ((gather & 1) == 1)), got_a[:, 256:]).astype(BF)

    def gathered(address, got):
        count = address.shape[0]
        place = iota((count, 16 * br_count), 1)
        match = (place >> 2).astype(F32) == address
        parts = jnp.concatenate([onehot(match & ((place & 3) == part)) for part in range(4)], axis=0)
        return dot(parts, got).astype(BF)

    taken = gathered(quad_col[:LIVE], got_a[:, :256])
    for n in range(4):
        for half in range(2):
            qrows[n, pl.ds(half * LIVE, LIVE)] = taken[n * LIVE:(n + 1) * LIVE, half * 128:(half + 1) * 128]
    key_pages.wait()
    value_pages.wait()

    def suffix_block(rows, anc, length, see):
        count = rows.shape[0]
        fold = jnp.zeros((count, 256), F32)
        for branch in range(BRANCHES):
            key = jnp.concatenate([kpage[lax.rem(page_ref[page, branch], 32)] for page in range(2)], axis=0)
            fold = jnp.where(anc == branch, dot_nt(rows, key), fold)
        fold = jnp.where(iota((count, 256), 1).astype(F32) < length, fold, MASKED)
        new = jnp.where(see > 0.5, dot_nt(rows, new_key), MASKED)
        peak = jnp.maximum(jnp.max(fold, axis=1, keepdims=True), jnp.max(new, axis=1, keepdims=True))
        weight = jnp.exp2((fold - peak) * EXP_SCALE)
        new = jnp.exp2((new - peak) * EXP_SCALE)
        total = jnp.sum(weight, axis=1, keepdims=True) + jnp.sum(new, axis=1, keepdims=True)
        weight = weight.astype(BF)
        summed = dot(new.astype(BF), new_value)
        for branch in range(0, BRANCHES, 2):
            value = jnp.concatenate([jnp.concatenate(
                [vpage[lax.rem(page_ref[page, b], 32)] for page in range(2)], axis=0)
                for b in (branch, branch + 1)], axis=1)
            both = dot(weight, value)
            summed = jnp.where(anc == branch, summed + both[:, :128], summed)
            summed = jnp.where(anc == branch + 1, summed + both[:, 128:], summed)
        largest = jnp.max(jnp.abs(summed), axis=1, keepdims=True)
        coded = jnp.round(summed * jnp.where(largest > 0.0, 32767.0 / largest, 0.0))
        upper = jnp.floor(coded / 256.0)
        sum_log = peak * EXP_SCALE + jnp.log2(total)
        return upper.astype(BF), (coded - 256.0 * upper).astype(BF), sum_log, largest / (32767.0 * total)

    def repeated(column, times):
        return jnp.concatenate([column] * times, axis=0)

    def stat_rows(stat, cut):
        lane = iota(stat.shape, 1)
        stat = jnp.where((lane >> 4).astype(F32) == slot_col[cut], stat, 0.0)
        home_at = iota((br_count, stat.shape[0]), 0).astype(F32)
        own_home = jnp.where(here_row[:, cut] & (home_at == row_info[1:2, cut]), 1.0, 0.0)
        return jnp.dot(own_home, stat, precision=lax.Precision.HIGHEST, preferred_element_type=F32)

    def return_rows(address, high, low):
        count = address.shape[1]
        rows = iota((16 * br_count, count), 0)
        spread = spread_over(rows, 4, (rows >> 2).astype(F32) == address)
        return (256.0 * dot(spread, high) + dot(spread, low)).astype(jnp.int32).astype(jnp.int16)

    def returned(group, i, source):
        return to_br(i, source, ret_send.at[group], ret_recv.at[group], r_send.at[group], r_recv.at[group])

    def returned_stat(group, i, source):
        peer = peer_r(i)
        return pltpu.make_async_remote_copy(
            src_ref=stat_send.at[group, peer], dst_ref=stat_recv.at[group, source],
            send_sem=s_send.at[group, peer], recv_sem=s_recv.at[group, source],
            device_id={"br": peer}, device_id_type=pl.DeviceIdType.MESH)

    def give_back(group, stat, rows):
        for home_index in range(br_count):
            stat_send[group, home_index] = stat[home_index:home_index + 1]
        ret_send[group] = rows

        @pl.loop(1, br_count)
        def _(i):
            returned_stat(group, i, me_r).start()
            returned(group, i, me_r).start()

        stat_recv[group, me_r] = stat_send[group, me_r]
        ret_recv[group, own16, :] = ret_send[group, own16, :]

    first_lane = iota((LIVE, 128), 1) & 15

    def suffix_quarter(n, stat):
        high, low, sum_log, unit = suffix_block(
            qrows[n], repeated(anc_col[:LIVE], 2), repeated(length_col[:LIVE], 2), repeated(path[:LIVE], 2))
        quarter = pl.ds(pl.multiple_of(n * LIVE, LIVE), LIVE)
        for half in range(2):
            cut = slice(half * LIVE, (half + 1) * LIVE)
            code_high[quarter, pl.ds(half * 128, 128)] = high[cut]
            code_low[quarter, pl.ds(half * 128, 128)] = low[cut]
            stat = jnp.where(first_lane == 2 * n + half, sum_log[cut], stat)
            stat = jnp.where(first_lane == 8 + 2 * n + half, unit[cut], stat)
        return stat

    stat_a = lax.fori_loop(0, 4, suffix_quarter, jnp.zeros((LIVE, 128), F32))

    give_back(0, stat_rows(stat_a, slice(0, LIVE)),
              return_rows(quad_row[:, :LIVE], code_high[...], code_low[...]))

    prompt_block(0, 1)

    @pl.loop(1, br_count)
    def _(i):
        message_b(0, peer_r(i)).wait_recv()

    late = slice(LIVE, LIVE + LATE)
    taken = gathered(quad_col[late] - QUAD, recv_b[...])
    rows = jnp.concatenate([
        taken[(h // 2) * LATE:(h // 2 + 1) * LATE, (h % 2) * 128:(h % 2 + 1) * 128] for h in range(8)], axis=0)
    high, low, sum_log, unit = suffix_block(
        rows, repeated(anc_col[late], 8), repeated(length_col[late], 8), repeated(path[late], 8))
    late_lane = iota((LATE, 128), 1) & 15
    stat_b = jnp.zeros((LATE, 128), F32)
    for h in range(8):
        cut = slice(h * LATE, (h + 1) * LATE)
        late_high[pl.ds((h // 2) * LATE, LATE), pl.ds((h % 2) * 128, 128)] = high[cut]
        late_low[pl.ds((h // 2) * LATE, LATE), pl.ds((h % 2) * 128, 128)] = low[cut]
        stat_b = jnp.where(late_lane == h, sum_log[cut], stat_b)
        stat_b = jnp.where(late_lane == 8 + h, unit[cut], stat_b)
    give_back(1, stat_rows(stat_b, late),
              return_rows(quad_row[:, late] - QUAD, late_high[...], late_low[...]))

    part_recv[chip] = part_send[chip]

    @pl.loop(1, chips)
    def _(t):
        part_copy(t, chip_at(t)).wait_recv()

    stats = [part_recv[c, pl.ds(ROWS, NODES)] for c in range(4)]
    top = functools.reduce(jnp.maximum, stats)
    factors = [jnp.exp2((stat - top) * EXP_SCALE) for stat in stats]
    den = jnp.zeros((NODES, 128), F32)
    for c in range(4):
        den = den + factors[c] * pltpu.roll(stats[c], 120, 1)
    for h in range(8):
        summed = jnp.zeros((NODES, 128), F32)
        for c in range(4):
            summed = summed + factors[c][:, h:h + 1] * part_recv[c, pl.ds(h * NODES, NODES)]
        num[h] = summed

    back_low = iota((4 * NODES, 16 * br_count), 1)
    address = repeated(own_dev * QUAD + own_slot, 4)
    quarter_at = iota((4 * NODES, 16 * br_count), 0) // NODES

    def collected(group, match):
        collect = onehot(match & ((back_low & 3) == quarter_at))
        arrived = ret_recv[group].astype(jnp.int32)
        upper = dot(collect, (arrived >> 8).astype(F32).astype(BF))
        return 256.0 * upper + dot(collect, (arrived & 255).astype(F32).astype(BF))

    in_first = repeated(own_slot, 4) < QUAD
    quad_at = (back_low >> 2).astype(F32)

    @pl.loop(1, br_count)
    def _(i):
        returned_stat(0, 0, peer_r(i)).wait_recv()
        returned(0, 0, peer_r(i)).wait_recv()

    coded = collected(0, in_first & (quad_at == address))

    @pl.loop(1, br_count)
    def _(i):
        returned_stat(1, 0, peer_r(i)).wait_recv()
        returned(1, 0, peer_r(i)).wait_recv()

    coded = coded + collected(1, jnp.logical_not(in_first) & (quad_at == address - QUAD))
    from_device = jnp.where(iota((NODES, br_count), 1).astype(F32) == own_dev, 1.0, 0.0)
    all_stat = jnp.concatenate([stat_recv[0, d] + stat_recv[1, d] for d in range(br_count)], axis=0)
    back_stat = jnp.dot(from_device, all_stat, precision=lax.Precision.HIGHEST, preferred_element_type=F32)
    back_stat = jnp.where((stat_lane >> 4).astype(F32) == own_slot, back_stat, 0.0)
    for shift in (64, 32, 16):
        back_stat = back_stat + pltpu.roll(back_stat, shift, 1)
    prompt_log = top * EXP_SCALE
    overall = jnp.maximum(prompt_log, back_stat)
    prompt_factor = jnp.exp2(prompt_log - overall)
    suffix_factor = jnp.exp2(back_stat - overall)
    den = prompt_factor * den + suffix_factor
    unit = suffix_factor * pltpu.roll(back_stat, 120, 1)
    for h in range(8):
        back_home = coded[(h // 2) * NODES:(h // 2 + 1) * NODES, (h % 2) * 128:(h % 2 + 1) * 128]
        joined = prompt_factor[:, h:h + 1] * num[h] + unit[:, h:h + 1] * back_home
        out_ref[:, pl.ds(h * 128, 128)] = (joined / den[:, h:h + 1]).astype(BF)

    @pl.loop(1, chips)
    def _(t):
        query_copy(t, chip).wait_send()
        part_copy(t, chip).wait_send()

    @pl.loop(0, chips)
    def _(t):
        kv_give(t, 0).wait_send()
        kv_give(t, 1).wait_send()

    @pl.loop(1, br_count)
    def _(i):
        message_a(i, me_r).wait_send()
        message_b(i, me_r).wait_send()
        for group in range(2):
            returned_stat(group, i, me_r).wait_send()
            returned(group, i, me_r).wait_send()


def local(
    prompt_key_value, suffix_page_store, page_table, lengths, parents, queries, fresh_key_value
):
    br_count = lax.axis_size("br")
    ctx_count = lax.axis_size("ctx")
    vmem = pl.BlockSpec(memory_space=pltpu.VMEM)
    smem = pl.BlockSpec(memory_space=pltpu.SMEM)
    anywhere = pl.BlockSpec(memory_space=pl.ANY)
    dma = pltpu.SemaphoreType.DMA
    out, flag = pl.pallas_call(
        functools.partial(kernel, br_count, ctx_count),
        out_shape=(
            jax.ShapeDtypeStruct((NODES, 1024), BF),
            jax.ShapeDtypeStruct((1, 1), jnp.int32),
        ),
        in_specs=[smem, smem, vmem, vmem, vmem, anywhere, anywhere],
        out_specs=(vmem, smem),
        scratch_shapes=[
            pltpu.VMEM((4, 2, 2048, 128), BF),
            pltpu.VMEM((4, 2, 2048, 128), BF),
            pltpu.VMEM((32, 128, 128), BF),
            pltpu.VMEM((32, 128, 128), BF),
            pltpu.VMEM((4, NODES, 1024), BF),
            pltpu.VMEM((16 * br_count, 384), BF),
            pltpu.VMEM((16 * br_count, 384), BF),
            pltpu.VMEM((16 * br_count, 256), BF),
            pltpu.VMEM((16 * br_count, 256), BF),
            pltpu.VMEM((4, 2 * LIVE, 128), BF),
            pltpu.VMEM((4, ROWS + NODES, 128), F32),
            pltpu.VMEM((4, ROWS + NODES, 128), F32),
            pltpu.VMEM((4 * LIVE, 256), BF),
            pltpu.VMEM((4 * LIVE, 256), BF),
            pltpu.VMEM((4 * LATE, 256), BF),
            pltpu.VMEM((4 * LATE, 256), BF),
            pltpu.VMEM((2, br_count, 1, 128), F32),
            pltpu.VMEM((2, br_count, 1, 128), F32),
            pltpu.VMEM((2, 16 * br_count, 256), jnp.int16),
            pltpu.VMEM((2, 16 * br_count, 256), jnp.int16),
            pltpu.VMEM((8, NODES, 128), F32),
            dma((2, 4)), dma((2, 4)), dma((2, 4)), dma((2,)), dma((4,)), dma((4,)), dma((32,)), dma((32,)), dma((32,)), dma((32,)),
            dma((4,)), dma((4,)), dma((2, 32)), dma((2, 32)), dma((2, 32)), dma((2, 32)),
        ],
        compiler_params=pltpu.CompilerParams(
            collective_id=0, has_side_effects=True, vmem_limit_bytes=56 * 1024 * 1024
        ),
    )(
        page_table.T, lengths, parents, queries.reshape(NODES, 1024), fresh_key_value,
        prompt_key_value, suffix_page_store,
    )
    operands = (
        prompt_key_value, suffix_page_store, page_table, lengths, parents, queries, fresh_key_value
    )
    return lax.cond(
        flag[0, 0] > 0,
        lambda *whole: general(*whole),
        lambda *whole: out.reshape(STEPS, BRANCHES, 1024),
        *operands,
    )


def solution(mesh):
    in_specs = (
        P(None, "ctx", None),
        P("br", None, None, "ctx"),
        P("br", None),
        P(),
        P(),
        P(None, "br", "ctx"),
        P(None, None, "br", "ctx"),
    )
    out_specs = P(None, "br", "ctx")
    return jax.shard_map(local, mesh=mesh, in_specs=in_specs, out_specs=out_specs, check_vma=False)
```

```python
import functools
import math

import jax
import jax.numpy as jnp
from jax import lax
from jax.experimental import pallas as pl
from jax.experimental.pallas import tpu as pltpu
from jax.sharding import PartitionSpec as P

QUERY_HEADS = 64
KEY_VALUE_HEADS = 8
HEAD_SIZE = 128


NEG_FILL = -1e30


def joined_2(part, axis, combine):
    gathered = jax.tree.map(lambda a: lax.all_gather(a, axis), part)

    def take(source):
        return jax.tree.map(lambda a: lax.dynamic_index_in_dim(a, source, 0, False), gathered)

    return lax.fori_loop(
        1, lax.axis_size(axis), lambda source, state: combine(state, take(source)), take(0)
    )


def block_stats(scores, values, einsum_form):
    peak_value = jnp.max(scores, axis=-1)
    weights = jnp.exp(scores - peak_value[..., None])
    weight_total = jnp.sum(weights, axis=-1)
    rounded = weights.astype(jnp.bfloat16)
    summed = jnp.einsum(einsum_form, rounded, values, preferred_element_type=jnp.float32)
    return (peak_value, weight_total, summed)


def fold_pair(left_stats, right_stats):
    peak_value = jnp.maximum(left_stats[0], right_stats[0])
    left_weight = jnp.exp(left_stats[0] - peak_value)
    right_weight = jnp.exp(right_stats[0] - peak_value)
    weight_total = left_stats[1] * left_weight + right_stats[1] * right_weight
    summed = left_stats[2] * left_weight[..., None] + right_stats[2] * right_weight[..., None]
    return (peak_value, weight_total, summed)


def suffix_stats(query_head_rows, suffix_tokens, live_length, score_scale):
    row_count = suffix_tokens.shape[0]
    suffix_length = suffix_tokens.shape[2]
    kv_local = query_head_rows.shape[1]
    branch_suffix_keys = suffix_tokens[:, 0].reshape(row_count, suffix_length, kv_local, HEAD_SIZE)
    branch_suffix_values = suffix_tokens[:, 1].reshape(
        row_count, suffix_length, kv_local, HEAD_SIZE
    )
    scores = (
        jnp.einsum(
            "bgrd,btgd->bgrt",
            query_head_rows,
            branch_suffix_keys,
            preferred_element_type=jnp.float32,
        )
        * score_scale
    )
    live_mask = jnp.arange(suffix_length, dtype=jnp.int32)[None, :] < live_length[:, None]
    scores = jnp.where(live_mask[:, None, None, :], scores, NEG_FILL)
    return block_stats(scores, branch_suffix_values, "bgrt,btgd->bgrd")


def routing(parent, branch_per_shard, br_index, slot_rank, slot_match):
    grid_owner = (parent // branch_per_shard).reshape(-1, branch_per_shard)
    grid_local = (parent % branch_per_shard).reshape(-1, branch_per_shard)
    matched = (grid_owner == br_index)[:, :, None] & slot_match[None, :, :]
    outgoing = jnp.sum(jnp.where(matched, grid_local[:, :, None], 0), axis=1)
    own_owner = (
        lax.dynamic_slice_in_dim(parent, br_index * branch_per_shard, branch_per_shard)
        // branch_per_shard
    )
    incoming = own_owner * slot_match.shape[1] + slot_rank
    return (outgoing, incoming, own_owner)


def move_suffix(suffix_tokens, outgoing, incoming):
    dest_count = outgoing.shape[0]
    slot_count = outgoing.shape[1]
    tail_shape = suffix_tokens.shape[1:]
    outbound = suffix_tokens[outgoing.reshape(-1)].reshape((dest_count, slot_count) + tail_shape)
    arrived = lax.all_to_all(outbound, "br", split_axis=0, concat_axis=0, tiled=True)
    return arrived.reshape((dest_count * slot_count,) + tail_shape)[incoming]


def append_token(suffix_tokens, position_at, fresh_token):
    suffix_length = suffix_tokens.shape[2]
    target_mask = jnp.arange(suffix_length, dtype=jnp.int32)[None, :] == position_at[:, None]
    return jnp.where(
        target_mask[:, None, :, None], jnp.swapaxes(fresh_token, 0, 1)[:, :, None, :], suffix_tokens
    )


def general(
    prompt_key_value, suffix_page_store, page_table, lengths, parents, queries, fresh_key_value
):
    br_count = lax.axis_size("br")
    br_index = lax.axis_index("br")
    ctx_index = lax.axis_index("ctx")
    branch_per_shard = page_table.shape[0]
    page_count = page_table.shape[1]
    pool_dev = suffix_page_store.shape[0]
    page_rows = suffix_page_store.shape[2]
    head_width = suffix_page_store.shape[3]
    step_count = queries.shape[0]
    kv_local = head_width // HEAD_SIZE
    group_width = QUERY_HEADS // KEY_VALUE_HEADS
    slot_count = max(1, branch_per_shard // br_count)
    score_scale = 1.0 / math.sqrt(HEAD_SIZE)
    slot_rank = jnp.arange(branch_per_shard, dtype=jnp.int32) % slot_count
    slot_match = slot_rank[:, None] == jnp.arange(slot_count, dtype=jnp.int32)[None, :]
    gathered_pages = suffix_page_store[page_table - br_index * pool_dev]
    suffix_tokens = jnp.swapaxes(gathered_pages, 1, 2).reshape(
        branch_per_shard, 2, page_count * page_rows, head_width
    )
    length = lengths
    head_listing = lax.all_gather(queries, "ctx", axis=2, tiled=True)
    shared_prompt_keys = prompt_key_value[0].reshape(-1, KEY_VALUE_HEADS, HEAD_SIZE)
    shared_prompt_values = prompt_key_value[1].reshape(-1, KEY_VALUE_HEADS, HEAD_SIZE)
    outputs = []
    for decode_step_index in range(step_count):
        parent = parents[decode_step_index]
        outgoing, incoming, own_owner = routing(
            parent, branch_per_shard, br_index, slot_rank, slot_match
        )
        parent_length = length[parent]
        own_parent_length = lax.dynamic_slice_in_dim(
            parent_length, br_index * branch_per_shard, branch_per_shard
        )
        fresh_token = fresh_key_value[decode_step_index]
        query_mine = queries[decode_step_index].reshape(
            branch_per_shard, kv_local, group_width, HEAD_SIZE
        )
        suffix_tokens = append_token(
            move_suffix(suffix_tokens, outgoing, incoming), own_parent_length, fresh_token
        )
        suffix_part = suffix_stats(query_mine, suffix_tokens, own_parent_length + 1, score_scale)
        length = parent_length + 1
        query_complete = head_listing[decode_step_index].reshape(
            branch_per_shard, KEY_VALUE_HEADS, group_width, HEAD_SIZE
        )
        prompt_scores = (
            jnp.einsum(
                "bgrd,tgd->bgrt",
                query_complete,
                shared_prompt_keys,
                preferred_element_type=jnp.float32,
            )
            * score_scale
        )
        prompt_part = block_stats(prompt_scores, shared_prompt_values, "bgrt,tgd->bgrd")
        head_start = ctx_index * kv_local
        own_heads = tuple(
            (lax.dynamic_slice_in_dim(member, head_start, kv_local, 1) for member in prompt_part)
        )
        joined = fold_pair(own_heads, suffix_part)
        placed = tuple(
            (
                lax.dynamic_update_slice_in_dim(whole_part, own_part, head_start, 1)
                for whole_part, own_part in zip(prompt_part, joined)
            )
        )
        merged = joined_2((placed[0], placed[1], placed[2]), "ctx", fold_pair)
        combined = tuple(
            (lax.dynamic_slice_in_dim(member, head_start, kv_local, 1) for member in merged)
        )
        attention = (combined[2] / combined[1][..., None]).reshape(
            branch_per_shard, kv_local * group_width * HEAD_SIZE
        )
        outputs.append(attention.astype(jnp.bfloat16))
    return jnp.stack(outputs)


STEPS = 3
BRANCHES = 16
NODES = STEPS * BRANCHES
CAP = 8
QUAD = 4
LIVE = 96
LATE = 16
ROWS = 8 * NODES
MASKED = -1e30
EXP_SCALE = math.log2(math.e) / math.sqrt(HEAD_SIZE)
BF = jnp.bfloat16
F32 = jnp.float32
NT = (((1,), (1,)), ((), ()))


def onehot(condition):
    return jnp.where(condition, 1.0, 0.0).astype(BF)


def iota(shape, axis):
    return lax.broadcasted_iota(jnp.int32, shape, axis)


def stacked(rows, count, width):
    at = iota((count, width), 0)
    out = jnp.zeros((count, width), F32)
    for index, row in enumerate(rows):
        out = jnp.where(at == index, row.astype(F32), out)
    return out.astype(BF)


def dot(left, right):
    return jnp.dot(left, right, preferred_element_type=F32)


def dot_nt(left, right):
    return lax.dot_general(left, right, NT, preferred_element_type=F32)


def softmax_block(query, key, value):
    raw = dot_nt(query, key)
    peak = jnp.max(raw, axis=1, keepdims=True)
    weight = jnp.exp2((raw - peak) * EXP_SCALE)
    total = jnp.sum(weight, axis=1, keepdims=True)
    return peak, total, dot(weight.astype(BF), value)


def kernel(
    br_count, ctx_count,
    page_ref, len_ref, par_ref, q_ref, fresh_ref, pkv_ref, pages_ref,
    out_ref, flag_ref,
    kbuf, vbuf, kpage, vpage, qbuf, send_a, recv_a, send_b, recv_b, qrows, part_send, part_recv,
    code_high, code_low, late_high, late_low, stat_send, stat_recv, ret_send, ret_recv, num,
    kv_sem, g_send, g_recv, page_sem, q_send, q_recv, a_send, a_recv, b_send, b_recv, p_send, p_recv,
    r_send, r_recv, s_send, s_recv,
):
    me_c = lax.axis_index("ctx")
    me_r = lax.axis_index("br")

    core = lax.rem(me_c, 2)
    chip = me_c // 2
    chips = ctx_count // 2
    partner = me_c + 1 - 2 * core

    def peer_r(i):
        return lax.rem(me_r + i, br_count)

    def chip_at(t):
        return lax.rem(chip + t, chips)

    barrier = pltpu.get_barrier_semaphore()

    @pl.loop(1, chips)
    def _(t):
        pl.semaphore_signal(
            barrier, inc=1, device_id={"ctx": chip_at(t) * 2 + core}, device_id_type=pl.DeviceIdType.MESH)

    pl.semaphore_signal(barrier, inc=1, device_id={"ctx": partner}, device_id_type=pl.DeviceIdType.MESH)

    @pl.loop(1, br_count)
    def _(i):
        pl.semaphore_signal(barrier, inc=1, device_id={"br": peer_r(i)}, device_id_type=pl.DeviceIdType.MESH)

    def head_columns(t, parity):
        return pl.ds(pl.multiple_of((chip_at(t) * 2 + parity) * HEAD_SIZE, HEAD_SIZE), HEAD_SIZE)

    def kv_copy(t, which):
        buffer = kbuf if which == 0 else vbuf
        return pltpu.make_async_copy(
            pkv_ref.at[which, :, head_columns(t, core)], buffer.at[t, 0], kv_sem.at[which, t])

    def kv_give(t, which):
        buffer = kbuf if which == 0 else vbuf
        return pltpu.make_async_remote_copy(
            src_ref=pkv_ref.at[which, :, head_columns(t, 1 - core)], dst_ref=buffer.at[t, 1],
            send_sem=g_send.at[which, t], recv_sem=g_recv.at[which, t],
            device_id={"ctx": partner}, device_id_type=pl.DeviceIdType.MESH)

    key_pages = pltpu.make_async_copy(pages_ref.at[:, 0], kpage, page_sem.at[0])
    value_pages = pltpu.make_async_copy(pages_ref.at[:, 1], vpage, page_sem.at[1])

    @pl.loop(0, chips)
    def _(t):
        kv_copy(t, 0).start()
        kv_copy(t, 1).start()

    key_pages.start()
    value_pages.start()

    parent = par_ref[...]
    device = lax.shift_right_logical(parent, 4)
    place = parent & 15
    width = parent.shape[1]
    row_at = iota((width, width), 0)
    pick1 = onehot(row_at == parent[1:2])
    pick2 = onehot(row_at == parent[2:3])
    first = dot(stacked([device[0:1], place[0:1]], 16, width), pick1)
    second = dot(stacked([first[0:1], first[1:2], device[1:2], place[1:2]], 16, width), pick2)
    anc_dev = [device[0:1].astype(F32), first[0:1], second[0:1]]
    anc_loc = [place[0:1].astype(F32), first[1:2], second[1:2]]
    missing = jnp.full((1, width), -1.0, F32)
    par_hi = [missing, device[1:2].astype(F32), device[2:3].astype(F32) + 32.0]
    par_lo = [missing, place[1:2].astype(F32), place[2:3].astype(F32)]
    old_hi = [missing, missing, second[2:3]]
    old_lo = [missing, missing, second[3:4]]

    owner = iota((br_count, width), 0).astype(F32)
    to_owner = [onehot(owner == anc_dev[s]) for s in range(STEPS)]
    j = iota((128, 256), 0)
    lane = iota((128, 256), 1)
    b = lane & 127
    same_home = (j >> 4) == (b >> 4)
    counting = onehot(same_home & ((lane >= 128) | (j < b)))
    slots = [[], [], []]
    pair_count = []
    for tile in range(width // 128):
        cut = [m[:, tile * 128:(tile + 1) * 128] for m in to_owner]
        counted = dot(jnp.concatenate(cut, axis=0), counting)
        before = jnp.zeros((br_count, 128), F32)
        for s in range(STEPS):
            block = counted[s * br_count:(s + 1) * br_count]
            slots[s].append(jnp.sum(cut[s].astype(F32) * (block[:, :128] + before), axis=0, keepdims=True))
            before = before + block[:, 128:]
        pair_count.append(before)
    slot = [jnp.concatenate(parts, axis=1) for parts in slots]
    count = jnp.concatenate(pair_count, axis=1)
    most = jnp.max(count)
    first_count = jnp.minimum(count, QUAD)
    fullest = jnp.max(jnp.sum(first_count, axis=1, keepdims=True)) / BRANCHES
    latest = jnp.max(jnp.sum(count - first_count, axis=1, keepdims=True)) / BRANCHES
    over = (most > CAP) | (fullest > LIVE) | (latest > LATE)
    flag_ref[0, 0] = jnp.where(over, 1, 0)

    node = iota((128, STEPS * width), 0)
    column = iota((128, STEPS * width), 1)
    mine = onehot(((column & (width - 1)) == me_r * BRANCHES + (node & 15)) & ((node >> 4) == column // width))
    whither = jnp.concatenate([stacked([anc_dev[s], slot[s]], 16, width) for s in range(STEPS)], axis=1)
    own_row = dot_nt(whither, mine)
    own_col = dot_nt(mine, whither)
    own_dev, own_slot = own_col[:NODES, 0:1], own_col[:NODES, 1:2]
    at = iota((16 * br_count, 128), 0)
    is_node = iota((16 * br_count, 128), 1) < NODES
    own_pair = is_node & ((at >> 1).astype(F32) == own_row[0:1] * CAP + own_row[1:2])
    quad_row = own_row[0:1] * QUAD + own_row[1:2]
    own_first = is_node & (own_row[1:2] < QUAD) & ((at >> 2).astype(F32) == quad_row)
    own_late = is_node & (own_row[1:2] >= QUAD) & ((at >> 2).astype(F32) == quad_row - QUAD)
    queries = q_ref[...]

    def padded(rows):
        return jnp.concatenate([rows, jnp.zeros((128 - NODES, rows.shape[1]), BF)], axis=0)

    fresh = [padded(jnp.concatenate([fresh_ref[s, kind] for s in range(STEPS)], axis=0)) for kind in range(2)]
    quarters = jnp.concatenate([padded(queries[:, 256 * n:256 * (n + 1)]) for n in range(4)], axis=0)

    def spread_over(rows, parts, mask):
        return jnp.concatenate([onehot(mask & ((rows & (parts - 1)) == part)) for part in range(parts)], axis=1)

    send_a[:, pl.ds(0, 256)] = dot(spread_over(at, 4, own_first), quarters).astype(BF)
    send_a[:, pl.ds(256, 128)] = dot(spread_over(at, 2, own_pair), jnp.concatenate(fresh, axis=0)).astype(BF)
    send_b[...] = dot(spread_over(at, 4, own_late), quarters).astype(BF)

    def rows16(index):
        return pl.ds(pl.multiple_of(index * 16, 16), 16)

    def to_br(i, source, send, recv, send_sem, recv_sem):
        peer = peer_r(i)
        return pltpu.make_async_remote_copy(
            src_ref=send.at[rows16(peer)], dst_ref=recv.at[rows16(source)],
            send_sem=send_sem.at[peer], recv_sem=recv_sem.at[source],
            device_id={"br": peer}, device_id_type=pl.DeviceIdType.MESH)

    def message_a(i, source):
        return to_br(i, source, send_a, recv_a, a_send, a_recv)

    def message_b(i, source):
        return to_br(i, source, send_b, recv_b, b_send, b_recv)

    def query_copy(t, source):
        return pltpu.make_async_remote_copy(
            src_ref=q_ref, dst_ref=qbuf.at[source],
            send_sem=q_send.at[t], recv_sem=q_recv.at[source],
            device_id={"ctx": chip_at(t) * 2 + core}, device_id_type=pl.DeviceIdType.MESH)

    pl.semaphore_wait(barrier, chips + br_count - 1)

    @pl.loop(1, chips)
    def _(t):
        query_copy(t, chip).start()
        kv_give(t, 0).start()
        kv_give(t, 1).start()

    kv_give(0, 0).start()
    kv_give(0, 1).start()

    @pl.loop(1, br_count)
    def _(i):
        message_a(i, me_r).start()

    @pl.loop(1, br_count)
    def _(i):
        message_b(i, me_r).start()

    own16 = rows16(me_r)
    recv_a[own16, :] = send_a[own16, :]
    recv_b[own16, :] = send_b[own16, :]
    qbuf[chip] = queries

    here = (iota((br_count, width), 0) == me_r).astype(F32)
    home_count = jnp.sum(here * count, axis=0, keepdims=True)
    col_at = iota((width, width), 1)
    earlier = onehot(((row_at & 15) == 0) & ((row_at >> 4) < (col_at >> 4)))
    home_first = jnp.minimum(home_count, QUAD)
    ahead = dot(stacked([home_first, home_count - home_first], 16, width), earlier)
    home = lax.shift_right_logical(iota((1, width), 1), 4).astype(F32)
    local_at = (iota((1, width), 1) & 15).astype(F32)
    ones = jnp.ones((1, width), F32)
    live_rows = iota((128, width), 0).astype(F32)
    chosen, known = [], []
    for s in range(STEPS):
        arrives = anc_dev[s] == me_r.astype(F32)
        first_at = ahead[0:1] + slot[s]
        late_at = ahead[1:2] + slot[s] - QUAD
        late_at = jnp.where((slot[s] < CAP) & (late_at < LATE), late_at + LIVE, -1.0)
        place_at = jnp.where(slot[s] < QUAD, jnp.where(first_at < LIVE, first_at, -1.0), late_at)
        place_at = jnp.where(arrives, place_at, -1.0)
        chosen.append(onehot(live_rows == place_at))
        known.append(stacked([
            ones, home, slot[s], anc_loc[s], home + 32.0 * s, local_at,
            par_hi[s], par_lo[s], old_hi[s], old_lo[s]], 16, width))
    chosen = jnp.concatenate(chosen, axis=1)
    known = jnp.concatenate(known, axis=1)
    row_info = dot_nt(known, chosen)
    col_info = dot_nt(chosen, known)
    here_row = row_info[0:1] > 0.5
    here_col = col_info[:, 0:1] > 0.5
    slot_row, slot_col = row_info[2:3], col_info[:, 2:3]
    pair_col = jnp.where(here_col, col_info[:, 1:2] * CAP + slot_col, -1.0)
    quad_col = jnp.where(here_col, col_info[:, 1:2] * QUAD + slot_col, -1.0)
    quad_row = jnp.where(here_row, row_info[1:2] * QUAD + slot_row, -1.0)
    self_row = jnp.where(here_row, row_info[4:5] * 16.0 + row_info[5:6], -100.0)
    on_path = self_row == col_info[:, 4:5] * 16.0 + col_info[:, 5:6]
    on_path = on_path | (self_row == col_info[:, 6:7] * 16.0 + col_info[:, 7:8])
    on_path = on_path | (self_row == col_info[:, 8:9] * 16.0 + col_info[:, 9:10])
    path = jnp.where(on_path, 1.0, 0.0)
    anc_col = col_info[:, 3:4]
    length_col = jnp.zeros((128, 1), F32)
    for branch in range(BRANCHES):
        length_col = jnp.where(anc_col == branch, len_ref[me_r * BRANCHES + branch].astype(F32), length_col)

    stat_lane = iota((NODES, 128), 1)

    def part_copy(t, source):
        peer = chip_at(t)
        return pltpu.make_async_remote_copy(
            src_ref=part_send.at[peer], dst_ref=part_recv.at[source],
            send_sem=p_send.at[peer], recv_sem=p_recv.at[source],
            device_id={"ctx": peer * 2 + core}, device_id_type=pl.DeviceIdType.MESH)

    def prompt_block(t, block):
        where = chip_at(t)
        if block == 0:
            kv_copy(t, 0).wait()
            kv_copy(t, 1).wait()
        else:
            kv_give(t, 0).wait_recv()
            kv_give(t, 1).wait_recv()
        key = kbuf[t, block]
        value = vbuf[t, block]
        old = part_send[where, pl.ds(ROWS, NODES)]
        stat = jnp.zeros((NODES, 128), F32)
        for half in range(2):
            heads = range(4 * half, 4 * half + 4)
            rows = jnp.concatenate([qbuf[where, :, pl.ds(h * 128, 128)] for h in heads], axis=0)
            peak, total, summed = softmax_block(rows, key, value)
            part = pl.ds(half * 4 * NODES, 4 * NODES)
            if block == 1:
                old_peak = jnp.concatenate([old[:, h:h + 1] for h in heads], axis=0)
                old_total = jnp.concatenate([old[:, 8 + h:9 + h] for h in heads], axis=0)
                joint = jnp.maximum(peak, old_peak)
                old_factor = jnp.exp2((old_peak - joint) * EXP_SCALE)
                factor = jnp.exp2((peak - joint) * EXP_SCALE)
                total = old_factor * old_total + factor * total
                summed = old_factor * part_send[where, part] + factor * summed
                peak = joint
            part_send[where, part] = summed
            for h in heads:
                cut = slice((h - 4 * half) * NODES, (h - 4 * half + 1) * NODES)
                stat = jnp.where(stat_lane == h, peak[cut], stat)
                stat = jnp.where(stat_lane == 8 + h, total[cut], stat)
        part_send[where, pl.ds(ROWS, NODES)] = stat

    def prompt_head(t):
        query_copy(t, chip_at(t)).wait_recv()
        prompt_block(t, 0)
        prompt_block(t, 1)
        part_copy(t, chip).start()

    prompt_block(0, 0)

    @pl.loop(1, chips - 1)
    def _(t):
        prompt_head(t)

    @pl.loop(1, br_count)
    def _(i):
        message_a(0, peer_r(i)).wait_recv()

    got_a = recv_a[...]
    gather = iota((128, 16 * br_count), 1)
    pairs = (gather >> 1).astype(F32) == pair_col
    new_key = dot(onehot(pairs & ((gather & 1) == 0)), got_a[:, 256:]).astype(BF)
    new_value = dot(onehot(pairs & ((gather & 1) == 1)), got_a[:, 256:]).astype(BF)

    def gathered(address, got):
        count = address.shape[0]
        place = iota((count, 16 * br_count), 1)
        match = (place >> 2).astype(F32) == address
        parts = jnp.concatenate([onehot(match & ((place & 3) == part)) for part in range(4)], axis=0)
        return dot(parts, got).astype(BF)

    taken = gathered(quad_col[:LIVE], got_a[:, :256])
    for n in range(4):
        for half in range(2):
            qrows[n, pl.ds(half * LIVE, LIVE)] = taken[n * LIVE:(n + 1) * LIVE, half * 128:(half + 1) * 128]
    key_pages.wait()
    value_pages.wait()

    def suffix_block(rows, anc, length, see):
        count = rows.shape[0]
        fold = jnp.zeros((count, 256), F32)
        for branch in range(BRANCHES):
            key = jnp.concatenate([kpage[lax.rem(page_ref[page, branch], 32)] for page in range(2)], axis=0)
            fold = jnp.where(anc == branch, dot_nt(rows, key), fold)
        fold = jnp.where(iota((count, 256), 1).astype(F32) < length, fold, MASKED)
        new = jnp.where(see > 0.5, dot_nt(rows, new_key), MASKED)
        peak = jnp.maximum(jnp.max(fold, axis=1, keepdims=True), jnp.max(new, axis=1, keepdims=True))
        weight = jnp.exp2((fold - peak) * EXP_SCALE)
        new = jnp.exp2((new - peak) * EXP_SCALE)
        total = jnp.sum(weight, axis=1, keepdims=True) + jnp.sum(new, axis=1, keepdims=True)
        weight = weight.astype(BF)
        summed = dot(new.astype(BF), new_value)
        for branch in range(0, BRANCHES, 2):
            value = jnp.concatenate([jnp.concatenate(
                [vpage[lax.rem(page_ref[page, b], 32)] for page in range(2)], axis=0)
                for b in (branch, branch + 1)], axis=1)
            both = dot(weight, value)
            summed = jnp.where(anc == branch, summed + both[:, :128], summed)
            summed = jnp.where(anc == branch + 1, summed + both[:, 128:], summed)
        largest = jnp.max(jnp.abs(summed), axis=1, keepdims=True)
        coded = jnp.round(summed * jnp.where(largest > 0.0, 32767.0 / largest, 0.0))
        upper = jnp.floor(coded / 256.0)
        sum_log = peak * EXP_SCALE + jnp.log2(total)
        return upper.astype(BF), (coded - 256.0 * upper).astype(BF), sum_log, largest / (32767.0 * total)

    def repeated(column, times):
        return jnp.concatenate([column] * times, axis=0)

    def stat_rows(stat, cut):
        lane = iota(stat.shape, 1)
        stat = jnp.where((lane >> 4).astype(F32) == slot_col[cut], stat, 0.0)
        home_at = iota((br_count, stat.shape[0]), 0).astype(F32)
        own_home = jnp.where(here_row[:, cut] & (home_at == row_info[1:2, cut]), 1.0, 0.0)
        return jnp.dot(own_home, stat, precision=lax.Precision.HIGHEST, preferred_element_type=F32)

    def return_rows(address, high, low):
        count = address.shape[1]
        rows = iota((16 * br_count, count), 0)
        spread = spread_over(rows, 4, (rows >> 2).astype(F32) == address)
        return (256.0 * dot(spread, high) + dot(spread, low)).astype(jnp.int32).astype(jnp.int16)

    def returned(group, i, source):
        return to_br(i, source, ret_send.at[group], ret_recv.at[group], r_send.at[group], r_recv.at[group])

    def returned_stat(group, i, source):
        peer = peer_r(i)
        return pltpu.make_async_remote_copy(
            src_ref=stat_send.at[group, peer], dst_ref=stat_recv.at[group, source],
            send_sem=s_send.at[group, peer], recv_sem=s_recv.at[group, source],
            device_id={"br": peer}, device_id_type=pl.DeviceIdType.MESH)

    def give_back(group, stat, rows):
        for home_index in range(br_count):
            stat_send[group, home_index] = stat[home_index:home_index + 1]
        ret_send[group] = rows

        @pl.loop(1, br_count)
        def _(i):
            returned_stat(group, i, me_r).start()
            returned(group, i, me_r).start()

        stat_recv[group, me_r] = stat_send[group, me_r]
        ret_recv[group, own16, :] = ret_send[group, own16, :]

    first_lane = iota((LIVE, 128), 1) & 15

    def suffix_quarter(n, stat):
        high, low, sum_log, unit = suffix_block(
            qrows[n], repeated(anc_col[:LIVE], 2), repeated(length_col[:LIVE], 2), repeated(path[:LIVE], 2))
        quarter = pl.ds(pl.multiple_of(n * LIVE, LIVE), LIVE)
        for half in range(2):
            cut = slice(half * LIVE, (half + 1) * LIVE)
            code_high[quarter, pl.ds(half * 128, 128)] = high[cut]
            code_low[quarter, pl.ds(half * 128, 128)] = low[cut]
            stat = jnp.where(first_lane == 2 * n + half, sum_log[cut], stat)
            stat = jnp.where(first_lane == 8 + 2 * n + half, unit[cut], stat)
        return stat

    stat_a = lax.fori_loop(0, 4, suffix_quarter, jnp.zeros((LIVE, 128), F32))

    give_back(0, stat_rows(stat_a, slice(0, LIVE)),
              return_rows(quad_row[:, :LIVE], code_high[...], code_low[...]))

    @pl.loop(1, br_count)
    def _(i):
        message_b(0, peer_r(i)).wait_recv()

    late = slice(LIVE, LIVE + LATE)
    taken = gathered(quad_col[late] - QUAD, recv_b[...])
    rows = jnp.concatenate([
        taken[(h // 2) * LATE:(h // 2 + 1) * LATE, (h % 2) * 128:(h % 2 + 1) * 128] for h in range(8)], axis=0)
    high, low, sum_log, unit = suffix_block(
        rows, repeated(anc_col[late], 8), repeated(length_col[late], 8), repeated(path[late], 8))
    late_lane = iota((LATE, 128), 1) & 15
    stat_b = jnp.zeros((LATE, 128), F32)
    for h in range(8):
        cut = slice(h * LATE, (h + 1) * LATE)
        late_high[pl.ds((h // 2) * LATE, LATE), pl.ds((h % 2) * 128, 128)] = high[cut]
        late_low[pl.ds((h // 2) * LATE, LATE), pl.ds((h % 2) * 128, 128)] = low[cut]
        stat_b = jnp.where(late_lane == h, sum_log[cut], stat_b)
        stat_b = jnp.where(late_lane == 8 + h, unit[cut], stat_b)
    give_back(1, stat_rows(stat_b, late),
              return_rows(quad_row[:, late] - QUAD, late_high[...], late_low[...]))

    prompt_head(chips - 1)
    prompt_block(0, 1)

    part_recv[chip] = part_send[chip]

    @pl.loop(1, chips)
    def _(t):
        part_copy(t, chip_at(t)).wait_recv()

    stats = [part_recv[c, pl.ds(ROWS, NODES)] for c in range(4)]
    top = functools.reduce(jnp.maximum, stats)
    factors = [jnp.exp2((stat - top) * EXP_SCALE) for stat in stats]
    den = jnp.zeros((NODES, 128), F32)
    for c in range(4):
        den = den + factors[c] * pltpu.roll(stats[c], 120, 1)
    for h in range(8):
        summed = jnp.zeros((NODES, 128), F32)
        for c in range(4):
            summed = summed + factors[c][:, h:h + 1] * part_recv[c, pl.ds(h * NODES, NODES)]
        num[h] = summed

    back_low = iota((4 * NODES, 16 * br_count), 1)
    address = repeated(own_dev * QUAD + own_slot, 4)
    quarter_at = iota((4 * NODES, 16 * br_count), 0) // NODES

    def collected(group, match):
        collect = onehot(match & ((back_low & 3) == quarter_at))
        arrived = ret_recv[group].astype(jnp.int32)
        upper = dot(collect, (arrived >> 8).astype(F32).astype(BF))
        return 256.0 * upper + dot(collect, (arrived & 255).astype(F32).astype(BF))

    in_first = repeated(own_slot, 4) < QUAD
    quad_at = (back_low >> 2).astype(F32)

    @pl.loop(1, br_count)
    def _(i):
        returned_stat(0, 0, peer_r(i)).wait_recv()
        returned(0, 0, peer_r(i)).wait_recv()

    coded = collected(0, in_first & (quad_at == address))

    @pl.loop(1, br_count)
    def _(i):
        returned_stat(1, 0, peer_r(i)).wait_recv()
        returned(1, 0, peer_r(i)).wait_recv()

    coded = coded + collected(1, jnp.logical_not(in_first) & (quad_at == address - QUAD))
    from_device = jnp.where(iota((NODES, br_count), 1).astype(F32) == own_dev, 1.0, 0.0)
    all_stat = jnp.concatenate([stat_recv[0, d] + stat_recv[1, d] for d in range(br_count)], axis=0)
    back_stat = jnp.dot(from_device, all_stat, precision=lax.Precision.HIGHEST, preferred_element_type=F32)
    back_stat = jnp.where((stat_lane >> 4).astype(F32) == own_slot, back_stat, 0.0)
    for shift in (64, 32, 16):
        back_stat = back_stat + pltpu.roll(back_stat, shift, 1)
    prompt_log = top * EXP_SCALE
    overall = jnp.maximum(prompt_log, back_stat)
    prompt_factor = jnp.exp2(prompt_log - overall)
    suffix_factor = jnp.exp2(back_stat - overall)
    den = prompt_factor * den + suffix_factor
    unit = suffix_factor * pltpu.roll(back_stat, 120, 1)
    for h in range(8):
        back_home = coded[(h // 2) * NODES:(h // 2 + 1) * NODES, (h % 2) * 128:(h % 2 + 1) * 128]
        joined = prompt_factor[:, h:h + 1] * num[h] + unit[:, h:h + 1] * back_home
        out_ref[:, pl.ds(h * 128, 128)] = (joined / den[:, h:h + 1]).astype(BF)

    @pl.loop(1, chips)
    def _(t):
        query_copy(t, chip).wait_send()
        part_copy(t, chip).wait_send()

    @pl.loop(0, chips)
    def _(t):
        kv_give(t, 0).wait_send()
        kv_give(t, 1).wait_send()

    @pl.loop(1, br_count)
    def _(i):
        message_a(i, me_r).wait_send()
        message_b(i, me_r).wait_send()
        for group in range(2):
            returned_stat(group, i, me_r).wait_send()
            returned(group, i, me_r).wait_send()


def local(
    prompt_key_value, suffix_page_store, page_table, lengths, parents, queries, fresh_key_value
):
    br_count = lax.axis_size("br")
    ctx_count = lax.axis_size("ctx")
    vmem = pl.BlockSpec(memory_space=pltpu.VMEM)
    smem = pl.BlockSpec(memory_space=pltpu.SMEM)
    anywhere = pl.BlockSpec(memory_space=pl.ANY)
    dma = pltpu.SemaphoreType.DMA
    out, flag = pl.pallas_call(
        functools.partial(kernel, br_count, ctx_count),
        out_shape=(
            jax.ShapeDtypeStruct((NODES, 1024), BF),
            jax.ShapeDtypeStruct((1, 1), jnp.int32),
        ),
        in_specs=[smem, smem, vmem, vmem, vmem, anywhere, anywhere],
        out_specs=(vmem, smem),
        scratch_shapes=[
            pltpu.VMEM((4, 2, 2048, 128), BF),
            pltpu.VMEM((4, 2, 2048, 128), BF),
            pltpu.VMEM((32, 128, 128), BF),
            pltpu.VMEM((32, 128, 128), BF),
            pltpu.VMEM((4, NODES, 1024), BF),
            pltpu.VMEM((16 * br_count, 384), BF),
            pltpu.VMEM((16 * br_count, 384), BF),
            pltpu.VMEM((16 * br_count, 256), BF),
            pltpu.VMEM((16 * br_count, 256), BF),
            pltpu.VMEM((4, 2 * LIVE, 128), BF),
            pltpu.VMEM((4, ROWS + NODES, 128), F32),
            pltpu.VMEM((4, ROWS + NODES, 128), F32),
            pltpu.VMEM((4 * LIVE, 256), BF),
            pltpu.VMEM((4 * LIVE, 256), BF),
            pltpu.VMEM((4 * LATE, 256), BF),
            pltpu.VMEM((4 * LATE, 256), BF),
            pltpu.VMEM((2, br_count, 1, 128), F32),
            pltpu.VMEM((2, br_count, 1, 128), F32),
            pltpu.VMEM((2, 16 * br_count, 256), jnp.int16),
            pltpu.VMEM((2, 16 * br_count, 256), jnp.int16),
            pltpu.VMEM((8, NODES, 128), F32),
            dma((2, 4)), dma((2, 4)), dma((2, 4)), dma((2,)), dma((4,)), dma((4,)), dma((32,)), dma((32,)), dma((32,)), dma((32,)),
            dma((4,)), dma((4,)), dma((2, 32)), dma((2, 32)), dma((2, 32)), dma((2, 32)),
        ],
        compiler_params=pltpu.CompilerParams(
            collective_id=0, has_side_effects=True, vmem_limit_bytes=56 * 1024 * 1024
        ),
    )(
        page_table.T, lengths, parents, queries.reshape(NODES, 1024), fresh_key_value,
        prompt_key_value, suffix_page_store,
    )
    operands = (
        prompt_key_value, suffix_page_store, page_table, lengths, parents, queries, fresh_key_value
    )
    return lax.cond(
        flag[0, 0] > 0,
        lambda *whole: general(*whole),
        lambda *whole: out.reshape(STEPS, BRANCHES, 1024),
        *operands,
    )


def solution(mesh):
    in_specs = (
        P(None, "ctx", None),
        P("br", None, None, "ctx"),
        P("br", None),
        P(),
        P(),
        P(None, "br", "ctx"),
        P(None, None, "br", "ctx"),
    )
    out_specs = P(None, "br", "ctx")
    return jax.shard_map(local, mesh=mesh, in_specs=in_specs, out_specs=out_specs, check_vma=False)
```

```python
import functools
import math

import jax
import jax.numpy as jnp
from jax import lax
from jax.experimental import pallas as pl
from jax.experimental.pallas import tpu as pltpu
from jax.sharding import PartitionSpec as P

QUERY_HEADS = 64
KEY_VALUE_HEADS = 8
HEAD_SIZE = 128


NEG_FILL = -1e30


def joined_2(part, axis, combine):
    gathered = jax.tree.map(lambda a: lax.all_gather(a, axis), part)

    def take(source):
        return jax.tree.map(lambda a: lax.dynamic_index_in_dim(a, source, 0, False), gathered)

    return lax.fori_loop(
        1, lax.axis_size(axis), lambda source, state: combine(state, take(source)), take(0)
    )


def block_stats(scores, values, einsum_form):
    peak_value = jnp.max(scores, axis=-1)
    weights = jnp.exp(scores - peak_value[..., None])
    weight_total = jnp.sum(weights, axis=-1)
    rounded = weights.astype(jnp.bfloat16)
    summed = jnp.einsum(einsum_form, rounded, values, preferred_element_type=jnp.float32)
    return (peak_value, weight_total, summed)


def fold_pair(left_stats, right_stats):
    peak_value = jnp.maximum(left_stats[0], right_stats[0])
    left_weight = jnp.exp(left_stats[0] - peak_value)
    right_weight = jnp.exp(right_stats[0] - peak_value)
    weight_total = left_stats[1] * left_weight + right_stats[1] * right_weight
    summed = left_stats[2] * left_weight[..., None] + right_stats[2] * right_weight[..., None]
    return (peak_value, weight_total, summed)


def suffix_stats(query_head_rows, suffix_tokens, live_length, score_scale):
    row_count = suffix_tokens.shape[0]
    suffix_length = suffix_tokens.shape[2]
    kv_local = query_head_rows.shape[1]
    branch_suffix_keys = suffix_tokens[:, 0].reshape(row_count, suffix_length, kv_local, HEAD_SIZE)
    branch_suffix_values = suffix_tokens[:, 1].reshape(
        row_count, suffix_length, kv_local, HEAD_SIZE
    )
    scores = (
        jnp.einsum(
            "bgrd,btgd->bgrt",
            query_head_rows,
            branch_suffix_keys,
            preferred_element_type=jnp.float32,
        )
        * score_scale
    )
    live_mask = jnp.arange(suffix_length, dtype=jnp.int32)[None, :] < live_length[:, None]
    scores = jnp.where(live_mask[:, None, None, :], scores, NEG_FILL)
    return block_stats(scores, branch_suffix_values, "bgrt,btgd->bgrd")


def routing(parent, branch_per_shard, br_index, slot_rank, slot_match):
    grid_owner = (parent // branch_per_shard).reshape(-1, branch_per_shard)
    grid_local = (parent % branch_per_shard).reshape(-1, branch_per_shard)
    matched = (grid_owner == br_index)[:, :, None] & slot_match[None, :, :]
    outgoing = jnp.sum(jnp.where(matched, grid_local[:, :, None], 0), axis=1)
    own_owner = (
        lax.dynamic_slice_in_dim(parent, br_index * branch_per_shard, branch_per_shard)
        // branch_per_shard
    )
    incoming = own_owner * slot_match.shape[1] + slot_rank
    return (outgoing, incoming, own_owner)


def move_suffix(suffix_tokens, outgoing, incoming):
    dest_count = outgoing.shape[0]
    slot_count = outgoing.shape[1]
    tail_shape = suffix_tokens.shape[1:]
    outbound = suffix_tokens[outgoing.reshape(-1)].reshape((dest_count, slot_count) + tail_shape)
    arrived = lax.all_to_all(outbound, "br", split_axis=0, concat_axis=0, tiled=True)
    return arrived.reshape((dest_count * slot_count,) + tail_shape)[incoming]


def append_token(suffix_tokens, position_at, fresh_token):
    suffix_length = suffix_tokens.shape[2]
    target_mask = jnp.arange(suffix_length, dtype=jnp.int32)[None, :] == position_at[:, None]
    return jnp.where(
        target_mask[:, None, :, None], jnp.swapaxes(fresh_token, 0, 1)[:, :, None, :], suffix_tokens
    )


def general(
    prompt_key_value, suffix_page_store, page_table, lengths, parents, queries, fresh_key_value
):
    br_count = lax.axis_size("br")
    br_index = lax.axis_index("br")
    ctx_index = lax.axis_index("ctx")
    branch_per_shard = page_table.shape[0]
    page_count = page_table.shape[1]
    pool_dev = suffix_page_store.shape[0]
    page_rows = suffix_page_store.shape[2]
    head_width = suffix_page_store.shape[3]
    step_count = queries.shape[0]
    kv_local = head_width // HEAD_SIZE
    group_width = QUERY_HEADS // KEY_VALUE_HEADS
    slot_count = max(1, branch_per_shard // br_count)
    score_scale = 1.0 / math.sqrt(HEAD_SIZE)
    slot_rank = jnp.arange(branch_per_shard, dtype=jnp.int32) % slot_count
    slot_match = slot_rank[:, None] == jnp.arange(slot_count, dtype=jnp.int32)[None, :]
    gathered_pages = suffix_page_store[page_table - br_index * pool_dev]
    suffix_tokens = jnp.swapaxes(gathered_pages, 1, 2).reshape(
        branch_per_shard, 2, page_count * page_rows, head_width
    )
    length = lengths
    head_listing = lax.all_gather(queries, "ctx", axis=2, tiled=True)
    shared_prompt_keys = prompt_key_value[0].reshape(-1, KEY_VALUE_HEADS, HEAD_SIZE)
    shared_prompt_values = prompt_key_value[1].reshape(-1, KEY_VALUE_HEADS, HEAD_SIZE)
    outputs = []
    for decode_step_index in range(step_count):
        parent = parents[decode_step_index]
        outgoing, incoming, own_owner = routing(
            parent, branch_per_shard, br_index, slot_rank, slot_match
        )
        parent_length = length[parent]
        own_parent_length = lax.dynamic_slice_in_dim(
            parent_length, br_index * branch_per_shard, branch_per_shard
        )
        fresh_token = fresh_key_value[decode_step_index]
        query_mine = queries[decode_step_index].reshape(
            branch_per_shard, kv_local, group_width, HEAD_SIZE
        )
        suffix_tokens = append_token(
            move_suffix(suffix_tokens, outgoing, incoming), own_parent_length, fresh_token
        )
        suffix_part = suffix_stats(query_mine, suffix_tokens, own_parent_length + 1, score_scale)
        length = parent_length + 1
        query_complete = head_listing[decode_step_index].reshape(
            branch_per_shard, KEY_VALUE_HEADS, group_width, HEAD_SIZE
        )
        prompt_scores = (
            jnp.einsum(
                "bgrd,tgd->bgrt",
                query_complete,
                shared_prompt_keys,
                preferred_element_type=jnp.float32,
            )
            * score_scale
        )
        prompt_part = block_stats(prompt_scores, shared_prompt_values, "bgrt,tgd->bgrd")
        head_start = ctx_index * kv_local
        own_heads = tuple(
            (lax.dynamic_slice_in_dim(member, head_start, kv_local, 1) for member in prompt_part)
        )
        joined = fold_pair(own_heads, suffix_part)
        placed = tuple(
            (
                lax.dynamic_update_slice_in_dim(whole_part, own_part, head_start, 1)
                for whole_part, own_part in zip(prompt_part, joined)
            )
        )
        merged = joined_2((placed[0], placed[1], placed[2]), "ctx", fold_pair)
        combined = tuple(
            (lax.dynamic_slice_in_dim(member, head_start, kv_local, 1) for member in merged)
        )
        attention = (combined[2] / combined[1][..., None]).reshape(
            branch_per_shard, kv_local * group_width * HEAD_SIZE
        )
        outputs.append(attention.astype(jnp.bfloat16))
    return jnp.stack(outputs)


STEPS = 3
BRANCHES = 16
NODES = STEPS * BRANCHES
CAP = 8
QUAD = 4
LIVE = 96
LATE = 16
ROWS = 8 * NODES
MASKED = -1e30
EXP_SCALE = math.log2(math.e) / math.sqrt(HEAD_SIZE)
BF = jnp.bfloat16
F32 = jnp.float32
NT = (((1,), (1,)), ((), ()))


def onehot(condition):
    return jnp.where(condition, 1.0, 0.0).astype(BF)


def iota(shape, axis):
    return lax.broadcasted_iota(jnp.int32, shape, axis)


def stacked(rows, count, width):
    at = iota((count, width), 0)
    out = jnp.zeros((count, width), F32)
    for index, row in enumerate(rows):
        out = jnp.where(at == index, row.astype(F32), out)
    return out.astype(BF)


def dot(left, right):
    return jnp.dot(left, right, preferred_element_type=F32)


def dot_nt(left, right):
    return lax.dot_general(left, right, NT, preferred_element_type=F32)


def softmax_block(query, key, value):
    raw = dot_nt(query, key)
    peak = jnp.max(raw, axis=1, keepdims=True)
    weight = jnp.exp2((raw - peak) * EXP_SCALE)
    total = jnp.sum(weight, axis=1, keepdims=True)
    return peak, total, dot(weight.astype(BF), value)


def kernel(
    br_count, ctx_count,
    page_ref, len_ref, par_ref, q_ref, fresh_ref, pkv_ref, pages_ref,
    out_ref, flag_ref,
    kbuf, vbuf, kpage, vpage, qbuf, send_a, recv_a, send_b, recv_b, qrows, part_send, part_recv,
    code_high, code_low, late_high, late_low, stat_send, stat_recv, ret_send, ret_recv, num,
    kv_sem, g_send, g_recv, page_sem, q_send, q_recv, a_send, a_recv, b_send, b_recv, p_send, p_recv,
    r_send, r_recv, s_send, s_recv,
):
    me_c = lax.axis_index("ctx")
    me_r = lax.axis_index("br")

    core = lax.rem(me_c, 2)
    chip = me_c // 2
    chips = ctx_count // 2
    partner = me_c + 1 - 2 * core

    def peer_r(i):
        return lax.rem(me_r + i, br_count)

    def chip_at(t):
        return lax.rem(chip + t, chips)

    barrier = pltpu.get_barrier_semaphore()

    @pl.loop(1, chips)
    def _(t):
        pl.semaphore_signal(
            barrier, inc=1, device_id={"ctx": chip_at(t) * 2 + core}, device_id_type=pl.DeviceIdType.MESH)

    pl.semaphore_signal(barrier, inc=1, device_id={"ctx": partner}, device_id_type=pl.DeviceIdType.MESH)

    @pl.loop(1, br_count)
    def _(i):
        pl.semaphore_signal(barrier, inc=1, device_id={"br": peer_r(i)}, device_id_type=pl.DeviceIdType.MESH)

    def head_columns(t, parity):
        return pl.ds(pl.multiple_of((chip_at(t) * 2 + parity) * HEAD_SIZE, HEAD_SIZE), HEAD_SIZE)

    def kv_copy(t, which):
        buffer = kbuf if which == 0 else vbuf
        return pltpu.make_async_copy(
            pkv_ref.at[which, :, head_columns(t, core)], buffer.at[t, 0], kv_sem.at[which, t])

    def kv_give(t, which):
        buffer = kbuf if which == 0 else vbuf
        return pltpu.make_async_remote_copy(
            src_ref=pkv_ref.at[which, :, head_columns(t, 1 - core)], dst_ref=buffer.at[t, 1],
            send_sem=g_send.at[which, t], recv_sem=g_recv.at[which, t],
            device_id={"ctx": partner}, device_id_type=pl.DeviceIdType.MESH)

    key_pages = pltpu.make_async_copy(pages_ref.at[:, 0], kpage, page_sem.at[0])
    value_pages = pltpu.make_async_copy(pages_ref.at[:, 1], vpage, page_sem.at[1])

    @pl.loop(0, chips)
    def _(t):
        kv_copy(t, 0).start()
        kv_copy(t, 1).start()

    key_pages.start()
    value_pages.start()

    parent = par_ref[...]
    device = lax.shift_right_logical(parent, 4)
    place = parent & 15
    width = parent.shape[1]
    row_at = iota((width, width), 0)
    pick1 = onehot(row_at == parent[1:2])
    pick2 = onehot(row_at == parent[2:3])
    first = dot(stacked([device[0:1], place[0:1]], 16, width), pick1)
    second = dot(stacked([first[0:1], first[1:2], device[1:2], place[1:2]], 16, width), pick2)
    anc_dev = [device[0:1].astype(F32), first[0:1], second[0:1]]
    anc_loc = [place[0:1].astype(F32), first[1:2], second[1:2]]
    missing = jnp.full((1, width), -1.0, F32)
    par_hi = [missing, device[1:2].astype(F32), device[2:3].astype(F32) + 32.0]
    par_lo = [missing, place[1:2].astype(F32), place[2:3].astype(F32)]
    old_hi = [missing, missing, second[2:3]]
    old_lo = [missing, missing, second[3:4]]

    owner = iota((br_count, width), 0).astype(F32)
    to_owner = [onehot(owner == anc_dev[s]) for s in range(STEPS)]
    j = iota((128, 256), 0)
    lane = iota((128, 256), 1)
    b = lane & 127
    same_home = (j >> 4) == (b >> 4)
    counting = onehot(same_home & ((lane >= 128) | (j < b)))
    slots = [[], [], []]
    pair_count = []
    for tile in range(width // 128):
        cut = [m[:, tile * 128:(tile + 1) * 128] for m in to_owner]
        counted = dot(jnp.concatenate(cut, axis=0), counting)
        before = jnp.zeros((br_count, 128), F32)
        for s in range(STEPS):
            block = counted[s * br_count:(s + 1) * br_count]
            slots[s].append(jnp.sum(cut[s].astype(F32) * (block[:, :128] + before), axis=0, keepdims=True))
            before = before + block[:, 128:]
        pair_count.append(before)
    slot = [jnp.concatenate(parts, axis=1) for parts in slots]
    count = jnp.concatenate(pair_count, axis=1)
    most = jnp.max(count)
    first_count = jnp.minimum(count, QUAD)
    fullest = jnp.max(jnp.sum(first_count, axis=1, keepdims=True)) / BRANCHES
    latest = jnp.max(jnp.sum(count - first_count, axis=1, keepdims=True)) / BRANCHES
    over = (most > CAP) | (fullest > LIVE) | (latest > LATE)
    flag_ref[0, 0] = jnp.where(over, 1, 0)

    node = iota((128, STEPS * width), 0)
    column = iota((128, STEPS * width), 1)
    mine = onehot(((column & (width - 1)) == me_r * BRANCHES + (node & 15)) & ((node >> 4) == column // width))
    whither = jnp.concatenate([stacked([anc_dev[s], slot[s]], 16, width) for s in range(STEPS)], axis=1)
    own_row = dot_nt(whither, mine)
    own_col = dot_nt(mine, whither)
    own_dev, own_slot = own_col[:NODES, 0:1], own_col[:NODES, 1:2]
    at = iota((16 * br_count, 128), 0)
    is_node = iota((16 * br_count, 128), 1) < NODES
    own_pair = is_node & ((at >> 1).astype(F32) == own_row[0:1] * CAP + own_row[1:2])
    quad_row = own_row[0:1] * QUAD + own_row[1:2]
    own_first = is_node & (own_row[1:2] < QUAD) & ((at >> 2).astype(F32) == quad_row)
    own_late = is_node & (own_row[1:2] >= QUAD) & ((at >> 2).astype(F32) == quad_row - QUAD)
    queries = q_ref[...]

    def padded(rows):
        return jnp.concatenate([rows, jnp.zeros((128 - NODES, rows.shape[1]), BF)], axis=0)

    fresh = [padded(jnp.concatenate([fresh_ref[s, kind] for s in range(STEPS)], axis=0)) for kind in range(2)]
    quarters = jnp.concatenate([padded(queries[:, 256 * n:256 * (n + 1)]) for n in range(4)], axis=0)

    def spread_over(rows, parts, mask):
        return jnp.concatenate([onehot(mask & ((rows & (parts - 1)) == part)) for part in range(parts)], axis=1)

    send_a[:, pl.ds(0, 256)] = dot(spread_over(at, 4, own_first), quarters).astype(BF)
    send_a[:, pl.ds(256, 128)] = dot(spread_over(at, 2, own_pair), jnp.concatenate(fresh, axis=0)).astype(BF)
    send_b[...] = dot(spread_over(at, 4, own_late), quarters).astype(BF)

    def rows16(index):
        return pl.ds(pl.multiple_of(index * 16, 16), 16)

    def to_br(i, source, send, recv, send_sem, recv_sem):
        peer = peer_r(i)
        return pltpu.make_async_remote_copy(
            src_ref=send.at[rows16(peer)], dst_ref=recv.at[rows16(source)],
            send_sem=send_sem.at[peer], recv_sem=recv_sem.at[source],
            device_id={"br": peer}, device_id_type=pl.DeviceIdType.MESH)

    def message_a(i, source):
        return to_br(i, source, send_a, recv_a, a_send, a_recv)

    def message_b(i, source):
        return to_br(i, source, send_b, recv_b, b_send, b_recv)

    def query_copy(t, source):
        return pltpu.make_async_remote_copy(
            src_ref=q_ref, dst_ref=qbuf.at[source],
            send_sem=q_send.at[t], recv_sem=q_recv.at[source],
            device_id={"ctx": chip_at(t) * 2 + core}, device_id_type=pl.DeviceIdType.MESH)

    pl.semaphore_wait(barrier, chips + br_count - 1)

    @pl.loop(1, chips)
    def _(t):
        query_copy(t, chip).start()

    @pl.loop(1, br_count)
    def _(i):
        message_a(i, me_r).start()

    @pl.loop(1, chips)
    def _(t):
        kv_give(t, 0).start()
        kv_give(t, 1).start()

    kv_give(0, 0).start()
    kv_give(0, 1).start()

    @pl.loop(1, br_count)
    def _(i):
        message_b(i, me_r).start()

    own16 = rows16(me_r)
    recv_a[own16, :] = send_a[own16, :]
    recv_b[own16, :] = send_b[own16, :]
    qbuf[chip] = queries

    here = (iota((br_count, width), 0) == me_r).astype(F32)
    home_count = jnp.sum(here * count, axis=0, keepdims=True)
    col_at = iota((width, width), 1)
    earlier = onehot(((row_at & 15) == 0) & ((row_at >> 4) < (col_at >> 4)))
    home_first = jnp.minimum(home_count, QUAD)
    ahead = dot(stacked([home_first, home_count - home_first], 16, width), earlier)
    home = lax.shift_right_logical(iota((1, width), 1), 4).astype(F32)
    local_at = (iota((1, width), 1) & 15).astype(F32)
    ones = jnp.ones((1, width), F32)
    live_rows = iota((128, width), 0).astype(F32)
    chosen, known = [], []
    for s in range(STEPS):
        arrives = anc_dev[s] == me_r.astype(F32)
        first_at = ahead[0:1] + slot[s]
        late_at = ahead[1:2] + slot[s] - QUAD
        late_at = jnp.where((slot[s] < CAP) & (late_at < LATE), late_at + LIVE, -1.0)
        place_at = jnp.where(slot[s] < QUAD, jnp.where(first_at < LIVE, first_at, -1.0), late_at)
        place_at = jnp.where(arrives, place_at, -1.0)
        chosen.append(onehot(live_rows == place_at))
        known.append(stacked([
            ones, home, slot[s], anc_loc[s], home + 32.0 * s, local_at,
            par_hi[s], par_lo[s], old_hi[s], old_lo[s]], 16, width))
    chosen = jnp.concatenate(chosen, axis=1)
    known = jnp.concatenate(known, axis=1)
    row_info = dot_nt(known, chosen)
    col_info = dot_nt(chosen, known)
    here_row = row_info[0:1] > 0.5
    here_col = col_info[:, 0:1] > 0.5
    slot_row, slot_col = row_info[2:3], col_info[:, 2:3]
    pair_col = jnp.where(here_col, col_info[:, 1:2] * CAP + slot_col, -1.0)
    quad_col = jnp.where(here_col, col_info[:, 1:2] * QUAD + slot_col, -1.0)
    quad_row = jnp.where(here_row, row_info[1:2] * QUAD + slot_row, -1.0)
    self_row = jnp.where(here_row, row_info[4:5] * 16.0 + row_info[5:6], -100.0)
    on_path = self_row == col_info[:, 4:5] * 16.0 + col_info[:, 5:6]
    on_path = on_path | (self_row == col_info[:, 6:7] * 16.0 + col_info[:, 7:8])
    on_path = on_path | (self_row == col_info[:, 8:9] * 16.0 + col_info[:, 9:10])
    path = jnp.where(on_path, 1.0, 0.0)
    anc_col = col_info[:, 3:4]
    length_col = jnp.zeros((128, 1), F32)
    for branch in range(BRANCHES):
        length_col = jnp.where(anc_col == branch, len_ref[me_r * BRANCHES + branch].astype(F32), length_col)

    stat_lane = iota((NODES, 128), 1)

    def part_copy(t, source):
        peer = chip_at(t)
        return pltpu.make_async_remote_copy(
            src_ref=part_send.at[peer], dst_ref=part_recv.at[source],
            send_sem=p_send.at[peer], recv_sem=p_recv.at[source],
            device_id={"ctx": peer * 2 + core}, device_id_type=pl.DeviceIdType.MESH)

    def prompt_block(t, block):
        where = chip_at(t)
        if block == 0:
            kv_copy(t, 0).wait()
            kv_copy(t, 1).wait()
        else:
            kv_give(t, 0).wait_recv()
            kv_give(t, 1).wait_recv()
        key = kbuf[t, block]
        value = vbuf[t, block]
        old = part_send[where, pl.ds(ROWS, NODES)]
        stat = jnp.zeros((NODES, 128), F32)
        for half in range(2):
            heads = range(4 * half, 4 * half + 4)
            rows = jnp.concatenate([qbuf[where, :, pl.ds(h * 128, 128)] for h in heads], axis=0)
            peak, total, summed = softmax_block(rows, key, value)
            part = pl.ds(half * 4 * NODES, 4 * NODES)
            if block == 1:
                old_peak = jnp.concatenate([old[:, h:h + 1] for h in heads], axis=0)
                old_total = jnp.concatenate([old[:, 8 + h:9 + h] for h in heads], axis=0)
                joint = jnp.maximum(peak, old_peak)
                old_factor = jnp.exp2((old_peak - joint) * EXP_SCALE)
                factor = jnp.exp2((peak - joint) * EXP_SCALE)
                total = old_factor * old_total + factor * total
                summed = old_factor * part_send[where, part] + factor * summed
                peak = joint
            part_send[where, part] = summed
            for h in heads:
                cut = slice((h - 4 * half) * NODES, (h - 4 * half + 1) * NODES)
                stat = jnp.where(stat_lane == h, peak[cut], stat)
                stat = jnp.where(stat_lane == 8 + h, total[cut], stat)
        part_send[where, pl.ds(ROWS, NODES)] = stat

    def prompt_head(t):
        query_copy(t, chip_at(t)).wait_recv()
        prompt_block(t, 0)
        prompt_block(t, 1)
        part_copy(t, chip).start()

    prompt_block(0, 0)

    @pl.loop(1, chips - 1)
    def _(t):
        prompt_head(t)

    @pl.loop(1, br_count)
    def _(i):
        message_a(0, peer_r(i)).wait_recv()

    got_a = recv_a[...]
    gather = iota((128, 16 * br_count), 1)
    pairs = (gather >> 1).astype(F32) == pair_col
    new_key = dot(onehot(pairs & ((gather & 1) == 0)), got_a[:, 256:]).astype(BF)
    new_value = dot(onehot(pairs & ((gather & 1) == 1)), got_a[:, 256:]).astype(BF)

    def gathered(address, got):
        count = address.shape[0]
        place = iota((count, 16 * br_count), 1)
        match = (place >> 2).astype(F32) == address
        parts = jnp.concatenate([onehot(match & ((place & 3) == part)) for part in range(4)], axis=0)
        return dot(parts, got).astype(BF)

    taken = gathered(quad_col[:LIVE], got_a[:, :256])
    for n in range(4):
        for half in range(2):
            qrows[n, pl.ds(half * LIVE, LIVE)] = taken[n * LIVE:(n + 1) * LIVE, half * 128:(half + 1) * 128]
    key_pages.wait()
    value_pages.wait()

    def suffix_block(rows, anc, length, see):
        count = rows.shape[0]
        fold = jnp.zeros((count, 256), F32)
        for branch in range(BRANCHES):
            key = jnp.concatenate([kpage[lax.rem(page_ref[page, branch], 32)] for page in range(2)], axis=0)
            fold = jnp.where(anc == branch, dot_nt(rows, key), fold)
        fold = jnp.where(iota((count, 256), 1).astype(F32) < length, fold, MASKED)
        new = jnp.where(see > 0.5, dot_nt(rows, new_key), MASKED)
        peak = jnp.maximum(jnp.max(fold, axis=1, keepdims=True), jnp.max(new, axis=1, keepdims=True))
        weight = jnp.exp2((fold - peak) * EXP_SCALE)
        new = jnp.exp2((new - peak) * EXP_SCALE)
        total = jnp.sum(weight, axis=1, keepdims=True) + jnp.sum(new, axis=1, keepdims=True)
        weight = weight.astype(BF)
        summed = dot(new.astype(BF), new_value)
        for branch in range(0, BRANCHES, 2):
            value = jnp.concatenate([jnp.concatenate(
                [vpage[lax.rem(page_ref[page, b], 32)] for page in range(2)], axis=0)
                for b in (branch, branch + 1)], axis=1)
            both = dot(weight, value)
            summed = jnp.where(anc == branch, summed + both[:, :128], summed)
            summed = jnp.where(anc == branch + 1, summed + both[:, 128:], summed)
        largest = jnp.max(jnp.abs(summed), axis=1, keepdims=True)
        coded = jnp.round(summed * jnp.where(largest > 0.0, 32767.0 / largest, 0.0))
        upper = jnp.floor(coded / 256.0)
        sum_log = peak * EXP_SCALE + jnp.log2(total)
        return upper.astype(BF), (coded - 256.0 * upper).astype(BF), sum_log, largest / (32767.0 * total)

    def repeated(column, times):
        return jnp.concatenate([column] * times, axis=0)

    def stat_rows(stat, cut):
        lane = iota(stat.shape, 1)
        stat = jnp.where((lane >> 4).astype(F32) == slot_col[cut], stat, 0.0)
        home_at = iota((br_count, stat.shape[0]), 0).astype(F32)
        own_home = jnp.where(here_row[:, cut] & (home_at == row_info[1:2, cut]), 1.0, 0.0)
        return jnp.dot(own_home, stat, precision=lax.Precision.HIGHEST, preferred_element_type=F32)

    def return_rows(address, high, low):
        count = address.shape[1]
        rows = iota((16 * br_count, count), 0)
        spread = spread_over(rows, 4, (rows >> 2).astype(F32) == address)
        return (256.0 * dot(spread, high) + dot(spread, low)).astype(jnp.int32).astype(jnp.int16)

    def returned(group, i, source):
        return to_br(i, source, ret_send.at[group], ret_recv.at[group], r_send.at[group], r_recv.at[group])

    def returned_stat(group, i, source):
        peer = peer_r(i)
        return pltpu.make_async_remote_copy(
            src_ref=stat_send.at[group, peer], dst_ref=stat_recv.at[group, source],
            send_sem=s_send.at[group, peer], recv_sem=s_recv.at[group, source],
            device_id={"br": peer}, device_id_type=pl.DeviceIdType.MESH)

    def give_back(group, stat, rows):
        for home_index in range(br_count):
            stat_send[group, home_index] = stat[home_index:home_index + 1]
        ret_send[group] = rows

        @pl.loop(1, br_count)
        def _(i):
            returned_stat(group, i, me_r).start()
            returned(group, i, me_r).start()

        stat_recv[group, me_r] = stat_send[group, me_r]
        ret_recv[group, own16, :] = ret_send[group, own16, :]

    first_lane = iota((LIVE, 128), 1) & 15

    def suffix_quarter(n, stat):
        high, low, sum_log, unit = suffix_block(
            qrows[n], repeated(anc_col[:LIVE], 2), repeated(length_col[:LIVE], 2), repeated(path[:LIVE], 2))
        quarter = pl.ds(pl.multiple_of(n * LIVE, LIVE), LIVE)
        for half in range(2):
            cut = slice(half * LIVE, (half + 1) * LIVE)
            code_high[quarter, pl.ds(half * 128, 128)] = high[cut]
            code_low[quarter, pl.ds(half * 128, 128)] = low[cut]
            stat = jnp.where(first_lane == 2 * n + half, sum_log[cut], stat)
            stat = jnp.where(first_lane == 8 + 2 * n + half, unit[cut], stat)
        return stat

    stat_a = lax.fori_loop(0, 4, suffix_quarter, jnp.zeros((LIVE, 128), F32))

    give_back(0, stat_rows(stat_a, slice(0, LIVE)),
              return_rows(quad_row[:, :LIVE], code_high[...], code_low[...]))

    @pl.loop(1, br_count)
    def _(i):
        message_b(0, peer_r(i)).wait_recv()

    late = slice(LIVE, LIVE + LATE)
    taken = gathered(quad_col[late] - QUAD, recv_b[...])
    rows = jnp.concatenate([
        taken[(h // 2) * LATE:(h // 2 + 1) * LATE, (h % 2) * 128:(h % 2 + 1) * 128] for h in range(8)], axis=0)
    high, low, sum_log, unit = suffix_block(
        rows, repeated(anc_col[late], 8), repeated(length_col[late], 8), repeated(path[late], 8))
    late_lane = iota((LATE, 128), 1) & 15
    stat_b = jnp.zeros((LATE, 128), F32)
    for h in range(8):
        cut = slice(h * LATE, (h + 1) * LATE)
        late_high[pl.ds((h // 2) * LATE, LATE), pl.ds((h % 2) * 128, 128)] = high[cut]
        late_low[pl.ds((h // 2) * LATE, LATE), pl.ds((h % 2) * 128, 128)] = low[cut]
        stat_b = jnp.where(late_lane == h, sum_log[cut], stat_b)
        stat_b = jnp.where(late_lane == 8 + h, unit[cut], stat_b)
    give_back(1, stat_rows(stat_b, late),
              return_rows(quad_row[:, late] - QUAD, late_high[...], late_low[...]))

    prompt_head(chips - 1)
    prompt_block(0, 1)

    part_recv[chip] = part_send[chip]

    @pl.loop(1, chips)
    def _(t):
        part_copy(t, chip_at(t)).wait_recv()

    stats = [part_recv[c, pl.ds(ROWS, NODES)] for c in range(4)]
    top = functools.reduce(jnp.maximum, stats)
    factors = [jnp.exp2((stat - top) * EXP_SCALE) for stat in stats]
    den = jnp.zeros((NODES, 128), F32)
    for c in range(4):
        den = den + factors[c] * pltpu.roll(stats[c], 120, 1)
    for h in range(8):
        summed = jnp.zeros((NODES, 128), F32)
        for c in range(4):
            summed = summed + factors[c][:, h:h + 1] * part_recv[c, pl.ds(h * NODES, NODES)]
        num[h] = summed

    back_low = iota((4 * NODES, 16 * br_count), 1)
    address = repeated(own_dev * QUAD + own_slot, 4)
    quarter_at = iota((4 * NODES, 16 * br_count), 0) // NODES

    def collected(group, match):
        collect = onehot(match & ((back_low & 3) == quarter_at))
        arrived = ret_recv[group].astype(jnp.int32)
        upper = dot(collect, (arrived >> 8).astype(F32).astype(BF))
        return 256.0 * upper + dot(collect, (arrived & 255).astype(F32).astype(BF))

    in_first = repeated(own_slot, 4) < QUAD
    quad_at = (back_low >> 2).astype(F32)

    @pl.loop(1, br_count)
    def _(i):
        returned_stat(0, 0, peer_r(i)).wait_recv()
        returned(0, 0, peer_r(i)).wait_recv()

    coded = collected(0, in_first & (quad_at == address))

    @pl.loop(1, br_count)
    def _(i):
        returned_stat(1, 0, peer_r(i)).wait_recv()
        returned(1, 0, peer_r(i)).wait_recv()

    coded = coded + collected(1, jnp.logical_not(in_first) & (quad_at == address - QUAD))
    from_device = jnp.where(iota((NODES, br_count), 1).astype(F32) == own_dev, 1.0, 0.0)
    all_stat = jnp.concatenate([stat_recv[0, d] + stat_recv[1, d] for d in range(br_count)], axis=0)
    back_stat = jnp.dot(from_device, all_stat, precision=lax.Precision.HIGHEST, preferred_element_type=F32)
    back_stat = jnp.where((stat_lane >> 4).astype(F32) == own_slot, back_stat, 0.0)
    for shift in (64, 32, 16):
        back_stat = back_stat + pltpu.roll(back_stat, shift, 1)
    prompt_log = top * EXP_SCALE
    overall = jnp.maximum(prompt_log, back_stat)
    prompt_factor = jnp.exp2(prompt_log - overall)
    suffix_factor = jnp.exp2(back_stat - overall)
    den = prompt_factor * den + suffix_factor
    unit = suffix_factor * pltpu.roll(back_stat, 120, 1)
    for h in range(8):
        back_home = coded[(h // 2) * NODES:(h // 2 + 1) * NODES, (h % 2) * 128:(h % 2 + 1) * 128]
        joined = prompt_factor[:, h:h + 1] * num[h] + unit[:, h:h + 1] * back_home
        out_ref[:, pl.ds(h * 128, 128)] = (joined / den[:, h:h + 1]).astype(BF)

    @pl.loop(1, chips)
    def _(t):
        query_copy(t, chip).wait_send()
        part_copy(t, chip).wait_send()

    @pl.loop(0, chips)
    def _(t):
        kv_give(t, 0).wait_send()
        kv_give(t, 1).wait_send()

    @pl.loop(1, br_count)
    def _(i):
        message_a(i, me_r).wait_send()
        message_b(i, me_r).wait_send()
        for group in range(2):
            returned_stat(group, i, me_r).wait_send()
            returned(group, i, me_r).wait_send()


def local(
    prompt_key_value, suffix_page_store, page_table, lengths, parents, queries, fresh_key_value
):
    br_count = lax.axis_size("br")
    ctx_count = lax.axis_size("ctx")
    vmem = pl.BlockSpec(memory_space=pltpu.VMEM)
    smem = pl.BlockSpec(memory_space=pltpu.SMEM)
    anywhere = pl.BlockSpec(memory_space=pl.ANY)
    dma = pltpu.SemaphoreType.DMA
    out, flag = pl.pallas_call(
        functools.partial(kernel, br_count, ctx_count),
        out_shape=(
            jax.ShapeDtypeStruct((NODES, 1024), BF),
            jax.ShapeDtypeStruct((1, 1), jnp.int32),
        ),
        in_specs=[smem, smem, vmem, vmem, vmem, anywhere, anywhere],
        out_specs=(vmem, smem),
        scratch_shapes=[
            pltpu.VMEM((4, 2, 2048, 128), BF),
            pltpu.VMEM((4, 2, 2048, 128), BF),
            pltpu.VMEM((32, 128, 128), BF),
            pltpu.VMEM((32, 128, 128), BF),
            pltpu.VMEM((4, NODES, 1024), BF),
            pltpu.VMEM((16 * br_count, 384), BF),
            pltpu.VMEM((16 * br_count, 384), BF),
            pltpu.VMEM((16 * br_count, 256), BF),
            pltpu.VMEM((16 * br_count, 256), BF),
            pltpu.VMEM((4, 2 * LIVE, 128), BF),
            pltpu.VMEM((4, ROWS + NODES, 128), F32),
            pltpu.VMEM((4, ROWS + NODES, 128), F32),
            pltpu.VMEM((4 * LIVE, 256), BF),
            pltpu.VMEM((4 * LIVE, 256), BF),
            pltpu.VMEM((4 * LATE, 256), BF),
            pltpu.VMEM((4 * LATE, 256), BF),
            pltpu.VMEM((2, br_count, 1, 128), F32),
            pltpu.VMEM((2, br_count, 1, 128), F32),
            pltpu.VMEM((2, 16 * br_count, 256), jnp.int16),
            pltpu.VMEM((2, 16 * br_count, 256), jnp.int16),
            pltpu.VMEM((8, NODES, 128), F32),
            dma((2, 4)), dma((2, 4)), dma((2, 4)), dma((2,)), dma((4,)), dma((4,)), dma((32,)), dma((32,)), dma((32,)), dma((32,)),
            dma((4,)), dma((4,)), dma((2, 32)), dma((2, 32)), dma((2, 32)), dma((2, 32)),
        ],
        compiler_params=pltpu.CompilerParams(
            collective_id=0, has_side_effects=True, vmem_limit_bytes=56 * 1024 * 1024
        ),
    )(
        page_table.T, lengths, parents, queries.reshape(NODES, 1024), fresh_key_value,
        prompt_key_value, suffix_page_store,
    )
    operands = (
        prompt_key_value, suffix_page_store, page_table, lengths, parents, queries, fresh_key_value
    )
    return lax.cond(
        flag[0, 0] > 0,
        lambda *whole: general(*whole),
        lambda *whole: out.reshape(STEPS, BRANCHES, 1024),
        *operands,
    )


def solution(mesh):
    in_specs = (
        P(None, "ctx", None),
        P("br", None, None, "ctx"),
        P("br", None),
        P(),
        P(),
        P(None, "br", "ctx"),
        P(None, None, "br", "ctx"),
    )
    out_specs = P(None, "br", "ctx")
    return jax.shard_map(local, mesh=mesh, in_specs=in_specs, out_specs=out_specs, check_vma=False)
```

```python
import functools
import math

import jax
import jax.numpy as jnp
from jax import lax
from jax.experimental import pallas as pl
from jax.experimental.pallas import tpu as pltpu
from jax.sharding import PartitionSpec as P

QUERY_HEADS = 64
KEY_VALUE_HEADS = 8
HEAD_SIZE = 128


NEG_FILL = -1e30


def joined_2(part, axis, combine):
    gathered = jax.tree.map(lambda a: lax.all_gather(a, axis), part)

    def take(source):
        return jax.tree.map(lambda a: lax.dynamic_index_in_dim(a, source, 0, False), gathered)

    return lax.fori_loop(
        1, lax.axis_size(axis), lambda source, state: combine(state, take(source)), take(0)
    )


def block_stats(scores, values, einsum_form):
    peak_value = jnp.max(scores, axis=-1)
    weights = jnp.exp(scores - peak_value[..., None])
    weight_total = jnp.sum(weights, axis=-1)
    rounded = weights.astype(jnp.bfloat16)
    summed = jnp.einsum(einsum_form, rounded, values, preferred_element_type=jnp.float32)
    return (peak_value, weight_total, summed)


def fold_pair(left_stats, right_stats):
    peak_value = jnp.maximum(left_stats[0], right_stats[0])
    left_weight = jnp.exp(left_stats[0] - peak_value)
    right_weight = jnp.exp(right_stats[0] - peak_value)
    weight_total = left_stats[1] * left_weight + right_stats[1] * right_weight
    summed = left_stats[2] * left_weight[..., None] + right_stats[2] * right_weight[..., None]
    return (peak_value, weight_total, summed)


def suffix_stats(query_head_rows, suffix_tokens, live_length, score_scale):
    row_count = suffix_tokens.shape[0]
    suffix_length = suffix_tokens.shape[2]
    kv_local = query_head_rows.shape[1]
    branch_suffix_keys = suffix_tokens[:, 0].reshape(row_count, suffix_length, kv_local, HEAD_SIZE)
    branch_suffix_values = suffix_tokens[:, 1].reshape(
        row_count, suffix_length, kv_local, HEAD_SIZE
    )
    scores = (
        jnp.einsum(
            "bgrd,btgd->bgrt",
            query_head_rows,
            branch_suffix_keys,
            preferred_element_type=jnp.float32,
        )
        * score_scale
    )
    live_mask = jnp.arange(suffix_length, dtype=jnp.int32)[None, :] < live_length[:, None]
    scores = jnp.where(live_mask[:, None, None, :], scores, NEG_FILL)
    return block_stats(scores, branch_suffix_values, "bgrt,btgd->bgrd")


def routing(parent, branch_per_shard, br_index, slot_rank, slot_match):
    grid_owner = (parent // branch_per_shard).reshape(-1, branch_per_shard)
    grid_local = (parent % branch_per_shard).reshape(-1, branch_per_shard)
    matched = (grid_owner == br_index)[:, :, None] & slot_match[None, :, :]
    outgoing = jnp.sum(jnp.where(matched, grid_local[:, :, None], 0), axis=1)
    own_owner = (
        lax.dynamic_slice_in_dim(parent, br_index * branch_per_shard, branch_per_shard)
        // branch_per_shard
    )
    incoming = own_owner * slot_match.shape[1] + slot_rank
    return (outgoing, incoming, own_owner)


def move_suffix(suffix_tokens, outgoing, incoming):
    dest_count = outgoing.shape[0]
    slot_count = outgoing.shape[1]
    tail_shape = suffix_tokens.shape[1:]
    outbound = suffix_tokens[outgoing.reshape(-1)].reshape((dest_count, slot_count) + tail_shape)
    arrived = lax.all_to_all(outbound, "br", split_axis=0, concat_axis=0, tiled=True)
    return arrived.reshape((dest_count * slot_count,) + tail_shape)[incoming]


def append_token(suffix_tokens, position_at, fresh_token):
    suffix_length = suffix_tokens.shape[2]
    target_mask = jnp.arange(suffix_length, dtype=jnp.int32)[None, :] == position_at[:, None]
    return jnp.where(
        target_mask[:, None, :, None], jnp.swapaxes(fresh_token, 0, 1)[:, :, None, :], suffix_tokens
    )


def general(
    prompt_key_value, suffix_page_store, page_table, lengths, parents, queries, fresh_key_value
):
    br_count = lax.axis_size("br")
    br_index = lax.axis_index("br")
    ctx_index = lax.axis_index("ctx")
    branch_per_shard = page_table.shape[0]
    page_count = page_table.shape[1]
    pool_dev = suffix_page_store.shape[0]
    page_rows = suffix_page_store.shape[2]
    head_width = suffix_page_store.shape[3]
    step_count = queries.shape[0]
    kv_local = head_width // HEAD_SIZE
    group_width = QUERY_HEADS // KEY_VALUE_HEADS
    slot_count = max(1, branch_per_shard // br_count)
    score_scale = 1.0 / math.sqrt(HEAD_SIZE)
    slot_rank = jnp.arange(branch_per_shard, dtype=jnp.int32) % slot_count
    slot_match = slot_rank[:, None] == jnp.arange(slot_count, dtype=jnp.int32)[None, :]
    gathered_pages = suffix_page_store[page_table - br_index * pool_dev]
    suffix_tokens = jnp.swapaxes(gathered_pages, 1, 2).reshape(
        branch_per_shard, 2, page_count * page_rows, head_width
    )
    length = lengths
    head_listing = lax.all_gather(queries, "ctx", axis=2, tiled=True)
    shared_prompt_keys = prompt_key_value[0].reshape(-1, KEY_VALUE_HEADS, HEAD_SIZE)
    shared_prompt_values = prompt_key_value[1].reshape(-1, KEY_VALUE_HEADS, HEAD_SIZE)
    outputs = []
    for decode_step_index in range(step_count):
        parent = parents[decode_step_index]
        outgoing, incoming, own_owner = routing(
            parent, branch_per_shard, br_index, slot_rank, slot_match
        )
        parent_length = length[parent]
        own_parent_length = lax.dynamic_slice_in_dim(
            parent_length, br_index * branch_per_shard, branch_per_shard
        )
        fresh_token = fresh_key_value[decode_step_index]
        query_mine = queries[decode_step_index].reshape(
            branch_per_shard, kv_local, group_width, HEAD_SIZE
        )
        suffix_tokens = append_token(
            move_suffix(suffix_tokens, outgoing, incoming), own_parent_length, fresh_token
        )
        suffix_part = suffix_stats(query_mine, suffix_tokens, own_parent_length + 1, score_scale)
        length = parent_length + 1
        query_complete = head_listing[decode_step_index].reshape(
            branch_per_shard, KEY_VALUE_HEADS, group_width, HEAD_SIZE
        )
        prompt_scores = (
            jnp.einsum(
                "bgrd,tgd->bgrt",
                query_complete,
                shared_prompt_keys,
                preferred_element_type=jnp.float32,
            )
            * score_scale
        )
        prompt_part = block_stats(prompt_scores, shared_prompt_values, "bgrt,tgd->bgrd")
        head_start = ctx_index * kv_local
        own_heads = tuple(
            (lax.dynamic_slice_in_dim(member, head_start, kv_local, 1) for member in prompt_part)
        )
        joined = fold_pair(own_heads, suffix_part)
        placed = tuple(
            (
                lax.dynamic_update_slice_in_dim(whole_part, own_part, head_start, 1)
                for whole_part, own_part in zip(prompt_part, joined)
            )
        )
        merged = joined_2((placed[0], placed[1], placed[2]), "ctx", fold_pair)
        combined = tuple(
            (lax.dynamic_slice_in_dim(member, head_start, kv_local, 1) for member in merged)
        )
        attention = (combined[2] / combined[1][..., None]).reshape(
            branch_per_shard, kv_local * group_width * HEAD_SIZE
        )
        outputs.append(attention.astype(jnp.bfloat16))
    return jnp.stack(outputs)


STEPS = 3
BRANCHES = 16
NODES = STEPS * BRANCHES
CAP = 8
QUAD = 4
LIVE = 96
LATE = 16
ROWS = 8 * NODES
MASKED = -1e30
EXP_SCALE = math.log2(math.e) / math.sqrt(HEAD_SIZE)
BF = jnp.bfloat16
F32 = jnp.float32
NT = (((1,), (1,)), ((), ()))


def onehot(condition):
    return jnp.where(condition, 1.0, 0.0).astype(BF)


def iota(shape, axis):
    return lax.broadcasted_iota(jnp.int32, shape, axis)


def stacked(rows, count, width):
    at = iota((count, width), 0)
    out = jnp.zeros((count, width), F32)
    for index, row in enumerate(rows):
        out = jnp.where(at == index, row.astype(F32), out)
    return out.astype(BF)


def dot(left, right):
    return jnp.dot(left, right, preferred_element_type=F32)


def dot_nt(left, right):
    return lax.dot_general(left, right, NT, preferred_element_type=F32)


def softmax_block(query, key, value):
    raw = dot_nt(query, key)
    peak = jnp.max(raw, axis=1, keepdims=True)
    weight = jnp.exp2((raw - peak) * EXP_SCALE)
    total = jnp.sum(weight, axis=1, keepdims=True)
    return peak, total, dot(weight.astype(BF), value)


def kernel(
    br_count, ctx_count,
    page_ref, len_ref, par_ref, q_ref, fresh_ref, pkv_ref, pages_ref,
    out_ref, flag_ref,
    kbuf, vbuf, kpage, vpage, qbuf, send_a, recv_a, send_b, recv_b, qrows, part_send, part_recv,
    code_high, code_low, late_high, late_low, stat_send, stat_recv, ret_send, ret_recv, late_send, late_recv, num,
    kv_sem, g_send, g_recv, page_sem, q_send, q_recv, a_send, a_recv, b_send, b_recv, p_send, p_recv,
    r_send, r_recv, s_send, s_recv,
):
    me_c = lax.axis_index("ctx")
    me_r = lax.axis_index("br")

    core = lax.rem(me_c, 2)
    chip = me_c // 2
    chips = ctx_count // 2
    partner = me_c + 1 - 2 * core

    def peer_r(i):
        return lax.rem(me_r + i, br_count)

    def chip_at(t):
        return lax.rem(chip + t, chips)

    barrier = pltpu.get_barrier_semaphore()

    @pl.loop(1, chips)
    def _(t):
        pl.semaphore_signal(
            barrier, inc=1, device_id={"ctx": chip_at(t) * 2 + core}, device_id_type=pl.DeviceIdType.MESH)

    pl.semaphore_signal(barrier, inc=1, device_id={"ctx": partner}, device_id_type=pl.DeviceIdType.MESH)

    @pl.loop(1, br_count)
    def _(i):
        pl.semaphore_signal(barrier, inc=1, device_id={"br": peer_r(i)}, device_id_type=pl.DeviceIdType.MESH)

    def head_columns(t, parity):
        return pl.ds(pl.multiple_of((chip_at(t) * 2 + parity) * HEAD_SIZE, HEAD_SIZE), HEAD_SIZE)

    def kv_copy(t, which):
        buffer = kbuf if which == 0 else vbuf
        return pltpu.make_async_copy(
            pkv_ref.at[which, :, head_columns(t, core)], buffer.at[t, 0], kv_sem.at[which, t])

    def kv_give(t, which):
        buffer = kbuf if which == 0 else vbuf
        return pltpu.make_async_remote_copy(
            src_ref=pkv_ref.at[which, :, head_columns(t, 1 - core)], dst_ref=buffer.at[t, 1],
            send_sem=g_send.at[which, t], recv_sem=g_recv.at[which, t],
            device_id={"ctx": partner}, device_id_type=pl.DeviceIdType.MESH)

    key_pages = pltpu.make_async_copy(pages_ref.at[:, 0], kpage, page_sem.at[0])
    value_pages = pltpu.make_async_copy(pages_ref.at[:, 1], vpage, page_sem.at[1])

    @pl.loop(0, chips)
    def _(t):
        kv_copy(t, 0).start()
        kv_copy(t, 1).start()

    key_pages.start()
    value_pages.start()

    parent = par_ref[...]
    device = lax.shift_right_logical(parent, 4)
    place = parent & 15
    width = parent.shape[1]
    row_at = iota((width, width), 0)
    pick1 = onehot(row_at == parent[1:2])
    pick2 = onehot(row_at == parent[2:3])
    first = dot(stacked([device[0:1], place[0:1]], 16, width), pick1)
    second = dot(stacked([first[0:1], first[1:2], device[1:2], place[1:2]], 16, width), pick2)
    anc_dev = [device[0:1].astype(F32), first[0:1], second[0:1]]
    anc_loc = [place[0:1].astype(F32), first[1:2], second[1:2]]
    missing = jnp.full((1, width), -1.0, F32)
    par_hi = [missing, device[1:2].astype(F32), device[2:3].astype(F32) + 32.0]
    par_lo = [missing, place[1:2].astype(F32), place[2:3].astype(F32)]
    old_hi = [missing, missing, second[2:3]]
    old_lo = [missing, missing, second[3:4]]

    owner = iota((br_count, width), 0).astype(F32)
    to_owner = [onehot(owner == anc_dev[s]) for s in range(STEPS)]
    j = iota((128, 256), 0)
    lane = iota((128, 256), 1)
    b = lane & 127
    same_home = (j >> 4) == (b >> 4)
    counting = onehot(same_home & ((lane >= 128) | (j < b)))
    slots = [[], [], []]
    pair_count = []
    for tile in range(width // 128):
        cut = [m[:, tile * 128:(tile + 1) * 128] for m in to_owner]
        counted = dot(jnp.concatenate(cut, axis=0), counting)
        before = jnp.zeros((br_count, 128), F32)
        for s in range(STEPS):
            block = counted[s * br_count:(s + 1) * br_count]
            slots[s].append(jnp.sum(cut[s].astype(F32) * (block[:, :128] + before), axis=0, keepdims=True))
            before = before + block[:, 128:]
        pair_count.append(before)
    slot = [jnp.concatenate(parts, axis=1) for parts in slots]
    count = jnp.concatenate(pair_count, axis=1)
    most = jnp.max(count)
    first_count = jnp.minimum(count, QUAD)
    fullest = jnp.max(jnp.sum(first_count, axis=1, keepdims=True)) / BRANCHES
    latest = jnp.max(jnp.sum(count - first_count, axis=1, keepdims=True)) / BRANCHES
    over = (most > CAP) | (fullest > LIVE) | (latest > LATE)
    flag_ref[0, 0] = jnp.where(over, 1, 0)

    node = iota((128, STEPS * width), 0)
    column = iota((128, STEPS * width), 1)
    mine = onehot(((column & (width - 1)) == me_r * BRANCHES + (node & 15)) & ((node >> 4) == column // width))
    whither = jnp.concatenate([stacked([anc_dev[s], slot[s]], 16, width) for s in range(STEPS)], axis=1)
    own_row = dot_nt(whither, mine)
    own_col = dot_nt(mine, whither)
    own_dev, own_slot = own_col[:NODES, 0:1], own_col[:NODES, 1:2]
    at = iota((16 * br_count, 128), 0)
    is_node = iota((16 * br_count, 128), 1) < NODES
    own_pair = is_node & ((at >> 1).astype(F32) == own_row[0:1] * CAP + own_row[1:2])
    quad_row = own_row[0:1] * QUAD + own_row[1:2]
    own_first = is_node & (own_row[1:2] < QUAD) & ((at >> 2).astype(F32) == quad_row)
    own_late = is_node & (own_row[1:2] >= QUAD) & ((at >> 2).astype(F32) == quad_row - QUAD)
    queries = q_ref[...]

    def padded(rows):
        return jnp.concatenate([rows, jnp.zeros((128 - NODES, rows.shape[1]), BF)], axis=0)

    fresh = [padded(jnp.concatenate([fresh_ref[s, kind] for s in range(STEPS)], axis=0)) for kind in range(2)]
    quarters = jnp.concatenate([padded(queries[:, 256 * n:256 * (n + 1)]) for n in range(4)], axis=0)

    def spread_over(rows, parts, mask):
        return jnp.concatenate([onehot(mask & ((rows & (parts - 1)) == part)) for part in range(parts)], axis=1)

    send_a[:, pl.ds(0, 256)] = dot(spread_over(at, 4, own_first), quarters).astype(BF)
    send_a[:, pl.ds(256, 128)] = dot(spread_over(at, 2, own_pair), jnp.concatenate(fresh, axis=0)).astype(BF)
    send_b[...] = dot(spread_over(at, 4, own_late), quarters).astype(BF)

    def rows16(index):
        return pl.ds(pl.multiple_of(index * 16, 16), 16)

    def to_br(i, source, send, recv, send_sem, recv_sem):
        peer = peer_r(i)
        return pltpu.make_async_remote_copy(
            src_ref=send.at[rows16(peer)], dst_ref=recv.at[rows16(source)],
            send_sem=send_sem.at[peer], recv_sem=recv_sem.at[source],
            device_id={"br": peer}, device_id_type=pl.DeviceIdType.MESH)

    def message_a(i, source):
        return to_br(i, source, send_a, recv_a, a_send, a_recv)

    def message_b(i, source):
        return to_br(i, source, send_b, recv_b, b_send, b_recv)

    def query_copy(t, source):
        return pltpu.make_async_remote_copy(
            src_ref=q_ref, dst_ref=qbuf.at[source],
            send_sem=q_send.at[t], recv_sem=q_recv.at[source],
            device_id={"ctx": chip_at(t) * 2 + core}, device_id_type=pl.DeviceIdType.MESH)

    pl.semaphore_wait(barrier, chips + br_count - 1)

    @pl.loop(1, chips)
    def _(t):
        query_copy(t, chip).start()

    @pl.loop(1, br_count)
    def _(i):
        message_a(i, me_r).start()

    @pl.loop(1, chips)
    def _(t):
        kv_give(t, 0).start()
        kv_give(t, 1).start()

    kv_give(0, 0).start()
    kv_give(0, 1).start()

    @pl.loop(1, br_count)
    def _(i):
        message_b(i, me_r).start()

    own16 = rows16(me_r)
    recv_a[own16, :] = send_a[own16, :]
    recv_b[own16, :] = send_b[own16, :]
    qbuf[chip] = queries

    here = (iota((br_count, width), 0) == me_r).astype(F32)
    home_count = jnp.sum(here * count, axis=0, keepdims=True)
    col_at = iota((width, width), 1)
    earlier = onehot(((row_at & 15) == 0) & ((row_at >> 4) < (col_at >> 4)))
    home_first = jnp.minimum(home_count, QUAD)
    ahead = dot(stacked([home_first, home_count - home_first], 16, width), earlier)
    home = lax.shift_right_logical(iota((1, width), 1), 4).astype(F32)
    local_at = (iota((1, width), 1) & 15).astype(F32)
    ones = jnp.ones((1, width), F32)
    live_rows = iota((128, width), 0).astype(F32)
    chosen, known = [], []
    for s in range(STEPS):
        arrives = anc_dev[s] == me_r.astype(F32)
        first_at = ahead[0:1] + slot[s]
        late_at = ahead[1:2] + slot[s] - QUAD
        late_at = jnp.where((slot[s] < CAP) & (late_at < LATE), late_at + LIVE, -1.0)
        place_at = jnp.where(slot[s] < QUAD, jnp.where(first_at < LIVE, first_at, -1.0), late_at)
        place_at = jnp.where(arrives, place_at, -1.0)
        chosen.append(onehot(live_rows == place_at))
        known.append(stacked([
            ones, home, slot[s], anc_loc[s], home + 32.0 * s, local_at,
            par_hi[s], par_lo[s], old_hi[s], old_lo[s]], 16, width))
    chosen = jnp.concatenate(chosen, axis=1)
    known = jnp.concatenate(known, axis=1)
    row_info = dot_nt(known, chosen)
    col_info = dot_nt(chosen, known)
    here_row = row_info[0:1] > 0.5
    here_col = col_info[:, 0:1] > 0.5
    slot_row, slot_col = row_info[2:3], col_info[:, 2:3]
    pair_col = jnp.where(here_col, col_info[:, 1:2] * CAP + slot_col, -1.0)
    quad_col = jnp.where(here_col, col_info[:, 1:2] * QUAD + slot_col, -1.0)
    quad_row = jnp.where(here_row, row_info[1:2] * QUAD + slot_row, -1.0)
    self_row = jnp.where(here_row, row_info[4:5] * 16.0 + row_info[5:6], -100.0)
    on_path = self_row == col_info[:, 4:5] * 16.0 + col_info[:, 5:6]
    on_path = on_path | (self_row == col_info[:, 6:7] * 16.0 + col_info[:, 7:8])
    on_path = on_path | (self_row == col_info[:, 8:9] * 16.0 + col_info[:, 9:10])
    path = jnp.where(on_path, 1.0, 0.0)
    anc_col = col_info[:, 3:4]
    length_col = jnp.zeros((128, 1), F32)
    for branch in range(BRANCHES):
        length_col = jnp.where(anc_col == branch, len_ref[me_r * BRANCHES + branch].astype(F32), length_col)

    stat_lane = iota((NODES, 128), 1)

    def part_copy(t, source):
        peer = chip_at(t)
        return pltpu.make_async_remote_copy(
            src_ref=part_send.at[peer], dst_ref=part_recv.at[source],
            send_sem=p_send.at[peer], recv_sem=p_recv.at[source],
            device_id={"ctx": peer * 2 + core}, device_id_type=pl.DeviceIdType.MESH)

    def prompt_block(t, block):
        where = chip_at(t)
        if block == 0:
            kv_copy(t, 0).wait()
            kv_copy(t, 1).wait()
        else:
            kv_give(t, 0).wait_recv()
            kv_give(t, 1).wait_recv()
        key = kbuf[t, block]
        value = vbuf[t, block]
        old = part_send[where, pl.ds(ROWS, NODES)]
        stat = jnp.zeros((NODES, 128), F32)
        for half in range(2):
            heads = range(4 * half, 4 * half + 4)
            rows = jnp.concatenate([qbuf[where, :, pl.ds(h * 128, 128)] for h in heads], axis=0)
            peak, total, summed = softmax_block(rows, key, value)
            part = pl.ds(half * 4 * NODES, 4 * NODES)
            if block == 1:
                old_peak = jnp.concatenate([old[:, h:h + 1] for h in heads], axis=0)
                old_total = jnp.concatenate([old[:, 8 + h:9 + h] for h in heads], axis=0)
                joint = jnp.maximum(peak, old_peak)
                old_factor = jnp.exp2((old_peak - joint) * EXP_SCALE)
                factor = jnp.exp2((peak - joint) * EXP_SCALE)
                total = old_factor * old_total + factor * total
                summed = old_factor * part_send[where, part] + factor * summed
                peak = joint
            part_send[where, part] = summed
            for h in heads:
                cut = slice((h - 4 * half) * NODES, (h - 4 * half + 1) * NODES)
                stat = jnp.where(stat_lane == h, peak[cut], stat)
                stat = jnp.where(stat_lane == 8 + h, total[cut], stat)
        part_send[where, pl.ds(ROWS, NODES)] = stat

    def prompt_head(t):
        query_copy(t, chip_at(t)).wait_recv()
        prompt_block(t, 0)
        prompt_block(t, 1)
        part_copy(t, chip).start()

    prompt_block(0, 0)

    @pl.loop(1, chips - 1)
    def _(t):
        prompt_head(t)

    @pl.loop(1, br_count)
    def _(i):
        message_a(0, peer_r(i)).wait_recv()

    got_a = recv_a[...]
    gather = iota((128, 16 * br_count), 1)
    pairs = (gather >> 1).astype(F32) == pair_col
    new_key = dot(onehot(pairs & ((gather & 1) == 0)), got_a[:, 256:]).astype(BF)
    new_value = dot(onehot(pairs & ((gather & 1) == 1)), got_a[:, 256:]).astype(BF)

    def gathered(address, got):
        count = address.shape[0]
        place = iota((count, 16 * br_count), 1)
        match = (place >> 2).astype(F32) == address
        parts = jnp.concatenate([onehot(match & ((place & 3) == part)) for part in range(4)], axis=0)
        return dot(parts, got).astype(BF)

    taken = gathered(quad_col[:LIVE], got_a[:, :256])
    for n in range(4):
        for parity in range(2):
            qrows[2 * parity + n // 2, pl.ds((n % 2) * LIVE, LIVE)] = taken[
                n * LIVE:(n + 1) * LIVE, parity * 128:(parity + 1) * 128]
    key_pages.wait()
    value_pages.wait()

    def suffix_block(rows, anc, length, see):
        count = rows.shape[0]
        fold = jnp.zeros((count, 256), F32)
        for branch in range(BRANCHES):
            key = jnp.concatenate([kpage[lax.rem(page_ref[page, branch], 32)] for page in range(2)], axis=0)
            fold = jnp.where(anc == branch, dot_nt(rows, key), fold)
        fold = jnp.where(iota((count, 256), 1).astype(F32) < length, fold, MASKED)
        new = jnp.where(see > 0.5, dot_nt(rows, new_key), MASKED)
        peak = jnp.maximum(jnp.max(fold, axis=1, keepdims=True), jnp.max(new, axis=1, keepdims=True))
        weight = jnp.exp2((fold - peak) * EXP_SCALE)
        new = jnp.exp2((new - peak) * EXP_SCALE)
        total = jnp.sum(weight, axis=1, keepdims=True) + jnp.sum(new, axis=1, keepdims=True)
        weight = weight.astype(BF)
        summed = dot(new.astype(BF), new_value)
        for branch in range(0, BRANCHES, 2):
            value = jnp.concatenate([jnp.concatenate(
                [vpage[lax.rem(page_ref[page, b], 32)] for page in range(2)], axis=0)
                for b in (branch, branch + 1)], axis=1)
            both = dot(weight, value)
            summed = jnp.where(anc == branch, summed + both[:, :128], summed)
            summed = jnp.where(anc == branch + 1, summed + both[:, 128:], summed)
        largest = jnp.max(jnp.abs(summed), axis=1, keepdims=True)
        coded = jnp.round(summed * jnp.where(largest > 0.0, 32767.0 / largest, 0.0))
        upper = jnp.floor(coded / 256.0)
        sum_log = peak * EXP_SCALE + jnp.log2(total)
        return upper.astype(BF), (coded - 256.0 * upper).astype(BF), sum_log, largest / (32767.0 * total)

    def repeated(column, times):
        return jnp.concatenate([column] * times, axis=0)

    def stat_rows(stat, cut):
        lane = iota(stat.shape, 1)
        stat = jnp.where((lane >> 4).astype(F32) == slot_col[cut], stat, 0.0)
        home_at = iota((br_count, stat.shape[0]), 0).astype(F32)
        own_home = jnp.where(here_row[:, cut] & (home_at == row_info[1:2, cut]), 1.0, 0.0)
        return jnp.dot(own_home, stat, precision=lax.Precision.HIGHEST, preferred_element_type=F32)

    def return_rows(address, high, low):
        count = address.shape[1]
        rows = iota((16 * br_count, count), 0)
        spread = spread_over(rows, 4, (rows >> 2).astype(F32) == address)
        return (256.0 * dot(spread, high) + dot(spread, low)).astype(jnp.int32).astype(jnp.int16)

    def returned(group, i, source):
        if group < 2:
            return to_br(i, source, ret_send.at[group], ret_recv.at[group], r_send.at[group], r_recv.at[group])
        return to_br(i, source, late_send, late_recv, r_send.at[2], r_recv.at[2])

    def returned_stat(group, i, source):
        peer = peer_r(i)
        return pltpu.make_async_remote_copy(
            src_ref=stat_send.at[group, peer], dst_ref=stat_recv.at[group, source],
            send_sem=s_send.at[group, peer], recv_sem=s_recv.at[group, source],
            device_id={"br": peer}, device_id_type=pl.DeviceIdType.MESH)

    def give_stat(group, stat):
        for home_index in range(br_count):
            stat_send[group, home_index] = stat[home_index:home_index + 1]

        @pl.loop(1, br_count)
        def _(i):
            returned_stat(group, i, me_r).start()

        stat_recv[group, me_r] = stat_send[group, me_r]

    first_lane = iota((LIVE, 128), 1) & 15
    stat_a = jnp.zeros((LIVE, 128), F32)
    for parity in range(2):

        def suffix_pair(pair, stat):
            high, low, sum_log, unit = suffix_block(
                qrows[2 * parity + pair], repeated(anc_col[:LIVE], 2), repeated(length_col[:LIVE], 2),
                repeated(path[:LIVE], 2))
            pair_rows = pl.ds(pl.multiple_of(pair * 2 * LIVE, 2 * LIVE), 2 * LIVE)
            code_high[pair_rows] = high
            code_low[pair_rows] = low
            for half in range(2):
                cut = slice(half * LIVE, (half + 1) * LIVE)
                head = 4 * pair + 2 * half + parity
                stat = jnp.where(first_lane == head, sum_log[cut], stat)
                stat = jnp.where(first_lane == 8 + head, unit[cut], stat)
            return stat

        stat_a = lax.fori_loop(0, 2, suffix_pair, stat_a)
        ret_send[parity] = return_rows(quad_row[:, :LIVE], code_high[...], code_low[...])

        @pl.loop(1, br_count)
        def _(i):
            returned(parity, i, me_r).start()

        ret_recv[parity, own16, :] = ret_send[parity, own16, :]

    give_stat(0, stat_rows(stat_a, slice(0, LIVE)))

    @pl.loop(1, br_count)
    def _(i):
        message_b(0, peer_r(i)).wait_recv()

    late = slice(LIVE, LIVE + LATE)
    taken = gathered(quad_col[late] - QUAD, recv_b[...])
    rows = jnp.concatenate([
        taken[(h // 2) * LATE:(h // 2 + 1) * LATE, (h % 2) * 128:(h % 2 + 1) * 128] for h in range(8)], axis=0)
    high, low, sum_log, unit = suffix_block(
        rows, repeated(anc_col[late], 8), repeated(length_col[late], 8), repeated(path[late], 8))
    late_lane = iota((LATE, 128), 1) & 15
    stat_b = jnp.zeros((LATE, 128), F32)
    for h in range(8):
        cut = slice(h * LATE, (h + 1) * LATE)
        late_high[pl.ds((h // 2) * LATE, LATE), pl.ds((h % 2) * 128, 128)] = high[cut]
        late_low[pl.ds((h // 2) * LATE, LATE), pl.ds((h % 2) * 128, 128)] = low[cut]
        stat_b = jnp.where(late_lane == h, sum_log[cut], stat_b)
        stat_b = jnp.where(late_lane == 8 + h, unit[cut], stat_b)
    late_send[...] = return_rows(quad_row[:, late] - QUAD, late_high[...], late_low[...])

    @pl.loop(1, br_count)
    def _(i):
        returned(2, i, me_r).start()

    late_recv[own16, :] = late_send[own16, :]
    give_stat(1, stat_rows(stat_b, late))

    prompt_head(chips - 1)
    prompt_block(0, 1)

    part_recv[chip] = part_send[chip]

    @pl.loop(1, chips)
    def _(t):
        part_copy(t, chip_at(t)).wait_recv()

    stats = [part_recv[c, pl.ds(ROWS, NODES)] for c in range(4)]
    top = functools.reduce(jnp.maximum, stats)
    factors = [jnp.exp2((stat - top) * EXP_SCALE) for stat in stats]
    den = jnp.zeros((NODES, 128), F32)
    for c in range(4):
        den = den + factors[c] * pltpu.roll(stats[c], 120, 1)
    for h in range(8):
        summed = jnp.zeros((NODES, 128), F32)
        for c in range(4):
            summed = summed + factors[c][:, h:h + 1] * part_recv[c, pl.ds(h * NODES, NODES)]
        num[h] = summed

    back_low = iota((4 * NODES, 16 * br_count), 1)
    address = repeated(own_dev * QUAD + own_slot, 4)
    quarter_at = iota((4 * NODES, 16 * br_count), 0) // NODES

    def collected(arrived, match):
        collect = onehot(match & ((back_low & 3) == quarter_at))
        arrived = arrived.astype(jnp.int32)
        upper = dot(collect, (arrived >> 8).astype(F32).astype(BF))
        return 256.0 * upper + dot(collect, (arrived & 255).astype(F32).astype(BF))

    in_first = repeated(own_slot, 4) < QUAD
    quad_at = (back_low >> 2).astype(F32)
    first_match = in_first & (quad_at == address)
    coded = []
    for parity in range(2):

        @pl.loop(1, br_count)
        def _(i):
            returned(parity, 0, peer_r(i)).wait_recv()

        coded.append(collected(ret_recv[parity], first_match))

    @pl.loop(1, br_count)
    def _(i):
        returned(2, 0, peer_r(i)).wait_recv()
        returned_stat(0, 0, peer_r(i)).wait_recv()
        returned_stat(1, 0, peer_r(i)).wait_recv()

    coded_late = collected(late_recv[...], jnp.logical_not(in_first) & (quad_at == address - QUAD))
    coded = jnp.concatenate(coded, axis=1) + coded_late
    from_device = jnp.where(iota((NODES, br_count), 1).astype(F32) == own_dev, 1.0, 0.0)
    all_stat = jnp.concatenate([stat_recv[0, d] + stat_recv[1, d] for d in range(br_count)], axis=0)
    back_stat = jnp.dot(from_device, all_stat, precision=lax.Precision.HIGHEST, preferred_element_type=F32)
    back_stat = jnp.where((stat_lane >> 4).astype(F32) == own_slot, back_stat, 0.0)
    for shift in (64, 32, 16):
        back_stat = back_stat + pltpu.roll(back_stat, shift, 1)
    prompt_log = top * EXP_SCALE
    overall = jnp.maximum(prompt_log, back_stat)
    prompt_factor = jnp.exp2(prompt_log - overall)
    suffix_factor = jnp.exp2(back_stat - overall)
    den = prompt_factor * den + suffix_factor
    unit = suffix_factor * pltpu.roll(back_stat, 120, 1)
    for h in range(8):
        back_home = coded[(h // 2) * NODES:(h // 2 + 1) * NODES, (h % 2) * 128:(h % 2 + 1) * 128]
        joined = prompt_factor[:, h:h + 1] * num[h] + unit[:, h:h + 1] * back_home
        out_ref[:, pl.ds(h * 128, 128)] = (joined / den[:, h:h + 1]).astype(BF)

    @pl.loop(1, chips)
    def _(t):
        query_copy(t, chip).wait_send()
        part_copy(t, chip).wait_send()

    @pl.loop(0, chips)
    def _(t):
        kv_give(t, 0).wait_send()
        kv_give(t, 1).wait_send()

    @pl.loop(1, br_count)
    def _(i):
        message_a(i, me_r).wait_send()
        message_b(i, me_r).wait_send()
        for group in range(2):
            returned_stat(group, i, me_r).wait_send()
        for group in range(3):
            returned(group, i, me_r).wait_send()


def local(
    prompt_key_value, suffix_page_store, page_table, lengths, parents, queries, fresh_key_value
):
    br_count = lax.axis_size("br")
    ctx_count = lax.axis_size("ctx")
    vmem = pl.BlockSpec(memory_space=pltpu.VMEM)
    smem = pl.BlockSpec(memory_space=pltpu.SMEM)
    anywhere = pl.BlockSpec(memory_space=pl.ANY)
    dma = pltpu.SemaphoreType.DMA
    out, flag = pl.pallas_call(
        functools.partial(kernel, br_count, ctx_count),
        out_shape=(
            jax.ShapeDtypeStruct((NODES, 1024), BF),
            jax.ShapeDtypeStruct((1, 1), jnp.int32),
        ),
        in_specs=[smem, smem, vmem, vmem, vmem, anywhere, anywhere],
        out_specs=(vmem, smem),
        scratch_shapes=[
            pltpu.VMEM((4, 2, 2048, 128), BF),
            pltpu.VMEM((4, 2, 2048, 128), BF),
            pltpu.VMEM((32, 128, 128), BF),
            pltpu.VMEM((32, 128, 128), BF),
            pltpu.VMEM((4, NODES, 1024), BF),
            pltpu.VMEM((16 * br_count, 384), BF),
            pltpu.VMEM((16 * br_count, 384), BF),
            pltpu.VMEM((16 * br_count, 256), BF),
            pltpu.VMEM((16 * br_count, 256), BF),
            pltpu.VMEM((4, 2 * LIVE, 128), BF),
            pltpu.VMEM((4, ROWS + NODES, 128), F32),
            pltpu.VMEM((4, ROWS + NODES, 128), F32),
            pltpu.VMEM((4 * LIVE, 128), BF),
            pltpu.VMEM((4 * LIVE, 128), BF),
            pltpu.VMEM((4 * LATE, 256), BF),
            pltpu.VMEM((4 * LATE, 256), BF),
            pltpu.VMEM((2, br_count, 1, 128), F32),
            pltpu.VMEM((2, br_count, 1, 128), F32),
            pltpu.VMEM((2, 16 * br_count, 128), jnp.int16),
            pltpu.VMEM((2, 16 * br_count, 128), jnp.int16),
            pltpu.VMEM((16 * br_count, 256), jnp.int16),
            pltpu.VMEM((16 * br_count, 256), jnp.int16),
            pltpu.VMEM((8, NODES, 128), F32),
            dma((2, 4)), dma((2, 4)), dma((2, 4)), dma((2,)), dma((4,)), dma((4,)), dma((32,)), dma((32,)), dma((32,)), dma((32,)),
            dma((4,)), dma((4,)), dma((3, 32)), dma((3, 32)), dma((2, 32)), dma((2, 32)),
        ],
        compiler_params=pltpu.CompilerParams(
            collective_id=0, has_side_effects=True, vmem_limit_bytes=56 * 1024 * 1024
        ),
    )(
        page_table.T, lengths, parents, queries.reshape(NODES, 1024), fresh_key_value,
        prompt_key_value, suffix_page_store,
    )
    operands = (
        prompt_key_value, suffix_page_store, page_table, lengths, parents, queries, fresh_key_value
    )
    return lax.cond(
        flag[0, 0] > 0,
        lambda *whole: general(*whole),
        lambda *whole: out.reshape(STEPS, BRANCHES, 1024),
        *operands,
    )


def solution(mesh):
    in_specs = (
        P(None, "ctx", None),
        P("br", None, None, "ctx"),
        P("br", None),
        P(),
        P(),
        P(None, "br", "ctx"),
        P(None, None, "br", "ctx"),
    )
    out_specs = P(None, "br", "ctx")
    return jax.shard_map(local, mesh=mesh, in_specs=in_specs, out_specs=out_specs, check_vma=False)
```
